32 devices in a mesh: row: 8 (over z, x), col: 4 (over y, core).
Axes of the slice: x: 2, y: 2, z: 4, core: 2. Of those that a mesh axis runs over, the one named last changes fastest.
Arguments:
- stereo_neuron_outputs: bfloat16 [2, 64, 64, 512], P(None, 'row', None, 'col'), may hold values from -6 to 6
- filter_tap_coefficients: bfloat16 [3, 3, 3, 64, 64], replicated, may hold values from -0.25 to 0.25
- filter_stack_intercepts: float32 [3, 64], replicated, may hold values from -3 to 3
- reference_picture_present: int32 [64, 512], P('row', 'col'), may hold values 0 or 1
- tile_shift_amounts: int32 [8, 4], P('row', 'col'), may hold values from 0 to 256, as said below
- smoothness_charges: int32 [2], replicated, may hold values from 4 to 96, as said below
Outputs:
- aggregated: float32 [64, 512, 128], P('row', 'col')
The draws below stay inside these ranges and needn't reach their ends.
Inputs may be any that keep to these rules, and one draw needn't show every extreme that they name: `tile_shift_amounts`: every tile's offset is a whole number of 0 to 256; some tile has exactly 256. smoothness_charges[0] lies in 4 to 16; smoothness_charges[1] is 96.
All inputs are finite; a program needn't handle non-finite values. No bound on the sum of `reference_picture_present` on one device may be relied on, other than what follows from the above.
Results may differ from the reference program's by a relative error of at most 0.006.
Values may be sent and summed in bfloat16 or wider, within the bound.
No kernel may reach another device: no remote copies, remote signals or barrier semaphores. Data moves between devices by JAX's collectives and lax.ppermute only.
A program may use at most 64 MiB of HBM per device.

```python
import jax
import jax.numpy as jnp
from jax import lax

CHANNELS = 64
DISPARITIES = 128
LAYERS = 3
TILE_ROWS = 8
TILE_COLS = 128
OFF_MOST = 256
TILES_DOWN = 8
TILES_ACROSS = 4
ROWS = 64
COLS = 512


def draw_tile_shift_amounts(key, part):
    first_key, second_key = jax.random.split(key)
    values = jax.random.randint(first_key, (TILES_DOWN, TILES_ACROSS), 0, OFF_MOST + 1)
    chosen = jax.random.randint(second_key, (), 0, TILES_DOWN * TILES_ACROSS)
    places = jnp.arange(TILES_DOWN * TILES_ACROSS).reshape(TILES_DOWN, TILES_ACROSS)
    return jnp.where(places == chosen, OFF_MOST, values).astype(jnp.int32)


def draw_smoothness_charges(key, part):
    first_key = jax.random.fold_in(key, 11)
    small_pen = jax.random.randint(first_key, (), 4, 17)
    large_pen = jnp.full((), 96, jnp.int32)
    return jnp.stack([small_pen.astype(jnp.int32), large_pen]).astype(jnp.int32)


def place_ends(array, rng, low, high):
    spot = [jax.random.randint(jax.random.fold_in(rng, axis), (), 0, length) for axis, length in enumerate(array.shape)]
    longest = array.shape.index(max(array.shape))
    next_to = spot[:longest] + [(spot[longest] + 1) % array.shape[longest]] + spot[longest + 1:]
    return array.at[tuple(spot)].set(low).at[tuple(next_to)].set(high)


def block_scale(own_key, dims, cuts, smallest, largest):
    def one(dim, blocks):
        heights = jax.random.uniform(jax.random.fold_in(jax.random.fold_in(own_key, 6), dim), (blocks,), jnp.float32, smallest / len(cuts), largest / len(cuts))
        return jnp.repeat(jnp.exp(heights), dims[dim] // blocks).reshape((-1,) + (1,) * (len(dims) - dim - 1))

    factor_of = one(*cuts[0])
    for cut in cuts[1:]:
        factor_of = factor_of * one(*cut)
    return factor_of


def centred(key, dims, deviation, most, cuts=(), kind=jnp.bfloat16):
    factor_of = block_scale(key, dims, cuts, -0.22, 0.18) if cuts else 1.0
    entries = jax.random.normal(key, dims, jnp.float32) * deviation * factor_of
    return jnp.minimum(jnp.maximum(entries, -most), most).astype(kind)


def setup_inputs(seed: int = 0) -> dict:
    key_list = jax.random.split(jax.random.key(seed), 7)
    stereo_neuron_outputs = centred(key_list[0], (2, ROWS, CHANNELS, COLS), 1.0, 6.0, ((1, 8), (3, 4)))
    filter_tap_coefficients = centred(key_list[1], (LAYERS, 3, 3, CHANNELS, CHANNELS), (9 * CHANNELS) ** -0.5, 0.25)
    filter_stack_intercepts = centred(key_list[2], (LAYERS, CHANNELS), 0.5, 3.0, (), jnp.float32)
    reference_picture_present = place_ends((jax.random.randint(key_list[3], (ROWS, COLS), 0, 8) < 7).astype(jnp.int32), jax.random.fold_in(key_list[3], 1), 0, 1)
    tile_shift_amounts = draw_tile_shift_amounts(jax.random.fold_in(key_list[6], 71), 0)
    smoothness_charges = draw_smoothness_charges(jax.random.fold_in(key_list[6], 71), 0)
    return dict(stereo_neuron_outputs=stereo_neuron_outputs, filter_tap_coefficients=filter_tap_coefficients, filter_stack_intercepts=filter_stack_intercepts, reference_picture_present=reference_picture_present, tile_shift_amounts=tile_shift_amounts, smoothness_charges=smoothness_charges)


def advance(state, cost_row, gentle_change_charge, steep_change_charge):
    least = lax.optimization_barrier(jnp.min(state, axis=-1, keepdims=True))
    barrier = jnp.full(state.shape[:-1] + (1,), jnp.inf, state.dtype)
    lower = jnp.concatenate([barrier, state[..., :-1]], axis=-1)
    upper = jnp.concatenate([state[..., 1:], barrier], axis=-1)
    best = jnp.minimum(jnp.minimum(state, jnp.minimum(lower, upper) + gentle_change_charge), least + steep_change_charge)
    return cost_row + best - least

def sweep(costs, incoming, gentle_change_charge, steep_change_charge, backward):

    def stepper(state, cost_row):
        fresh = advance(state, cost_row, gentle_change_charge, steep_change_charge)
        return (fresh, fresh)
    return lax.scan(stepper, incoming, costs, reverse=backward)

def one_image(image, filter_tap_coefficients, filter_stack_intercepts):
    hidden = image[None]
    features = None
    for layer_number in range(LAYERS):
        summed = lax.conv_general_dilated(hidden.astype(jnp.float32), filter_tap_coefficients[layer_number].astype(jnp.float32), (1, 1), 'SAME', dimension_numbers=('NHCW', 'HWOI', 'NHCW'), precision=lax.Precision.HIGHEST)
        summed = summed + filter_stack_intercepts[layer_number][None, None, :, None]
        if layer_number < LAYERS - 1:
            hidden = jnp.maximum(summed, 0.0).astype(jnp.bfloat16)
        else:
            features = summed
    features = features[0]
    scale = lax.rsqrt(lax.optimization_barrier(jnp.sum(features * features, axis=1, keepdims=True)) + 1e-06)
    return (features * scale).astype(jnp.bfloat16)

def reference(stereo_neuron_outputs, filter_tap_coefficients, filter_stack_intercepts, reference_picture_present, tile_shift_amounts, smoothness_charges):
    unit = lax.map(lambda image: one_image(image, filter_tap_coefficients, filter_stack_intercepts), stereo_neuron_outputs)
    shift_map = jnp.repeat(jnp.repeat(tile_shift_amounts, TILE_ROWS, axis=0), TILE_COLS, axis=1).astype(jnp.int32)
    columns = jnp.arange(COLS, dtype=jnp.int32)
    levels = jnp.arange(DISPARITIES, dtype=jnp.int32)

    def row_cost(items):
        left_row, right_row, disparity_offset_row, valid_row = items
        source = columns[:, None] - disparity_offset_row[:, None] - levels[None, :]
        inside = source >= 0
        taken = right_row.astype(jnp.float32)[:, jnp.maximum(source, 0)]
        taken = jnp.where(inside[None], taken, 0.0)
        similar = lax.optimization_barrier(jnp.sum(left_row.astype(jnp.float32)[:, :, None] * taken, axis=0))
        return jnp.where(valid_row[:, None] == 1, 1.0 - similar, 1.0)
    cost = lax.map(row_cost, (unit[0], unit[1], shift_map, reference_picture_present))
    gentle_change_charge = smoothness_charges[0].astype(jnp.float32) / 64.0
    steep_change_charge = smoothness_charges[1].astype(jnp.float32) / 64.0
    start_cols = jnp.zeros((COLS, DISPARITIES), jnp.float32)
    final_down, down_layers = sweep(cost, start_cols, gentle_change_charge, steep_change_charge, False)
    final_up, up_layers = sweep(cost, start_cols, gentle_change_charge, steep_change_charge, True)
    vertical = down_layers + up_layers
    across = jnp.swapaxes(cost, 0, 1)
    start_rows = jnp.zeros((ROWS, DISPARITIES), jnp.float32)
    final_right, right_layers = sweep(across, start_rows, gentle_change_charge, steep_change_charge, False)
    final_left, left_layers = sweep(across, start_rows, gentle_change_charge, steep_change_charge, True)
    horizontal = right_layers + left_layers
    return vertical + jnp.swapaxes(horizontal, 0, 1)
```

```python
import functools

import jax
import jax.numpy as jnp
from jax import lax
from jax.experimental import pallas as pl
from jax.experimental.pallas import tpu as pltpu
from jax.sharding import PartitionSpec as P

DISPARITIES = 128
OFF_MOST = 256
SUB = 8
REGS = DISPARITIES // SUB
VMEM_LIMIT = 56 * 1024 * 1024


def lane_to_disparity(lane):
    return (lane % SUB) * REGS + lane // SUB


def disparity_to_lane(disparity):
    return (disparity % REGS) * SUB + disparity // REGS


def advance(state, cost, p1, p2):
    lanes = state[0].shape[1]
    row = lax.broadcasted_iota(jnp.int32, (SUB, lanes), 0)
    below = jnp.where(row == 0, jnp.inf, pltpu.roll(state[-1], 1, 0))
    above = jnp.where(row == SUB - 1, jnp.inf, pltpu.roll(state[0], SUB - 1, 0))
    least = list(state)
    while len(least) > 1:
        least = [jnp.minimum(a, b) for a, b in zip(least[::2], least[1::2])]
    least = least[0]
    for turn in (4, 2, 1):
        least = jnp.minimum(least, pltpu.roll(least, turn, 0))
    lower = [below] + state[:-1]
    upper = state[1:] + [above]
    fresh = []
    for s, l, u, c in zip(state, lower, upper, cost):
        t = jnp.minimum(s, jnp.minimum(l, u) + p1)
        fresh.append(c + jnp.minimum(t - least, p2))
    return fresh


def charges(charge_ref):
    return (
        charge_ref[0].astype(jnp.float32) * (1.0 / 64.0),
        charge_ref[1].astype(jnp.float32) * (1.0 / 64.0),
    )


def registers(array):
    return [array[SUB * v : SUB * (v + 1)] for v in range(REGS)]


def band_kernel(
    place_ref, given_ref, filter_ref, bias_ref, cost_ref, own_ref,
    maps_a, maps_b, left_unit, right_unit, present,
):
    parts, _, channels, width = given_ref.shape
    layers = filter_ref.shape[0]
    rows = own_ref.shape[0]
    cols = parts * width
    high = rows + 2 * layers
    first_row = place_ref[0] * rows
    rows_total = place_ref[1] * rows
    own = place_ref[2]
    lead = (OFF_MOST + 2 * width - 1) // width * width

    for p in range(parts):
        present[:, p * width : (p + 1) * width] = given_ref[p, 2 * high, 0:16, :].astype(
            jnp.float32
        )
    right_unit[:, 0:lead] = jnp.zeros((rows * channels, lead), jnp.bfloat16)
    right_unit[:, lead + cols :] = jnp.zeros((rows * channels, width), jnp.bfloat16)

    column = lax.broadcasted_iota(jnp.int32, (1, cols), 1)
    for image in range(2):

        @pl.loop(0, high)
        def _(row):
            for p in range(parts):
                maps_a[pl.ds(pl.multiple_of(row * channels, channels), channels),
                       p * width : (p + 1) * width] = given_ref[p, image * high + row]

        for layer in range(layers):
            source, target = (maps_a, maps_b) if layer % 2 == 0 else (maps_b, maps_a)
            margin = layers - 1 - layer

            @pl.loop(0, rows + 2 * margin, unroll=2)
            def _(row):
                start = pl.multiple_of(row * channels, channels)
                window = source[pl.ds(start, 3 * channels), :]
                taps = jnp.dot(filter_ref[layer], window, preferred_element_type=jnp.float32)
                before = pltpu.roll(taps[:channels], 1, 1)
                after = pltpu.roll(taps[2 * channels :], cols - 1, 1)
                z = taps[channels : 2 * channels] + jnp.where(column == 0, 0.0, before)
                z = z + jnp.where(column == cols - 1, 0.0, after) + bias_ref[layer]
                if layer < layers - 1:
                    there = first_row - margin + row
                    inside = jnp.logical_and(there >= 0, there < rows_total)
                    z = jnp.maximum(z, 0.0) * jnp.where(inside, 1.0, 0.0)
                    target[pl.ds(start, channels), :] = z.astype(jnp.bfloat16)
                else:
                    scale = lax.rsqrt(jnp.sum(z * z, axis=0, keepdims=True) + 1e-06)
                    unit = (z * scale).astype(jnp.bfloat16)
                    if image == 0:
                        seen = present[pl.ds(row, 1), :]
                        unit = jnp.where(seen > 0.5, unit.astype(jnp.float32), 0.0)
                        left_unit[pl.ds(start, channels), :] = unit.astype(jnp.bfloat16)
                    else:
                        right_unit[pl.ds(start, channels), lead : lead + cols] = unit

    lane = lax.broadcasted_iota(jnp.int32, (width, DISPARITIES), 1)
    place = lax.broadcasted_iota(jnp.int32, (width, DISPARITIES), 0)

    @pl.loop(0, parts)
    def _(p):
        shift_block = given_ref[p, 2 * high, 16:32, :].astype(jnp.float32)
        shift = jnp.max(shift_block).astype(jnp.int32)
        base = p * width - shift + lead
        block = base // width
        ahead = place + (base - block * width)
        index = (ahead - lane_to_disparity(lane)) & (DISPARITIES - 1)
        start = pl.multiple_of((block - 1) * width, width)
        here = pl.multiple_of(p * width, width)
        for y in range(rows):
            left = left_unit[y * channels : (y + 1) * channels, pl.ds(here, width)]
            right = right_unit[y * channels : (y + 1) * channels, pl.ds(start, 3 * width)]
            product = lax.dot_general(
                left, right, (((0,), (0,)), ((), ())), preferred_element_type=jnp.float32
            )
            chosen = jnp.where(lane <= ahead, product[:, width : 2 * width], product[:, :width])
            chosen = jnp.where(lane <= ahead - width, product[:, 2 * width :], chosen)
            chosen = 1.0 - jnp.take_along_axis(chosen, index, axis=1, mode="promise_in_bounds")
            cost_ref[pl.ds(here, width), y, :] = chosen

            @pl.when(p == own)
            def _():
                own_ref[y] = chosen.T.astype(jnp.bfloat16)


def across_kernel(place_ref, charge_ref, cost_ref, kept_ref):
    cols, rows, _ = cost_ref.shape
    width = kept_ref.shape[0]
    parts = cols // width
    own = place_ref[2]
    p1, p2 = charges(charge_ref)

    def step(i, state, keep, first_col, last_col):
        right = cost_ref[first_col + i]
        left = cost_ref[last_col - i]
        cost = jnp.concatenate([right, left], axis=0).T
        fresh = advance(list(state), registers(cost), p1, p2)
        if keep:
            back = jnp.concatenate(fresh, axis=0).T
            kept_ref[i, 0:rows] = back[0:rows]
            kept_ref[width - 1 - i, rows : 2 * rows] = back[rows : 2 * rows]
        return tuple(fresh)

    state = tuple(jnp.zeros((SUB, 2 * rows), jnp.float32) for _ in range(REGS))

    def segment(p, state):
        first_col = p * width
        last_col = cols - 1 - p * width

        def plain(state):
            return lax.fori_loop(
                0, width, lambda i, s: step(i, s, False, first_col, last_col), state, unroll=8
            )

        def keeping(state):
            def body(i, s):
                right = cost_ref[first_col + i]
                left = cost_ref[last_col - i]
                cost = jnp.concatenate([right, left], axis=0).T
                fresh = advance(list(s), registers(cost), p1, p2)
                back = jnp.concatenate(fresh, axis=0).T

                @pl.when(p == own)
                def _():
                    kept_ref[i, 0:rows] = back[0:rows]

                @pl.when(parts - 1 - p == own)
                def _():
                    kept_ref[width - 1 - i, rows : 2 * rows] = back[rows : 2 * rows]

                return tuple(fresh)

            return lax.fori_loop(0, width, body, state, unroll=8)

        mine = jnp.logical_or(p == own, parts - 1 - p == own)
        return lax.cond(mine, keeping, plain, state)

    lax.fori_loop(0, parts, segment, state)


def down_or_up(forward, first_own, cost_ref, state, p1, p2, keep):
    group, rows = cost_ref.shape[:2]
    count = group * rows

    def body(i, state):
        row = jnp.where(forward, i, count - 1 - i)
        block = row // rows
        inner = row - block * rows
        cost = cost_ref[block, inner].astype(jnp.float32)
        fresh = advance(list(state), registers(cost), p1, p2)

        @pl.when(block == first_own)
        def _():
            keep(inner, jnp.concatenate(fresh, axis=0))

        return tuple(fresh)

    return lax.fori_loop(0, count, body, state, unroll=4)


def first_vertical_kernel(place_ref, charge_ref, cost_ref, kept_ref, last_ref):
    p1, p2 = charges(charge_ref)
    width = cost_ref.shape[-1]
    state = tuple(jnp.zeros((SUB, width), jnp.float32) for _ in range(REGS))

    def keep(row, value):
        kept_ref[row] = value

    final = down_or_up(place_ref[3] == 0, place_ref[4], cost_ref, state, p1, p2, keep)
    last_ref[...] = jnp.concatenate(final, axis=0).astype(jnp.bfloat16)


def second_vertical_kernel(
    place_ref, charge_ref, cost_ref, kept_ref, came_ref, across_ref, out_ref, total
):
    p1, p2 = charges(charge_ref)
    rows, _, width = kept_ref.shape
    state = tuple(registers(came_ref[...].astype(jnp.float32)))

    def keep(row, value):
        total[row] = value + kept_ref[row]

    down_or_up(place_ref[3] != 0, place_ref[4], cost_ref, state, p1, p2, keep)
    lane = lax.broadcasted_iota(jnp.int32, (width, DISPARITIES), 1)
    index = disparity_to_lane(lane)
    for row in range(rows):
        value = total[row].T + (across_ref[:, row, :] + across_ref[:, rows + row, :])
        out_ref[row] = jnp.take_along_axis(value, index, axis=1, mode="promise_in_bounds")


SMEM = functools.partial(pl.BlockSpec, memory_space=pltpu.SMEM)
VMEM = functools.partial(pl.BlockSpec, memory_space=pltpu.VMEM)


def call(kernel, outs, specs, scratch=(), flops=0):
    return pl.pallas_call(
        kernel,
        out_shape=outs,
        in_specs=specs,
        out_specs=jax.tree.map(lambda _: VMEM(), outs),
        scratch_shapes=list(scratch),
        compiler_params=pltpu.CompilerParams(vmem_limit_bytes=VMEM_LIMIT),
        cost_estimate=pl.CostEstimate(flops=flops, bytes_accessed=1 << 22, transcendentals=0),
    )


def per_device(activations, filters, biases, present, shifts, smooth):
    _, rows, channels, width = activations.shape
    layers = filters.shape[0]
    high = rows + 2 * layers
    row_rank, row_count = lax.axis_index("row"), lax.axis_size("row")
    col_rank, parts = lax.axis_index("col"), lax.axis_size("col")
    half = row_count // 2
    cols = parts * width
    place = jnp.stack(
        [row_rank, jnp.int32(row_count), col_rank, row_rank // half, row_rank % half]
    ).astype(jnp.int32)

    downward = [(i, i + 1) for i in range(row_count - 1)]
    upward = [(i + 1, i) for i in range(row_count - 1)]
    before = lax.ppermute(activations[:, rows - layers :], "row", downward)
    after = lax.ppermute(activations[:, :layers], "row", upward)
    extra = jnp.concatenate(
        [
            present.astype(jnp.bfloat16),
            jnp.zeros((16 - rows, width), jnp.bfloat16),
            jnp.broadcast_to(shifts.astype(jnp.bfloat16), (channels - 16, width)),
        ],
        axis=0,
    )
    block = jnp.concatenate([before, activations, after], axis=1)
    block = jnp.concatenate([block.reshape(2 * high, channels, width), extra[None]], axis=0)
    given = lax.all_gather(block, "col", axis=0)
    taps = jnp.transpose(filters, (0, 2, 3, 1, 4)).reshape(layers, 3 * channels, 3 * channels)

    f32, bf16 = jnp.float32, jnp.bfloat16
    lead = (OFF_MOST + 2 * width - 1) // width * width
    cost, own = call(
        band_kernel,
        (
            jax.ShapeDtypeStruct((cols, rows, DISPARITIES), f32),
            jax.ShapeDtypeStruct((rows, DISPARITIES, width), bf16),
        ),
        [SMEM(), VMEM(), VMEM(), VMEM()],
        [
            pltpu.VMEM((high * channels, cols), bf16),
            pltpu.VMEM(((high - 2) * channels, cols), bf16),
            pltpu.VMEM((rows * channels, cols), bf16),
            pltpu.VMEM((rows * channels, lead + cols + width), bf16),
            pltpu.VMEM((16, cols), f32),
        ],
        flops=10**10,
    )(place, given, taps, biases[:, :, None])

    groups = [list(range(half)), list(range(half, row_count))]
    gathered = lax.all_gather(own, "row", axis=0, axis_index_groups=groups)

    across = call(
        across_kernel,
        jax.ShapeDtypeStruct((width, 2 * rows, DISPARITIES), f32),
        [SMEM(), SMEM(), VMEM()],
        flops=2 * 10**10,
    )(place, smooth, cost)

    kept, last = call(
        first_vertical_kernel,
        (
            jax.ShapeDtypeStruct((rows, DISPARITIES, width), f32),
            jax.ShapeDtypeStruct((DISPARITIES, width), bf16),
        ),
        [SMEM(), SMEM(), VMEM()],
        flops=2 * 10**9,
    )(place, smooth, gathered)

    swap = [(i, (i + half) % row_count) for i in range(row_count)]
    came = lax.ppermute(last, "row", swap)

    return call(
        second_vertical_kernel,
        jax.ShapeDtypeStruct((rows, width, DISPARITIES), f32),
        [SMEM(), SMEM(), VMEM(), VMEM(), VMEM(), VMEM()],
        [pltpu.VMEM((rows, DISPARITIES, width), f32)],
        flops=3 * 10**9,
    )(place, smooth, gathered, kept, came, across)


def solution(mesh):
    return jax.shard_map(
        per_device,
        mesh=mesh,
        in_specs=(P(None, "row", None, "col"), P(), P(), P("row", "col"), P("row", "col"), P()),
        out_specs=P("row", "col", None),
        check_vma=False,
    )
```

```python
import functools

import jax
import jax.numpy as jnp
from jax import lax
from jax.experimental import pallas as pl
from jax.experimental.pallas import tpu as pltpu
from jax.sharding import PartitionSpec as P

DISPARITIES = 128
OFF_MOST = 256
SUB = 8
REGS = DISPARITIES // SUB
VMEM_LIMIT = 56 * 1024 * 1024


def lane_to_disparity(lane):
    return (lane % SUB) * REGS + lane // SUB


def disparity_to_lane(disparity):
    return (disparity % REGS) * SUB + disparity // REGS


def advance(state, cost, p1, p2):
    lanes = state[0].shape[1]
    row = lax.broadcasted_iota(jnp.int32, (SUB, lanes), 0)
    below = jnp.where(row == 0, jnp.inf, pltpu.roll(state[-1], 1, 0))
    above = jnp.where(row == SUB - 1, jnp.inf, pltpu.roll(state[0], SUB - 1, 0))
    least = list(state)
    while len(least) > 1:
        least = [jnp.minimum(a, b) for a, b in zip(least[::2], least[1::2])]
    least = least[0]
    for turn in (4, 2, 1):
        least = jnp.minimum(least, pltpu.roll(least, turn, 0))
    lower = [below] + state[:-1]
    upper = state[1:] + [above]
    fresh = []
    for s, l, u, c in zip(state, lower, upper, cost):
        t = jnp.minimum(s, jnp.minimum(l, u) + p1)
        fresh.append(c + jnp.minimum(t - least, p2))
    return fresh


def charges(charge_ref):
    return (
        charge_ref[0].astype(jnp.float32) * (1.0 / 64.0),
        charge_ref[1].astype(jnp.float32) * (1.0 / 64.0),
    )


def registers(array):
    return [array[SUB * v : SUB * (v + 1)] for v in range(REGS)]


def band_kernel(
    place_ref, given_ref, filter_ref, bias_ref, cost_ref, own_ref,
    maps_a, maps_b, left_unit, right_unit, present,
):
    parts, _, channels, width = given_ref.shape
    layers = filter_ref.shape[0]
    rows = own_ref.shape[0]
    cols = parts * width
    high = rows + 2 * layers
    first_row = place_ref[0] * rows
    rows_total = place_ref[1] * rows
    own = place_ref[2]
    lead = (OFF_MOST + 2 * width - 1) // width * width

    for p in range(parts):
        present[:, p * width : (p + 1) * width] = given_ref[p, 2 * high, 0:16, :].astype(
            jnp.float32
        )
    right_unit[:, 0:lead] = jnp.zeros((rows * channels, lead), jnp.bfloat16)
    right_unit[:, lead + cols :] = jnp.zeros((rows * channels, width), jnp.bfloat16)

    column = lax.broadcasted_iota(jnp.int32, (1, cols), 1)
    for image in range(2):

        @pl.loop(0, high)
        def _(row):
            for p in range(parts):
                maps_a[pl.ds(pl.multiple_of(row * channels, channels), channels),
                       p * width : (p + 1) * width] = given_ref[p, image * high + row]

        for layer in range(layers):
            source, target = (maps_a, maps_b) if layer % 2 == 0 else (maps_b, maps_a)
            margin = layers - 1 - layer

            @pl.loop(0, rows + 2 * margin, unroll=2)
            def _(row):
                start = pl.multiple_of(row * channels, channels)
                window = source[pl.ds(start, 3 * channels), :]
                taps = jnp.dot(filter_ref[layer], window, preferred_element_type=jnp.float32)
                before = pltpu.roll(taps[:channels], 1, 1)
                after = pltpu.roll(taps[2 * channels :], cols - 1, 1)
                z = taps[channels : 2 * channels] + jnp.where(column == 0, 0.0, before)
                z = z + jnp.where(column == cols - 1, 0.0, after) + bias_ref[layer]
                if layer < layers - 1:
                    there = first_row - margin + row
                    inside = jnp.logical_and(there >= 0, there < rows_total)
                    z = jnp.maximum(z, 0.0) * jnp.where(inside, 1.0, 0.0)
                    target[pl.ds(start, channels), :] = z.astype(jnp.bfloat16)
                else:
                    scale = lax.rsqrt(jnp.sum(z * z, axis=0, keepdims=True) + 1e-06)
                    unit = (z * scale).astype(jnp.bfloat16)
                    if image == 0:
                        seen = present[pl.ds(row, 1), :]
                        unit = jnp.where(seen > 0.5, unit.astype(jnp.float32), 0.0)
                        left_unit[pl.ds(start, channels), :] = unit.astype(jnp.bfloat16)
                    else:
                        right_unit[pl.ds(start, channels), lead : lead + cols] = unit

    lane = lax.broadcasted_iota(jnp.int32, (width, DISPARITIES), 1)
    place = lax.broadcasted_iota(jnp.int32, (width, DISPARITIES), 0)

    @pl.loop(0, parts)
    def _(p):
        shift_block = given_ref[p, 2 * high, 16:32, :].astype(jnp.float32)
        shift = jnp.max(shift_block).astype(jnp.int32)
        base = p * width - shift + lead
        block = base // width
        ahead = place + (base - block * width)
        index = (ahead - lane) & (DISPARITIES - 1)
        turned = (ahead - lane_to_disparity(lane)) & (DISPARITIES - 1)
        start = pl.multiple_of((block - 1) * width, width)
        here = pl.multiple_of(p * width, width)
        for y in range(rows):
            left = left_unit[y * channels : (y + 1) * channels, pl.ds(here, width)]
            right = right_unit[y * channels : (y + 1) * channels, pl.ds(start, 3 * width)]
            product = lax.dot_general(
                left, right, (((0,), (0,)), ((), ())), preferred_element_type=jnp.float32
            )
            chosen = jnp.where(lane <= ahead, product[:, width : 2 * width], product[:, :width])
            chosen = jnp.where(lane <= ahead - width, product[:, 2 * width :], chosen)
            cost_ref[pl.ds(here, width), y, :] = 1.0 - jnp.take_along_axis(
                chosen, index, axis=1, mode="promise_in_bounds"
            )

            @pl.when(p == own)
            def _():
                mine = jnp.take_along_axis(chosen, turned, axis=1, mode="promise_in_bounds")
                own_ref[y] = (1.0 - mine).T.astype(jnp.bfloat16)


def across_kernel(place_ref, charge_ref, cost_ref, kept_ref):
    cols, rows, _ = cost_ref.shape
    width = kept_ref.shape[0]
    parts = cols // width
    own = place_ref[2]
    p1, p2 = charges(charge_ref)
    lane = lax.broadcasted_iota(jnp.int32, (rows, DISPARITIES), 1)
    from_lower = jnp.where(lane == 0, jnp.inf, p1)
    from_upper = jnp.where(lane == DISPARITIES - 1, jnp.inf, p1)

    def one(state, jump, cost):
        near = jnp.minimum(
            pltpu.roll(state, 1, 1) + from_lower,
            pltpu.roll(state, DISPARITIES - 1, 1) + from_upper,
        )
        walked = cost + jnp.minimum(state, near)
        cheapest = jnp.min(cost, axis=1, keepdims=True)
        fresh = jnp.minimum(walked, cost + jump)
        least = jnp.minimum(jnp.min(walked, axis=1, keepdims=True), cheapest + jump)
        return fresh, least + p2

    def segment(p, carry):
        first_col = p * width
        last_col = cols - 1 - p * width

        def run(keep_right, keep_left, carry):
            def body(i, carry):
                right, right_jump, left, left_jump = carry
                fresh_right, next_right = one(right, right_jump, cost_ref[first_col + i])
                fresh_left, next_left = one(left, left_jump, cost_ref[last_col - i])
                if keep_right:
                    kept_ref[i, 0:rows] = fresh_right - (right_jump - p2)
                if keep_left:
                    kept_ref[width - 1 - i, rows : 2 * rows] = fresh_left - (left_jump - p2)
                return fresh_right, next_right, fresh_left, next_left

            return lax.fori_loop(0, width, body, carry, unroll=8)

        choice = jnp.where(p == own, 1, 0) + jnp.where(parts - 1 - p == own, 2, 0)
        carry = lax.switch(
            choice,
            [functools.partial(run, bool(k & 1), bool(k & 2)) for k in range(4)],
            carry,
        )
        right, right_jump, left, left_jump = carry
        right, left = right - (right_jump - p2), left - (left_jump - p2)
        level = jnp.zeros_like(right_jump) + p2
        return right, level, left, level

    zero = jnp.zeros((rows, DISPARITIES), jnp.float32)
    level = jnp.zeros((rows, 1), jnp.float32) + p2
    lax.fori_loop(0, parts, segment, (zero, level, zero, level))


def down_or_up(forward, first_own, cost_ref, state, p1, p2, keep):
    group, rows = cost_ref.shape[:2]
    count = group * rows

    def body(i, state):
        row = jnp.where(forward, i, count - 1 - i)
        block = row // rows
        inner = row - block * rows
        cost = cost_ref[block, inner].astype(jnp.float32)
        fresh = advance(list(state), registers(cost), p1, p2)

        @pl.when(block == first_own)
        def _():
            keep(inner, jnp.concatenate(fresh, axis=0))

        return tuple(fresh)

    return lax.fori_loop(0, count, body, state, unroll=4)


def first_vertical_kernel(place_ref, charge_ref, *refs):
    *block_refs, kept_ref, last_ref, cost_ref = refs
    p1, p2 = charges(charge_ref)
    group, _, _, width = cost_ref.shape
    for k, block_ref in enumerate(block_refs):
        cost_ref[lax.rem(place_ref[4] + group - k, group)] = block_ref[...]
    state = tuple(jnp.zeros((SUB, width), jnp.float32) for _ in range(REGS))

    def keep(row, value):
        kept_ref[row] = value

    final = down_or_up(place_ref[3] == 0, place_ref[4], cost_ref, state, p1, p2, keep)
    last_ref[...] = jnp.concatenate(final, axis=0).astype(jnp.bfloat16)


def second_vertical_kernel(place_ref, charge_ref, *refs):
    *block_refs, kept_ref, came_ref, across_ref, out_ref, total, cost_ref = refs
    p1, p2 = charges(charge_ref)
    group = cost_ref.shape[0]
    for k, block_ref in enumerate(block_refs):
        cost_ref[lax.rem(place_ref[4] + group - k, group)] = block_ref[...]
    rows, _, width = kept_ref.shape
    state = tuple(registers(came_ref[...].astype(jnp.float32)))

    def keep(row, value):
        total[row] = value + kept_ref[row]

    down_or_up(place_ref[3] != 0, place_ref[4], cost_ref, state, p1, p2, keep)
    lane = lax.broadcasted_iota(jnp.int32, (width, DISPARITIES), 1)
    index = disparity_to_lane(lane)
    for row in range(rows):
        vertical = jnp.take_along_axis(total[row].T, index, axis=1, mode="promise_in_bounds")
        out_ref[row] = vertical + (across_ref[:, row, :] + across_ref[:, rows + row, :])


SMEM = functools.partial(pl.BlockSpec, memory_space=pltpu.SMEM)
VMEM = functools.partial(pl.BlockSpec, memory_space=pltpu.VMEM)


def call(kernel, outs, specs, scratch=(), flops=0):
    return pl.pallas_call(
        kernel,
        out_shape=outs,
        in_specs=specs,
        out_specs=jax.tree.map(lambda _: VMEM(), outs),
        scratch_shapes=list(scratch),
        compiler_params=pltpu.CompilerParams(vmem_limit_bytes=VMEM_LIMIT),
        cost_estimate=pl.CostEstimate(flops=flops, bytes_accessed=1 << 22, transcendentals=0),
    )


def per_device(activations, filters, biases, present, shifts, smooth):
    _, rows, channels, width = activations.shape
    layers = filters.shape[0]
    high = rows + 2 * layers
    row_rank, row_count = lax.axis_index("row"), lax.axis_size("row")
    col_rank, parts = lax.axis_index("col"), lax.axis_size("col")
    half = row_count // 2
    cols = parts * width
    place = jnp.stack(
        [row_rank, jnp.int32(row_count), col_rank, row_rank // half, row_rank % half]
    ).astype(jnp.int32)

    downward = [(i, i + 1) for i in range(row_count - 1)]
    upward = [(i + 1, i) for i in range(row_count - 1)]
    before = lax.ppermute(activations[:, rows - layers :], "row", downward)
    after = lax.ppermute(activations[:, :layers], "row", upward)
    extra = jnp.concatenate(
        [
            present.astype(jnp.bfloat16),
            jnp.zeros((16 - rows, width), jnp.bfloat16),
            jnp.broadcast_to(shifts.astype(jnp.bfloat16), (channels - 16, width)),
        ],
        axis=0,
    )
    block = jnp.concatenate([before, activations, after], axis=1)
    block = jnp.concatenate([block.reshape(2 * high, channels, width), extra[None]], axis=0)
    given = lax.all_gather(block, "col", axis=0)
    taps = jnp.transpose(filters, (0, 2, 3, 1, 4)).reshape(layers, 3 * channels, 3 * channels)

    f32, bf16 = jnp.float32, jnp.bfloat16
    lead = (OFF_MOST + 2 * width - 1) // width * width
    cost, own = call(
        band_kernel,
        (
            jax.ShapeDtypeStruct((cols, rows, DISPARITIES), f32),
            jax.ShapeDtypeStruct((rows, DISPARITIES, width), bf16),
        ),
        [SMEM(), VMEM(), VMEM(), VMEM()],
        [
            pltpu.VMEM((high * channels, cols), bf16),
            pltpu.VMEM(((high - 2) * channels, cols), bf16),
            pltpu.VMEM((rows * channels, cols), bf16),
            pltpu.VMEM((rows * channels, lead + cols + width), bf16),
            pltpu.VMEM((16, cols), f32),
        ],
        flops=10**10,
    )(place, given, taps, biases[:, :, None])

    blocks = [own]
    for k in range(1, half):
        turn = [(i, i // half * half + (i + k) % half) for i in range(row_count)]
        blocks.append(lax.ppermute(own, "row", turn))

    across = call(
        across_kernel,
        jax.ShapeDtypeStruct((width, 2 * rows, DISPARITIES), f32),
        [SMEM(), SMEM(), VMEM()],
        flops=2 * 10**10,
    )(place, smooth, cost)
    *blocks, across = lax.optimization_barrier((*blocks, across))

    joined = pltpu.VMEM((half, rows, DISPARITIES, width), bf16)
    kept, last = call(
        first_vertical_kernel,
        (
            jax.ShapeDtypeStruct((rows, DISPARITIES, width), f32),
            jax.ShapeDtypeStruct((DISPARITIES, width), bf16),
        ),
        [SMEM(), SMEM()] + [VMEM()] * half,
        [joined],
        flops=2 * 10**9,
    )(place, smooth, *blocks)

    swap = [(i, (i + half) % row_count) for i in range(row_count)]
    came = lax.ppermute(last, "row", swap)

    return call(
        second_vertical_kernel,
        jax.ShapeDtypeStruct((rows, width, DISPARITIES), f32),
        [SMEM(), SMEM()] + [VMEM()] * (half + 3),
        [pltpu.VMEM((rows, DISPARITIES, width), f32), joined],
        flops=3 * 10**9,
    )(place, smooth, *blocks, kept, came, across)


def solution(mesh):
    return jax.shard_map(
        per_device,
        mesh=mesh,
        in_specs=(P(None, "row", None, "col"), P(), P(), P("row", "col"), P("row", "col"), P()),
        out_specs=P("row", "col", None),
        check_vma=False,
    )
```

```python
import functools

import jax
import jax.numpy as jnp
from jax import lax
from jax.experimental import pallas as pl
from jax.experimental.pallas import tpu as pltpu
from jax.sharding import PartitionSpec as P

DISPARITIES = 128
OFF_MOST = 256
SUB = 8
REGS = DISPARITIES // SUB
VMEM_LIMIT = 56 * 1024 * 1024


def lane_to_disparity(lane):
    return (lane % SUB) * REGS + lane // SUB


def disparity_to_lane(disparity):
    return (disparity % REGS) * SUB + disparity // REGS


def advance(state, cost, p1, p2):
    lanes = state[0].shape[1]
    row = lax.broadcasted_iota(jnp.int32, (SUB, lanes), 0)
    below = jnp.where(row == 0, jnp.inf, pltpu.roll(state[-1], 1, 0))
    above = jnp.where(row == SUB - 1, jnp.inf, pltpu.roll(state[0], SUB - 1, 0))
    least = list(state)
    while len(least) > 1:
        least = [jnp.minimum(a, b) for a, b in zip(least[::2], least[1::2])]
    least = least[0]
    turned = [least] + [pltpu.roll(least, turn, 0) for turn in range(1, SUB)]
    while len(turned) > 1:
        turned = [jnp.minimum(a, b) for a, b in zip(turned[::2], turned[1::2])]
    least = turned[0]
    lower = [below] + state[:-1]
    upper = state[1:] + [above]
    fresh = []
    for s, l, u, c in zip(state, lower, upper, cost):
        t = jnp.minimum(s, jnp.minimum(l, u) + p1)
        fresh.append(c + jnp.minimum(t - least, p2))
    return fresh


def charges(charge_ref):
    return (
        charge_ref[0].astype(jnp.float32) * (1.0 / 64.0),
        charge_ref[1].astype(jnp.float32) * (1.0 / 64.0),
    )


def registers(array):
    return [array[SUB * v : SUB * (v + 1)] for v in range(REGS)]


def band_kernel(
    place_ref, given_ref, filter_ref, bias_ref, cost_ref, own_ref,
    maps_a, maps_b, left_unit, right_unit, present,
):
    parts, _, channels, width = given_ref.shape
    layers = filter_ref.shape[0]
    rows = own_ref.shape[0]
    cols = parts * width
    high = rows + 2 * layers
    first_row = place_ref[0] * rows
    rows_total = place_ref[1] * rows
    own = place_ref[2]
    lead = (OFF_MOST + 2 * width - 1) // width * width

    for p in range(parts):
        present[:, p * width : (p + 1) * width] = given_ref[p, 2 * high, 0:16, :].astype(
            jnp.float32
        )
    right_unit[:, 0:lead] = jnp.zeros((rows * channels, lead), jnp.bfloat16)
    right_unit[:, lead + cols :] = jnp.zeros((rows * channels, width), jnp.bfloat16)

    column = lax.broadcasted_iota(jnp.int32, (1, cols), 1)
    for image in range(2):

        @pl.loop(0, high)
        def _(row):
            for p in range(parts):
                maps_a[pl.ds(pl.multiple_of(row * channels, channels), channels),
                       p * width : (p + 1) * width] = given_ref[p, image * high + row]

        for layer in range(layers):
            source, target = (maps_a, maps_b) if layer % 2 == 0 else (maps_b, maps_a)
            margin = layers - 1 - layer

            @pl.loop(0, rows + 2 * margin, unroll=2)
            def _(row):
                start = pl.multiple_of(row * channels, channels)
                window = source[pl.ds(start, 3 * channels), :]
                taps = jnp.dot(filter_ref[layer], window, preferred_element_type=jnp.float32)
                before = pltpu.roll(taps[:channels], 1, 1)
                after = pltpu.roll(taps[2 * channels :], cols - 1, 1)
                z = taps[channels : 2 * channels] + jnp.where(column == 0, 0.0, before)
                z = z + jnp.where(column == cols - 1, 0.0, after) + bias_ref[layer]
                if layer < layers - 1:
                    there = first_row - margin + row
                    inside = jnp.logical_and(there >= 0, there < rows_total)
                    z = jnp.maximum(z, 0.0) * jnp.where(inside, 1.0, 0.0)
                    target[pl.ds(start, channels), :] = z.astype(jnp.bfloat16)
                else:
                    scale = lax.rsqrt(jnp.sum(z * z, axis=0, keepdims=True) + 1e-06)
                    unit = (z * scale).astype(jnp.bfloat16)
                    if image == 0:
                        seen = present[pl.ds(row, 1), :]
                        unit = jnp.where(seen > 0.5, unit.astype(jnp.float32), 0.0)
                        left_unit[pl.ds(start, channels), :] = unit.astype(jnp.bfloat16)
                    else:
                        right_unit[pl.ds(start, channels), lead : lead + cols] = unit

    lane = lax.broadcasted_iota(jnp.int32, (width, DISPARITIES), 1)
    place = lax.broadcasted_iota(jnp.int32, (width, DISPARITIES), 0)

    @pl.loop(0, parts)
    def _(p):
        shift_block = given_ref[p, 2 * high, 16:32, :].astype(jnp.float32)
        shift = jnp.max(shift_block).astype(jnp.int32)
        base = p * width - shift + lead
        block = base // width
        ahead = place + (base - block * width)
        index = (ahead - lane_to_disparity(lane)) & (DISPARITIES - 1)
        start = pl.multiple_of((block - 1) * width, width)
        here = pl.multiple_of(p * width, width)
        for y in range(rows):
            left = left_unit[y * channels : (y + 1) * channels, pl.ds(here, width)]
            right = right_unit[y * channels : (y + 1) * channels, pl.ds(start, 3 * width)]
            product = lax.dot_general(
                left, right, (((0,), (0,)), ((), ())), preferred_element_type=jnp.float32
            )
            chosen = jnp.where(lane <= ahead, product[:, width : 2 * width], product[:, :width])
            chosen = jnp.where(lane <= ahead - width, product[:, 2 * width :], chosen)
            chosen = 1.0 - jnp.take_along_axis(chosen, index, axis=1, mode="promise_in_bounds")
            cost_ref[pl.ds(here, width), y, :] = chosen

            @pl.when(p == own)
            def _():
                own_ref[y] = chosen.T.astype(jnp.bfloat16)


def across_kernel(place_ref, charge_ref, cost_ref, kept_ref):
    cols, rows, _ = cost_ref.shape
    width = kept_ref.shape[0]
    parts = cols // width
    own = place_ref[2]
    p1, p2 = charges(charge_ref)

    def segment(p, state):
        first_col = p * width
        last_col = cols - 1 - p * width

        def run(keep_right, keep_left, state):
            def body(i, state):
                pair = [cost_ref[first_col + i], cost_ref[last_col - i]]
                cost = jnp.concatenate(pair, axis=0).T
                fresh = advance(list(state), registers(cost), p1, p2)
                if keep_right or keep_left:
                    back = jnp.concatenate(fresh, axis=0).T
                if keep_right:
                    kept_ref[i, 0:rows] = back[0:rows]
                if keep_left:
                    kept_ref[width - 1 - i, rows : 2 * rows] = back[rows : 2 * rows]
                return tuple(fresh)

            return lax.fori_loop(0, width, body, state, unroll=8)

        choice = jnp.where(p == own, 1, 0) + jnp.where(parts - 1 - p == own, 2, 0)
        return lax.switch(
            choice,
            [functools.partial(run, bool(k & 1), bool(k & 2)) for k in range(4)],
            state,
        )

    state = tuple(jnp.zeros((SUB, 2 * rows), jnp.float32) for _ in range(REGS))
    lax.fori_loop(0, parts, segment, state)


def down_or_up(forward, first_own, cost_ref, state, p1, p2, keep):
    group, rows = cost_ref.shape[:2]

    def block(b, state):
        member = jnp.where(forward, b, group - 1 - b)

        def run(kept, state):
            for i in range(rows):
                inner = jnp.where(forward, i, rows - 1 - i)
                cost = cost_ref[member, inner].astype(jnp.float32)
                state = advance(list(state), registers(cost), p1, p2)
                if kept:
                    keep(inner, jnp.concatenate(state, axis=0))
            return tuple(state)

        return lax.cond(
            member == first_own,
            functools.partial(run, True),
            functools.partial(run, False),
            state,
        )

    return lax.fori_loop(0, group, block, state)


def first_vertical_kernel(place_ref, charge_ref, *refs):
    *block_refs, kept_ref, last_ref, cost_ref = refs
    p1, p2 = charges(charge_ref)
    group, _, _, width = cost_ref.shape
    for k, block_ref in enumerate(block_refs):
        cost_ref[lax.rem(place_ref[4] + group - k, group)] = block_ref[...]
    state = tuple(jnp.zeros((SUB, width), jnp.float32) for _ in range(REGS))

    def keep(row, value):
        kept_ref[row] = value

    final = down_or_up(place_ref[3] == 0, place_ref[4], cost_ref, state, p1, p2, keep)
    last_ref[...] = jnp.concatenate(final, axis=0).astype(jnp.bfloat16)


def second_vertical_kernel(place_ref, charge_ref, *refs):
    *block_refs, kept_ref, came_ref, across_ref, out_ref, total, cost_ref = refs
    p1, p2 = charges(charge_ref)
    group = cost_ref.shape[0]
    for k, block_ref in enumerate(block_refs):
        cost_ref[lax.rem(place_ref[4] + group - k, group)] = block_ref[...]
    rows, _, width = kept_ref.shape
    state = tuple(registers(came_ref[...].astype(jnp.float32)))

    def keep(row, value):
        total[row] = value + kept_ref[row]

    down_or_up(place_ref[3] != 0, place_ref[4], cost_ref, state, p1, p2, keep)
    lane = lax.broadcasted_iota(jnp.int32, (width, DISPARITIES), 1)
    index = disparity_to_lane(lane)
    for row in range(rows):
        value = total[row].T + (across_ref[:, row, :] + across_ref[:, rows + row, :])
        out_ref[row] = jnp.take_along_axis(value, index, axis=1, mode="promise_in_bounds")


SMEM = functools.partial(pl.BlockSpec, memory_space=pltpu.SMEM)
VMEM = functools.partial(pl.BlockSpec, memory_space=pltpu.VMEM)


def call(kernel, outs, specs, scratch=(), flops=0):
    return pl.pallas_call(
        kernel,
        out_shape=outs,
        in_specs=specs,
        out_specs=jax.tree.map(lambda _: VMEM(), outs),
        scratch_shapes=list(scratch),
        compiler_params=pltpu.CompilerParams(vmem_limit_bytes=VMEM_LIMIT),
        cost_estimate=pl.CostEstimate(flops=flops, bytes_accessed=1 << 22, transcendentals=0),
    )


def per_device(activations, filters, biases, present, shifts, smooth):
    _, rows, channels, width = activations.shape
    layers = filters.shape[0]
    high = rows + 2 * layers
    row_rank, row_count = lax.axis_index("row"), lax.axis_size("row")
    col_rank, parts = lax.axis_index("col"), lax.axis_size("col")
    half = row_count // 2
    cols = parts * width
    place = jnp.stack(
        [row_rank, jnp.int32(row_count), col_rank, row_rank // half, row_rank % half]
    ).astype(jnp.int32)

    downward = [(i, i + 1) for i in range(row_count - 1)]
    upward = [(i + 1, i) for i in range(row_count - 1)]
    before = lax.ppermute(activations[:, rows - layers :], "row", downward)
    after = lax.ppermute(activations[:, :layers], "row", upward)
    extra = jnp.concatenate(
        [
            present.astype(jnp.bfloat16),
            jnp.zeros((16 - rows, width), jnp.bfloat16),
            jnp.broadcast_to(shifts.astype(jnp.bfloat16), (channels - 16, width)),
        ],
        axis=0,
    )
    block = jnp.concatenate([before, activations, after], axis=1)
    block = jnp.concatenate([block.reshape(2 * high, channels, width), extra[None]], axis=0)
    given = lax.all_gather(block, "col", axis=0)
    taps = jnp.transpose(filters, (0, 2, 3, 1, 4)).reshape(layers, 3 * channels, 3 * channels)

    f32, bf16 = jnp.float32, jnp.bfloat16
    lead = (OFF_MOST + 2 * width - 1) // width * width
    cost, own = call(
        band_kernel,
        (
            jax.ShapeDtypeStruct((cols, rows, DISPARITIES), f32),
            jax.ShapeDtypeStruct((rows, DISPARITIES, width), bf16),
        ),
        [SMEM(), VMEM(), VMEM(), VMEM()],
        [
            pltpu.VMEM((high * channels, cols), bf16),
            pltpu.VMEM(((high - 2) * channels, cols), bf16),
            pltpu.VMEM((rows * channels, cols), bf16),
            pltpu.VMEM((rows * channels, lead + cols + width), bf16),
            pltpu.VMEM((16, cols), f32),
        ],
        flops=10**10,
    )(place, given, taps, biases[:, :, None])

    blocks = [own]
    for k in range(1, half):
        turn = [(i, i // half * half + (i + k) % half) for i in range(row_count)]
        blocks.append(lax.ppermute(own, "row", turn))

    across = call(
        across_kernel,
        jax.ShapeDtypeStruct((width, 2 * rows, DISPARITIES), f32),
        [SMEM(), SMEM(), VMEM()],
        flops=2 * 10**10,
    )(place, smooth, cost)
    *blocks, across = lax.optimization_barrier((*blocks, across))

    joined = pltpu.VMEM((half, rows, DISPARITIES, width), bf16)
    kept, last = call(
        first_vertical_kernel,
        (
            jax.ShapeDtypeStruct((rows, DISPARITIES, width), f32),
            jax.ShapeDtypeStruct((DISPARITIES, width), bf16),
        ),
        [SMEM(), SMEM()] + [VMEM()] * half,
        [joined],
        flops=2 * 10**9,
    )(place, smooth, *blocks)

    swap = [(i, (i + half) % row_count) for i in range(row_count)]
    came = lax.ppermute(last, "row", swap)

    return call(
        second_vertical_kernel,
        jax.ShapeDtypeStruct((rows, width, DISPARITIES), f32),
        [SMEM(), SMEM()] + [VMEM()] * (half + 3),
        [pltpu.VMEM((rows, DISPARITIES, width), f32), joined],
        flops=3 * 10**9,
    )(place, smooth, *blocks, kept, came, across)


def solution(mesh):
    return jax.shard_map(
        per_device,
        mesh=mesh,
        in_specs=(P(None, "row", None, "col"), P(), P(), P("row", "col"), P("row", "col"), P()),
        out_specs=P("row", "col", None),
        check_vma=False,
    )
```

```python
import functools

import jax
import jax.numpy as jnp
from jax import lax
from jax.experimental import pallas as pl
from jax.experimental.pallas import tpu as pltpu
from jax.sharding import PartitionSpec as P

DISPARITIES = 128
OFF_MOST = 256
SUB = 8
REGS = DISPARITIES // SUB
MEBI = 1024 * 1024


def lane_to_disparity(lane):
    return (lane % SUB) * REGS + lane // SUB


def disparity_to_lane(disparity):
    return (disparity % REGS) * SUB + disparity // REGS


def advance(state, cost, p1, p2):
    lanes = state[0].shape[1]
    row = lax.broadcasted_iota(jnp.int32, (SUB, lanes), 0)
    below = jnp.where(row == 0, jnp.inf, pltpu.roll(state[-1], 1, 0))
    above = jnp.where(row == SUB - 1, jnp.inf, pltpu.roll(state[0], SUB - 1, 0))
    least = list(state)
    while len(least) > 1:
        least = [jnp.minimum(a, b) for a, b in zip(least[::2], least[1::2])]
    least = least[0]
    turned = [least] + [pltpu.roll(least, turn, 0) for turn in range(1, SUB)]
    while len(turned) > 1:
        turned = [jnp.minimum(a, b) for a, b in zip(turned[::2], turned[1::2])]
    least = turned[0]
    lower = [below] + state[:-1]
    upper = state[1:] + [above]
    fresh = []
    for s, l, u, c in zip(state, lower, upper, cost):
        t = jnp.minimum(s, jnp.minimum(l, u) + p1)
        fresh.append(c + jnp.minimum(t - least, p2))
    return fresh


def charges(charge_ref):
    return (
        charge_ref[0].astype(jnp.float32) * (1.0 / 64.0),
        charge_ref[1].astype(jnp.float32) * (1.0 / 64.0),
    )


def registers(array):
    return [array[SUB * v : SUB * (v + 1)] for v in range(REGS)]


def band_kernel(
    place_ref, given_ref, filter_ref, bias_ref, cost_ref, own_ref,
    maps_a, maps_b, left_unit, right_unit, present,
):
    parts, _, channels, width = given_ref.shape
    layers = filter_ref.shape[0]
    rows = own_ref.shape[0]
    cols = parts * width
    high = rows + 2 * layers
    first_row = place_ref[0] * rows
    rows_total = place_ref[1] * rows
    own = place_ref[2]
    lead = (OFF_MOST + 2 * width - 1) // width * width

    for p in range(parts):
        present[:, p * width : (p + 1) * width] = given_ref[p, 2 * high, 0:16, :].astype(
            jnp.float32
        )
    right_unit[:, 0:lead] = jnp.zeros((rows * channels, lead), jnp.bfloat16)
    right_unit[:, lead + cols :] = jnp.zeros((rows * channels, width), jnp.bfloat16)

    column = lax.broadcasted_iota(jnp.int32, (1, cols), 1)
    for image in range(2):

        @pl.loop(0, high)
        def _(row):
            for p in range(parts):
                maps_a[pl.ds(pl.multiple_of(row * channels, channels), channels),
                       p * width : (p + 1) * width] = given_ref[p, image * high + row]

        for layer in range(layers):
            source, target = (maps_a, maps_b) if layer % 2 == 0 else (maps_b, maps_a)
            margin = layers - 1 - layer

            steps = rows + 2 * margin

            @pl.loop(0, steps, unroll=max(k for k in range(1, 6) if steps % k == 0))
            def _(row):
                start = pl.multiple_of(row * channels, channels)
                window = source[pl.ds(start, 3 * channels), :]
                taps = jnp.dot(filter_ref[layer], window, preferred_element_type=jnp.float32)
                before = pltpu.roll(taps[:channels], 1, 1)
                after = pltpu.roll(taps[2 * channels :], cols - 1, 1)
                z = taps[channels : 2 * channels] + jnp.where(column == 0, 0.0, before)
                z = z + jnp.where(column == cols - 1, 0.0, after) + bias_ref[layer]
                if layer < layers - 1:
                    there = first_row - margin + row
                    inside = jnp.logical_and(there >= 0, there < rows_total)
                    z = jnp.maximum(z, 0.0) * jnp.where(inside, 1.0, 0.0)
                    target[pl.ds(start, channels), :] = z.astype(jnp.bfloat16)
                else:
                    scale = lax.rsqrt(jnp.sum(z * z, axis=0, keepdims=True) + 1e-06)
                    unit = (z * scale).astype(jnp.bfloat16)
                    if image == 0:
                        seen = present[pl.ds(row, 1), :]
                        unit = jnp.where(seen > 0.5, unit.astype(jnp.float32), 0.0)
                        left_unit[pl.ds(start, channels), :] = unit.astype(jnp.bfloat16)
                    else:
                        right_unit[pl.ds(start, channels), lead : lead + cols] = unit

    lane = lax.broadcasted_iota(jnp.int32, (width, DISPARITIES), 1)
    place = lax.broadcasted_iota(jnp.int32, (width, DISPARITIES), 0)

    @pl.loop(0, parts)
    def _(p):
        shift_block = given_ref[p, 2 * high, 16:32, :].astype(jnp.float32)
        shift = jnp.max(shift_block).astype(jnp.int32)
        base = p * width - shift + lead
        block = base // width
        ahead = place + (base - block * width)
        index = (ahead - lane_to_disparity(lane)) & (DISPARITIES - 1)
        start = pl.multiple_of((block - 1) * width, width)
        here = pl.multiple_of(p * width, width)

        def tile_costs(mine):
            for y in range(rows):
                left = left_unit[y * channels : (y + 1) * channels, pl.ds(here, width)]
                right = right_unit[y * channels : (y + 1) * channels, pl.ds(start, 3 * width)]
                product = lax.dot_general(
                    left, right, (((0,), (0,)), ((), ())), preferred_element_type=jnp.float32
                )
                chosen = jnp.where(lane <= ahead, product[:, width : 2 * width], product[:, :width])
                chosen = jnp.where(lane <= ahead - width, product[:, 2 * width :], chosen)
                chosen = jnp.take_along_axis(chosen, index, axis=1, mode="promise_in_bounds")
                chosen = 1.0 - chosen
                cost_ref[pl.ds(here, width), y, :] = chosen
                if mine:
                    own_ref[y] = chosen.T.astype(jnp.bfloat16)

        pl.when(p == own)(functools.partial(tile_costs, True))
        pl.when(p != own)(functools.partial(tile_costs, False))


def across_kernel(second, place_ref, charge_ref, cost_ref, *refs):
    kept_ref, last_ref = refs[-2:]
    cols = cost_ref.shape[0]
    width, rows, _ = kept_ref.shape
    parts = cols // width
    own = place_ref[2]
    p1, p2 = charges(charge_ref)

    def segment(p, state):
        first_col = p * width
        last_col = cols - 1 - p * width

        def run(keep_right, keep_left, state):
            def body(i, state):
                pair = [cost_ref[first_col + i], cost_ref[last_col - i]]
                cost = jnp.concatenate(pair, axis=0).T
                fresh = advance(list(state), registers(cost), p1, p2)
                if keep_right or keep_left:
                    back = jnp.concatenate(fresh, axis=0).T
                if keep_right:
                    kept_ref[i] = back[0:rows]
                if keep_left:
                    kept_ref[width - 1 - i] = back[rows : 2 * rows]
                return tuple(fresh)

            return lax.fori_loop(0, width, body, state, unroll=16)

        choice = jnp.where(p == own, 1, 0) + jnp.where(parts - 1 - p == own, 2, 0)
        return lax.switch(
            choice,
            [functools.partial(run, k == 1, k == 2) for k in range(3)],
            state,
        )

    if second:
        state = tuple(registers(refs[0][...]))
        span = (parts // 2, parts)
    else:
        state = tuple(jnp.zeros((SUB, 2 * rows), jnp.float32) for _ in range(REGS))
        span = (0, parts // 2)
    last_ref[...] = jnp.concatenate(lax.fori_loop(*span, segment, state), axis=0)


def down_or_up(forward, first_own, cost_ref, state, p1, p2, keep):
    group, rows = cost_ref.shape[:2]

    def block(b, state):
        member = jnp.where(forward, b, group - 1 - b)

        def run(kept, state):
            for i in range(rows):
                inner = jnp.where(forward, i, rows - 1 - i)
                cost = cost_ref[member, inner].astype(jnp.float32)
                state = advance(list(state), registers(cost), p1, p2)
                if kept:
                    keep(inner, jnp.concatenate(state, axis=0))
            return tuple(state)

        return lax.cond(
            member == first_own,
            functools.partial(run, True),
            functools.partial(run, False),
            state,
        )

    return lax.fori_loop(0, group, block, state)


def first_vertical_kernel(place_ref, charge_ref, *refs):
    *block_refs, kept_ref, last_ref, cost_ref = refs
    p1, p2 = charges(charge_ref)
    group, _, _, width = cost_ref.shape
    for k, block_ref in enumerate(block_refs):
        cost_ref[lax.rem(place_ref[4] + group - k, group)] = block_ref[...]
    state = tuple(jnp.zeros((SUB, width), jnp.float32) for _ in range(REGS))

    def keep(row, value):
        kept_ref[row] = value

    final = down_or_up(place_ref[3] == 0, place_ref[4], cost_ref, state, p1, p2, keep)
    last_ref[...] = jnp.concatenate(final, axis=0).astype(jnp.bfloat16)


def second_vertical_kernel(place_ref, charge_ref, *refs):
    *block_refs, kept_ref, came_ref, early_ref, late_ref, out_ref, total, cost_ref = refs
    p1, p2 = charges(charge_ref)
    group = cost_ref.shape[0]
    for k, block_ref in enumerate(block_refs):
        cost_ref[lax.rem(place_ref[4] + group - k, group)] = block_ref[...]
    rows, _, width = kept_ref.shape
    state = tuple(registers(came_ref[...].astype(jnp.float32)))

    def keep(row, value):
        total[row] = value + kept_ref[row]

    down_or_up(place_ref[3] != 0, place_ref[4], cost_ref, state, p1, p2, keep)
    lane = lax.broadcasted_iota(jnp.int32, (width, DISPARITIES), 1)
    index = disparity_to_lane(lane)
    for row in range(rows):
        value = total[row].T + (early_ref[:, row, :] + late_ref[:, row, :])
        out_ref[row] = jnp.take_along_axis(value, index, axis=1, mode="promise_in_bounds")


SMEM = functools.partial(pl.BlockSpec, memory_space=pltpu.SMEM)
VMEM = functools.partial(pl.BlockSpec, memory_space=pltpu.VMEM)


def call(kernel, outs, specs, scratch=(), flops=0, vmem=20):
    return pl.pallas_call(
        kernel,
        out_shape=outs,
        in_specs=specs,
        out_specs=jax.tree.map(lambda _: VMEM(), outs),
        scratch_shapes=list(scratch),
        compiler_params=pltpu.CompilerParams(vmem_limit_bytes=vmem * MEBI),
        cost_estimate=pl.CostEstimate(flops=flops, bytes_accessed=1 << 22, transcendentals=0),
    )


def per_device(activations, filters, biases, present, shifts, smooth):
    _, rows, channels, width = activations.shape
    layers = filters.shape[0]
    high = rows + 2 * layers
    row_rank, row_count = lax.axis_index("row"), lax.axis_size("row")
    col_rank, parts = lax.axis_index("col"), lax.axis_size("col")
    half = row_count // 2
    cols = parts * width
    place = jnp.stack(
        [row_rank, jnp.int32(row_count), col_rank, row_rank // half, row_rank % half]
    ).astype(jnp.int32)

    downward = [(i, i + 1) for i in range(row_count - 1)]
    upward = [(i + 1, i) for i in range(row_count - 1)]
    before = lax.ppermute(activations[:, rows - layers :], "row", downward)
    after = lax.ppermute(activations[:, :layers], "row", upward)
    extra = jnp.concatenate(
        [
            present.astype(jnp.bfloat16),
            jnp.zeros((16 - rows, width), jnp.bfloat16),
            jnp.broadcast_to(shifts.astype(jnp.bfloat16), (channels - 16, width)),
        ],
        axis=0,
    )
    block = jnp.concatenate([before, activations, after], axis=1)
    block = jnp.concatenate([block.reshape(2 * high, channels, width), extra[None]], axis=0)
    given = lax.all_gather(block, "col", axis=0)
    taps = jnp.transpose(filters, (0, 2, 3, 1, 4)).reshape(layers, 3 * channels, 3 * channels)

    f32, bf16 = jnp.float32, jnp.bfloat16
    lead = (OFF_MOST + 2 * width - 1) // width * width
    cost, own = call(
        band_kernel,
        (
            jax.ShapeDtypeStruct((cols, rows, DISPARITIES), f32),
            jax.ShapeDtypeStruct((rows, DISPARITIES, width), bf16),
        ),
        [SMEM(), VMEM(), VMEM(), VMEM()],
        [
            pltpu.VMEM((high * channels, cols), bf16),
            pltpu.VMEM(((high - 2) * channels, cols), bf16),
            pltpu.VMEM((rows * channels, cols), bf16),
            pltpu.VMEM((rows * channels, lead + cols + width), bf16),
            pltpu.VMEM((16, cols), f32),
        ],
        flops=10**10,
        vmem=40,
    )(place, given, taps, biases[:, :, None])

    blocks = [own]
    for k in range(1, half):
        turn = [(i, i // half * half + (i + k) % half) for i in range(row_count)]
        blocks.append(lax.ppermute(own, "row", turn))

    halves = (
        jax.ShapeDtypeStruct((width, rows, DISPARITIES), f32),
        jax.ShapeDtypeStruct((DISPARITIES, 2 * rows), f32),
    )
    early, state = call(
        functools.partial(across_kernel, False),
        halves,
        [SMEM(), SMEM(), VMEM()],
        flops=10**10,
    )(place, smooth, cost)
    *blocks, state = lax.optimization_barrier((*blocks, state))

    joined = pltpu.VMEM((half, rows, DISPARITIES, width), bf16)
    kept, last = call(
        first_vertical_kernel,
        (
            jax.ShapeDtypeStruct((rows, DISPARITIES, width), f32),
            jax.ShapeDtypeStruct((DISPARITIES, width), bf16),
        ),
        [SMEM(), SMEM()] + [VMEM()] * half,
        [joined],
        flops=2 * 10**9,
    )(place, smooth, *blocks)

    swap = [(i, (i + half) % row_count) for i in range(row_count)]
    last, state = lax.optimization_barrier((last, state))
    came = lax.ppermute(last, "row", swap)
    late, _ = call(
        functools.partial(across_kernel, True),
        halves,
        [SMEM(), SMEM(), VMEM(), VMEM()],
        flops=10**10,
    )(place, smooth, cost, state)

    return call(
        second_vertical_kernel,
        jax.ShapeDtypeStruct((rows, width, DISPARITIES), f32),
        [SMEM(), SMEM()] + [VMEM()] * (half + 4),
        [pltpu.VMEM((rows, DISPARITIES, width), f32), joined],
        flops=3 * 10**9,
    )(place, smooth, *blocks, kept, came, early, late)


def solution(mesh):
    return jax.shard_map(
        per_device,
        mesh=mesh,
        in_specs=(P(None, "row", None, "col"), P(), P(), P("row", "col"), P("row", "col"), P()),
        out_specs=P("row", "col", None),
        check_vma=False,
    )
```

```python
import functools

import jax
import jax.numpy as jnp
from jax import lax
from jax.experimental import pallas as pl
from jax.experimental.pallas import tpu as pltpu
from jax.sharding import PartitionSpec as P

DISPARITIES = 128
OFF_MOST = 256
SUB = 8
REGS = DISPARITIES // SUB
MEBI = 1024 * 1024


def lane_to_disparity(lane):
    return (lane % SUB) * REGS + lane // SUB


def disparity_to_lane(disparity):
    return (disparity % REGS) * SUB + disparity // REGS


def advance(state, cost, p1, p2):
    lanes = state[0].shape[1]
    row = lax.broadcasted_iota(jnp.int32, (SUB, lanes), 0)
    below = jnp.where(row == 0, jnp.inf, pltpu.roll(state[-1], 1, 0))
    above = jnp.where(row == SUB - 1, jnp.inf, pltpu.roll(state[0], SUB - 1, 0))
    least = list(state)
    while len(least) > 1:
        least = [jnp.minimum(a, b) for a, b in zip(least[::2], least[1::2])]
    least = least[0]
    turned = [least] + [pltpu.roll(least, turn, 0) for turn in range(1, SUB)]
    while len(turned) > 1:
        turned = [jnp.minimum(a, b) for a, b in zip(turned[::2], turned[1::2])]
    least = turned[0]
    lower = [below] + state[:-1]
    upper = state[1:] + [above]
    fresh = []
    for s, l, u, c in zip(state, lower, upper, cost):
        t = jnp.minimum(s, jnp.minimum(l, u) + p1)
        fresh.append(c + jnp.minimum(t - least, p2))
    return fresh


def charges(charge_ref):
    return (
        charge_ref[0].astype(jnp.float32) * (1.0 / 64.0),
        charge_ref[1].astype(jnp.float32) * (1.0 / 64.0),
    )


def registers(array):
    return [array[SUB * v : SUB * (v + 1)] for v in range(REGS)]


def band_kernel(masks, place_ref, filter_ref, bias_ref, *refs):
    parts = len(masks)
    tile_refs, edge_refs, refs = refs[:parts], refs[parts : 2 * parts], refs[2 * parts :]
    cost_ref, own_ref, maps_a, maps_b, left_unit, right_unit, present, shifts = refs
    _, channels, width = tile_refs[0].shape
    layers = filter_ref.shape[0]
    rows = own_ref.shape[0]
    cols = parts * width
    high = rows + 2 * layers
    first_row = place_ref[0] * rows
    rows_total = place_ref[1] * rows
    own = place_ref[2]
    lead = (OFF_MOST + 2 * width - 1) // width * width

    for mask, edge_ref in zip(masks, edge_refs):
        member = own ^ mask
        extra = edge_ref[4 * layers].astype(jnp.float32)
        present[:, pl.ds(pl.multiple_of(member * width, width), width)] = extra[0:16]
        shifts[member] = extra[16:24]
    right_unit[:, 0:lead] = jnp.zeros((rows * channels, lead), jnp.bfloat16)
    right_unit[:, lead + cols :] = jnp.zeros((rows * channels, width), jnp.bfloat16)

    column = lax.broadcasted_iota(jnp.int32, (1, cols), 1)
    for image in range(2):

        for mask, tile_ref, edge_ref in zip(masks, tile_refs, edge_refs):
            there = pl.ds(pl.multiple_of((own ^ mask) * width, width), width)
            for row in range(high):
                if row < layers:
                    value = edge_ref[image * layers + row]
                elif row < layers + rows:
                    value = tile_ref[image * rows + row - layers]
                else:
                    value = edge_ref[(2 + image) * layers + row - layers - rows]
                maps_a[row * channels : (row + 1) * channels, there] = value

        for layer in range(layers):
            source, target = (maps_a, maps_b) if layer % 2 == 0 else (maps_b, maps_a)
            margin = layers - 1 - layer

            steps = rows + 2 * margin

            @pl.loop(0, steps, unroll=max(k for k in range(1, 6) if steps % k == 0))
            def _(row):
                start = pl.multiple_of(row * channels, channels)
                window = source[pl.ds(start, 3 * channels), :]
                taps = jnp.dot(filter_ref[layer], window, preferred_element_type=jnp.float32)
                before = pltpu.roll(taps[:channels], 1, 1)
                after = pltpu.roll(taps[2 * channels :], cols - 1, 1)
                z = taps[channels : 2 * channels] + jnp.where(column == 0, 0.0, before)
                z = z + jnp.where(column == cols - 1, 0.0, after) + bias_ref[layer]
                if layer < layers - 1:
                    there = first_row - margin + row
                    inside = jnp.logical_and(there >= 0, there < rows_total)
                    z = jnp.maximum(z, 0.0) * jnp.where(inside, 1.0, 0.0)
                    target[pl.ds(start, channels), :] = z.astype(jnp.bfloat16)
                else:
                    scale = lax.rsqrt(jnp.sum(z * z, axis=0, keepdims=True) + 1e-06)
                    unit = (z * scale).astype(jnp.bfloat16)
                    if image == 0:
                        seen = present[pl.ds(row, 1), :]
                        unit = jnp.where(seen > 0.5, unit.astype(jnp.float32), 0.0)
                        left_unit[pl.ds(start, channels), :] = unit.astype(jnp.bfloat16)
                    else:
                        right_unit[pl.ds(start, channels), lead : lead + cols] = unit

    lane = lax.broadcasted_iota(jnp.int32, (width, DISPARITIES), 1)
    place = lax.broadcasted_iota(jnp.int32, (width, DISPARITIES), 0)

    @pl.loop(0, parts)
    def _(p):
        shift = jnp.max(shifts[p]).astype(jnp.int32)
        base = p * width - shift + lead
        block = base // width
        ahead = place + (base - block * width)
        index = (ahead - lane_to_disparity(lane)) & (DISPARITIES - 1)
        start = pl.multiple_of((block - 1) * width, width)
        here = pl.multiple_of(p * width, width)

        def tile_costs(mine):
            for y in range(rows):
                left = left_unit[y * channels : (y + 1) * channels, pl.ds(here, width)]
                right = right_unit[y * channels : (y + 1) * channels, pl.ds(start, 3 * width)]
                product = lax.dot_general(
                    left, right, (((0,), (0,)), ((), ())), preferred_element_type=jnp.float32
                )
                chosen = jnp.where(lane <= ahead, product[:, width : 2 * width], product[:, :width])
                chosen = jnp.where(lane <= ahead - width, product[:, 2 * width :], chosen)
                chosen = jnp.take_along_axis(chosen, index, axis=1, mode="promise_in_bounds")
                chosen = 1.0 - chosen
                cost_ref[pl.ds(here, width), y, :] = chosen
                if mine:
                    own_ref[y] = chosen.T.astype(jnp.bfloat16)

        pl.when(p == own)(functools.partial(tile_costs, True))
        pl.when(p != own)(functools.partial(tile_costs, False))


def across_kernel(second, place_ref, charge_ref, cost_ref, *refs):
    kept_ref, last_ref = refs[-2:]
    cols = cost_ref.shape[0]
    width, rows, _ = kept_ref.shape
    parts = cols // width
    own = place_ref[2]
    p1, p2 = charges(charge_ref)

    def segment(p, state):
        first_col = p * width
        last_col = cols - 1 - p * width

        def run(keep_right, keep_left, state):
            def body(i, state):
                pair = [cost_ref[first_col + i], cost_ref[last_col - i]]
                cost = jnp.concatenate(pair, axis=0).T
                fresh = advance(list(state), registers(cost), p1, p2)
                if keep_right or keep_left:
                    back = jnp.concatenate(fresh, axis=0).T
                if keep_right:
                    kept_ref[i] = back[0:rows]
                if keep_left:
                    kept_ref[width - 1 - i] = back[rows : 2 * rows]
                return tuple(fresh)

            return lax.fori_loop(0, width, body, state, unroll=16)

        choice = jnp.where(p == own, 1, 0) + jnp.where(parts - 1 - p == own, 2, 0)
        return lax.switch(
            choice,
            [functools.partial(run, k == 1, k == 2) for k in range(3)],
            state,
        )

    if second:
        state = tuple(registers(refs[0][...]))
        span = (parts // 2, parts)
    else:
        state = tuple(jnp.zeros((SUB, 2 * rows), jnp.float32) for _ in range(REGS))
        span = (0, parts // 2)
    last_ref[...] = jnp.concatenate(lax.fori_loop(*span, segment, state), axis=0)


def down_or_up(forward, first_own, cost_ref, state, p1, p2, keep):
    group, rows = cost_ref.shape[:2]

    def block(b, state):
        member = jnp.where(forward, b, group - 1 - b)

        def run(kept, state):
            for i in range(rows):
                inner = jnp.where(forward, i, rows - 1 - i)
                cost = cost_ref[member, inner].astype(jnp.float32)
                state = advance(list(state), registers(cost), p1, p2)
                if kept:
                    keep(inner, jnp.concatenate(state, axis=0))
            return tuple(state)

        return lax.cond(
            member == first_own,
            functools.partial(run, True),
            functools.partial(run, False),
            state,
        )

    return lax.fori_loop(0, group, block, state)


def first_vertical_kernel(place_ref, charge_ref, *refs):
    *block_refs, kept_ref, last_ref, cost_ref = refs
    p1, p2 = charges(charge_ref)
    group, _, _, width = cost_ref.shape
    for k, block_ref in enumerate(block_refs):
        cost_ref[lax.rem(place_ref[4] + group - k, group)] = block_ref[...]
    state = tuple(jnp.zeros((SUB, width), jnp.float32) for _ in range(REGS))

    def keep(row, value):
        kept_ref[row] = value

    final = down_or_up(place_ref[3] == 0, place_ref[4], cost_ref, state, p1, p2, keep)
    last_ref[...] = jnp.concatenate(final, axis=0).astype(jnp.bfloat16)


def second_vertical_kernel(place_ref, charge_ref, *refs):
    *block_refs, kept_ref, came_ref, early_ref, late_ref, out_ref, total, cost_ref = refs
    p1, p2 = charges(charge_ref)
    group = cost_ref.shape[0]
    for k, block_ref in enumerate(block_refs):
        cost_ref[lax.rem(place_ref[4] + group - k, group)] = block_ref[...]
    rows, _, width = kept_ref.shape
    state = tuple(registers(came_ref[...].astype(jnp.float32)))

    def keep(row, value):
        total[row] = value + kept_ref[row]

    down_or_up(place_ref[3] != 0, place_ref[4], cost_ref, state, p1, p2, keep)
    lane = lax.broadcasted_iota(jnp.int32, (width, DISPARITIES), 1)
    index = disparity_to_lane(lane)
    for row in range(rows):
        value = total[row].T + (early_ref[:, row, :] + late_ref[:, row, :])
        out_ref[row] = jnp.take_along_axis(value, index, axis=1, mode="promise_in_bounds")


SMEM = functools.partial(pl.BlockSpec, memory_space=pltpu.SMEM)
VMEM = functools.partial(pl.BlockSpec, memory_space=pltpu.VMEM)


def call(kernel, outs, specs, scratch=(), flops=0, vmem=20):
    return pl.pallas_call(
        kernel,
        out_shape=outs,
        in_specs=specs,
        out_specs=jax.tree.map(lambda _: VMEM(), outs),
        scratch_shapes=list(scratch),
        compiler_params=pltpu.CompilerParams(vmem_limit_bytes=vmem * MEBI),
        cost_estimate=pl.CostEstimate(flops=flops, bytes_accessed=1 << 22, transcendentals=0),
    )


def spread(block, parts):
    masks, blocks = [0], [block]
    bit = parts // 2
    while bit:
        route = [(i, i ^ bit) for i in range(parts)]
        blocks += [lax.ppermute(held, "col", route) for held in blocks]
        masks += [mask ^ bit for mask in masks]
        bit //= 2
    return masks, blocks


def per_device(activations, filters, biases, present, shifts, smooth):
    _, rows, channels, width = activations.shape
    layers = filters.shape[0]
    high = rows + 2 * layers
    row_rank, row_count = lax.axis_index("row"), lax.axis_size("row")
    col_rank, parts = lax.axis_index("col"), lax.axis_size("col")
    half = row_count // 2
    cols = parts * width
    place = jnp.stack(
        [row_rank, jnp.int32(row_count), col_rank, row_rank // half, row_rank % half]
    ).astype(jnp.int32)

    downward = [(i, i + 1) for i in range(row_count - 1)]
    upward = [(i + 1, i) for i in range(row_count - 1)]
    before = lax.ppermute(activations[:, rows - layers :], "row", downward)
    after = lax.ppermute(activations[:, :layers], "row", upward)
    extra = jnp.concatenate(
        [
            present.astype(jnp.bfloat16),
            jnp.zeros((16 - rows, width), jnp.bfloat16),
            jnp.broadcast_to(shifts.astype(jnp.bfloat16), (channels - 16, width)),
        ],
        axis=0,
    )
    edges = jnp.concatenate(
        [before.reshape(-1, channels, width), after.reshape(-1, channels, width), extra[None]],
        axis=0,
    )
    masks, tiles = spread(activations.reshape(2 * rows, channels, width), parts)
    _, edges = spread(edges, parts)
    taps = jnp.transpose(filters, (0, 2, 3, 1, 4)).reshape(layers, 3 * channels, 3 * channels)

    f32, bf16 = jnp.float32, jnp.bfloat16
    lead = (OFF_MOST + 2 * width - 1) // width * width
    cost, own = call(
        functools.partial(band_kernel, masks),
        (
            jax.ShapeDtypeStruct((cols, rows, DISPARITIES), f32),
            jax.ShapeDtypeStruct((rows, DISPARITIES, width), bf16),
        ),
        [SMEM()] + [VMEM()] * (2 + 2 * parts),
        [
            pltpu.VMEM((high * channels, cols), bf16),
            pltpu.VMEM(((high - 2) * channels, cols), bf16),
            pltpu.VMEM((rows * channels, cols), bf16),
            pltpu.VMEM((rows * channels, lead + cols + width), bf16),
            pltpu.VMEM((16, cols), f32),
            pltpu.VMEM((parts, SUB, width), f32),
        ],
        flops=10**10,
        vmem=40,
    )(place, taps, biases[:, :, None], *tiles, *edges)

    blocks = [own]
    for k in range(1, half):
        turn = [(i, i // half * half + (i + k) % half) for i in range(row_count)]
        blocks.append(lax.ppermute(own, "row", turn))

    halves = (
        jax.ShapeDtypeStruct((width, rows, DISPARITIES), f32),
        jax.ShapeDtypeStruct((DISPARITIES, 2 * rows), f32),
    )
    early, state = call(
        functools.partial(across_kernel, False),
        halves,
        [SMEM(), SMEM(), VMEM()],
        flops=10**10,
    )(place, smooth, cost)
    *blocks, state = lax.optimization_barrier((*blocks, state))

    joined = pltpu.VMEM((half, rows, DISPARITIES, width), bf16)
    kept, last = call(
        first_vertical_kernel,
        (
            jax.ShapeDtypeStruct((rows, DISPARITIES, width), f32),
            jax.ShapeDtypeStruct((DISPARITIES, width), bf16),
        ),
        [SMEM(), SMEM()] + [VMEM()] * half,
        [joined],
        flops=2 * 10**9,
    )(place, smooth, *blocks)

    swap = [(i, (i + half) % row_count) for i in range(row_count)]
    last, state = lax.optimization_barrier((last, state))
    came = lax.ppermute(last, "row", swap)
    late, _ = call(
        functools.partial(across_kernel, True),
        halves,
        [SMEM(), SMEM(), VMEM(), VMEM()],
        flops=10**10,
    )(place, smooth, cost, state)

    return call(
        second_vertical_kernel,
        jax.ShapeDtypeStruct((rows, width, DISPARITIES), f32),
        [SMEM(), SMEM()] + [VMEM()] * (half + 4),
        [pltpu.VMEM((rows, DISPARITIES, width), f32), joined],
        flops=3 * 10**9,
    )(place, smooth, *blocks, kept, came, early, late)


def solution(mesh):
    return jax.shard_map(
        per_device,
        mesh=mesh,
        in_specs=(P(None, "row", None, "col"), P(), P(), P("row", "col"), P("row", "col"), P()),
        out_specs=P("row", "col", None),
        check_vma=False,
    )
```

```python
import functools

import jax
import jax.numpy as jnp
from jax import lax
from jax.experimental import pallas as pl
from jax.experimental.pallas import tpu as pltpu
from jax.sharding import PartitionSpec as P

DISPARITIES = 128
OFF_MOST = 256
SUB = 8
REGS = DISPARITIES // SUB
MEBI = 1024 * 1024


def lane_to_disparity(lane):
    return (lane % SUB) * REGS + lane // SUB


def disparity_to_lane(disparity):
    return (disparity % REGS) * SUB + disparity // REGS


def least_of(values):
    while len(values) > 1:
        values = [jnp.minimum(a, b) for a, b in zip(values[::2], values[1::2])]
    turned = values + [pltpu.roll(values[0], turn, 0) for turn in range(1, SUB)]
    while len(turned) > 1:
        turned = [jnp.minimum(a, b) for a, b in zip(turned[::2], turned[1::2])]
    return turned[0]


def stepped(state, p1):
    row = lax.broadcasted_iota(jnp.int32, state[0].shape, 0)
    below = jnp.where(row == 0, jnp.inf, pltpu.roll(state[-1], 1, 0))
    above = jnp.where(row == SUB - 1, jnp.inf, pltpu.roll(state[0], SUB - 1, 0))
    lower = [below] + state[:-1]
    upper = state[1:] + [above]
    return [
        jnp.minimum(s, jnp.minimum(l, u) + p1) for s, l, u in zip(state, lower, upper)
    ]


def advance(state, cost, p1, p2):
    least = least_of(state)
    return [c + jnp.minimum(t - least, p2) for t, c in zip(stepped(state, p1), cost)]


def advance_ahead(sums, jump, cost, p1, p2):
    walked = [c + t for t, c in zip(stepped(sums, p1), cost)]
    fresh = [jnp.minimum(w, c + jump) for w, c in zip(walked, cost)]
    following = jnp.minimum(least_of(walked) + p2, (least_of(cost) + p2) + jump)
    return fresh, following


def charges(charge_ref):
    return (
        charge_ref[0].astype(jnp.float32) * (1.0 / 64.0),
        charge_ref[1].astype(jnp.float32) * (1.0 / 64.0),
    )


def registers(array):
    return [array[SUB * v : SUB * (v + 1)] for v in range(REGS)]


def band_kernel(masks, place_ref, filter_ref, bias_ref, *refs):
    parts = len(masks)
    tile_refs, edge_refs, refs = refs[:parts], refs[parts : 2 * parts], refs[2 * parts :]
    cost_ref, own_ref, maps_a, maps_b, left_unit, right_unit, present, shifts, taps_ref = refs
    _, channels, width = tile_refs[0].shape
    layers = filter_ref.shape[0]
    rows = own_ref.shape[0]
    cols = parts * width
    high = rows + 2 * layers
    first_row = place_ref[0] * rows
    rows_total = place_ref[1] * rows
    own = place_ref[2]
    lead = (OFF_MOST + 2 * width - 1) // width * width

    for layer in range(layers):
        for a in range(3):
            for b in range(3):
                taps_ref[
                    layer, b * channels : (b + 1) * channels, a * channels : (a + 1) * channels
                ] = filter_ref[layer, a, b]

    for mask, edge_ref in zip(masks, edge_refs):
        member = own ^ mask
        extra = edge_ref[4 * layers].astype(jnp.float32)
        present[:, pl.ds(pl.multiple_of(member * width, width), width)] = extra[0:16]
        shifts[member] = extra[16:24]
    right_unit[:, 0:lead] = jnp.zeros((rows * channels, lead), jnp.bfloat16)
    right_unit[:, lead + cols :] = jnp.zeros((rows * channels, width), jnp.bfloat16)

    column = lax.broadcasted_iota(jnp.int32, (1, cols), 1)
    for image in range(2):

        for mask, tile_ref, edge_ref in zip(masks, tile_refs, edge_refs):
            there = pl.ds(pl.multiple_of((own ^ mask) * width, width), width)
            for row in range(high):
                if row < layers:
                    value = edge_ref[image * layers + row]
                elif row < layers + rows:
                    value = tile_ref[image * rows + row - layers]
                else:
                    value = edge_ref[(2 + image) * layers + row - layers - rows]
                maps_a[row * channels : (row + 1) * channels, there] = value

        for layer in range(layers):
            source, target = (maps_a, maps_b) if layer % 2 == 0 else (maps_b, maps_a)
            margin = layers - 1 - layer

            steps = rows + 2 * margin

            @pl.loop(0, steps, unroll=max(k for k in range(1, 6) if steps % k == 0))
            def _(row):
                start = pl.multiple_of(row * channels, channels)
                window = source[pl.ds(start, 3 * channels), :]
                taps = jnp.dot(taps_ref[layer], window, preferred_element_type=jnp.float32)
                before = pltpu.roll(taps[:channels], 1, 1)
                after = pltpu.roll(taps[2 * channels :], cols - 1, 1)
                z = taps[channels : 2 * channels] + jnp.where(column == 0, 0.0, before)
                z = z + jnp.where(column == cols - 1, 0.0, after) + bias_ref[layer]
                if layer < layers - 1:
                    there = first_row - margin + row
                    inside = jnp.logical_and(there >= 0, there < rows_total)
                    z = jnp.maximum(z, 0.0) * jnp.where(inside, 1.0, 0.0)
                    target[pl.ds(start, channels), :] = z.astype(jnp.bfloat16)
                else:
                    scale = lax.rsqrt(jnp.sum(z * z, axis=0, keepdims=True) + 1e-06)
                    unit = (z * scale).astype(jnp.bfloat16)
                    if image == 0:
                        seen = present[pl.ds(row, 1), :]
                        unit = jnp.where(seen > 0.5, unit.astype(jnp.float32), 0.0)
                        left_unit[pl.ds(start, channels), :] = unit.astype(jnp.bfloat16)
                    else:
                        right_unit[pl.ds(start, channels), lead : lead + cols] = unit

    lane = lax.broadcasted_iota(jnp.int32, (width, DISPARITIES), 1)
    place = lax.broadcasted_iota(jnp.int32, (width, DISPARITIES), 0)

    @pl.loop(0, parts)
    def _(p):
        shift = jnp.max(shifts[p]).astype(jnp.int32)
        base = p * width - shift + lead
        block = base // width
        ahead = place + (base - block * width)
        index = (ahead - lane_to_disparity(lane)) & (DISPARITIES - 1)
        start = pl.multiple_of((block - 1) * width, width)
        here = pl.multiple_of(p * width, width)

        def tile_costs(mine):
            for y in range(rows):
                left = left_unit[y * channels : (y + 1) * channels, pl.ds(here, width)]
                right = right_unit[y * channels : (y + 1) * channels, pl.ds(start, 3 * width)]
                product = lax.dot_general(
                    left, right, (((0,), (0,)), ((), ())), preferred_element_type=jnp.float32
                )
                chosen = jnp.where(lane <= ahead, product[:, width : 2 * width], product[:, :width])
                chosen = jnp.where(lane <= ahead - width, product[:, 2 * width :], chosen)
                chosen = jnp.take_along_axis(chosen, index, axis=1, mode="promise_in_bounds")
                chosen = 1.0 - chosen
                cost_ref[pl.ds(here, width), y, :] = chosen
                if mine:
                    own_ref[y] = chosen.T.astype(jnp.bfloat16)

        pl.when(p == own)(functools.partial(tile_costs, True))
        pl.when(p != own)(functools.partial(tile_costs, False))


def across_kernel(second, place_ref, charge_ref, cost_ref, *refs):
    kept_ref, last_ref = refs[-2:]
    cols = cost_ref.shape[0]
    width, rows, _ = kept_ref.shape
    parts = cols // width
    own = place_ref[2]
    p1, p2 = charges(charge_ref)

    def cost_at(step):
        step = jnp.minimum(step, cols - 1)
        pair = [cost_ref[step], cost_ref[cols - 1 - step]]
        return registers(jnp.concatenate(pair, axis=0).T)

    def segment(p, state):
        first_step = p * width

        def run(keep_right, keep_left, state):
            def body(i, carry):
                sums, jump, cost = carry
                ahead = cost_at(first_step + i + 1)
                fresh, following = advance_ahead(list(sums), jump, list(cost), p1, p2)
                if keep_right or keep_left:
                    base = jump - p2
                    back = jnp.concatenate([f - base for f in fresh], axis=0).T
                if keep_right:
                    kept_ref[i] = back[0:rows]
                if keep_left:
                    kept_ref[width - 1 - i] = back[rows : 2 * rows]
                return tuple(fresh), following, tuple(ahead)

            level = jnp.zeros((SUB, 2 * rows), jnp.float32) + p2
            carry = (state, level, tuple(cost_at(first_step)))
            sums, jump, _ = lax.fori_loop(0, width, body, carry, unroll=16)
            return tuple(s - (jump - p2) for s in sums)

        choice = jnp.where(p == own, 1, 0) + jnp.where(parts - 1 - p == own, 2, 0)
        return lax.switch(
            choice,
            [functools.partial(run, k == 1, k == 2) for k in range(3)],
            state,
        )

    if second:
        state = tuple(registers(refs[0][...]))
        span = (parts // 2, parts)
    else:
        state = tuple(jnp.zeros((SUB, 2 * rows), jnp.float32) for _ in range(REGS))
        span = (0, parts // 2)
    last_ref[...] = jnp.concatenate(lax.fori_loop(*span, segment, state), axis=0)


def down_or_up(forward, first_own, cost_ref, state, p1, p2, keep):
    group, rows = cost_ref.shape[:2]

    def block(b, state):
        member = jnp.where(forward, b, group - 1 - b)

        def run(kept, state):
            for i in range(rows):
                inner = jnp.where(forward, i, rows - 1 - i)
                cost = cost_ref[member, inner].astype(jnp.float32)
                state = advance(list(state), registers(cost), p1, p2)
                if kept:
                    keep(inner, jnp.concatenate(state, axis=0))
            return tuple(state)

        return lax.cond(
            member == first_own,
            functools.partial(run, True),
            functools.partial(run, False),
            state,
        )

    return lax.fori_loop(0, group, block, state)


def first_vertical_kernel(place_ref, charge_ref, *refs):
    *block_refs, kept_ref, last_ref, cost_ref = refs
    p1, p2 = charges(charge_ref)
    group, _, _, width = cost_ref.shape
    for k, block_ref in enumerate(block_refs):
        cost_ref[lax.rem(place_ref[4] + group - k, group)] = block_ref[...]
    state = tuple(jnp.zeros((SUB, width), jnp.float32) for _ in range(REGS))

    def keep(row, value):
        kept_ref[row] = value

    final = down_or_up(place_ref[3] == 0, place_ref[4], cost_ref, state, p1, p2, keep)
    last_ref[...] = jnp.concatenate(final, axis=0).astype(jnp.bfloat16)


def second_vertical_kernel(place_ref, charge_ref, *refs):
    *block_refs, kept_ref, came_ref, early_ref, late_ref, out_ref, total, cost_ref = refs
    p1, p2 = charges(charge_ref)
    group = cost_ref.shape[0]
    for k, block_ref in enumerate(block_refs):
        cost_ref[lax.rem(place_ref[4] + group - k, group)] = block_ref[...]
    rows, _, width = kept_ref.shape
    state = tuple(registers(came_ref[...].astype(jnp.float32)))

    def keep(row, value):
        total[row] = value + kept_ref[row]

    down_or_up(place_ref[3] != 0, place_ref[4], cost_ref, state, p1, p2, keep)
    lane = lax.broadcasted_iota(jnp.int32, (width, DISPARITIES), 1)
    index = disparity_to_lane(lane)
    for row in range(rows):
        value = total[row].T + (early_ref[:, row, :] + late_ref[:, row, :])
        out_ref[row] = jnp.take_along_axis(value, index, axis=1, mode="promise_in_bounds")


SMEM = functools.partial(pl.BlockSpec, memory_space=pltpu.SMEM)
VMEM = functools.partial(pl.BlockSpec, memory_space=pltpu.VMEM)


def call(kernel, outs, specs, scratch=(), flops=0, vmem=20):
    return pl.pallas_call(
        kernel,
        out_shape=outs,
        in_specs=specs,
        out_specs=jax.tree.map(lambda _: VMEM(), outs),
        scratch_shapes=list(scratch),
        compiler_params=pltpu.CompilerParams(vmem_limit_bytes=vmem * MEBI),
        cost_estimate=pl.CostEstimate(flops=flops, bytes_accessed=1 << 22, transcendentals=0),
    )


def spread(block, parts):
    masks, blocks = [0], [block]
    bit = parts // 2
    while bit:
        route = [(i, i ^ bit) for i in range(parts)]
        blocks += [lax.ppermute(held, "col", route) for held in blocks]
        masks += [mask ^ bit for mask in masks]
        bit //= 2
    return masks, blocks


def per_device(activations, filters, biases, present, shifts, smooth):
    _, rows, channels, width = activations.shape
    layers = filters.shape[0]
    high = rows + 2 * layers
    row_rank, row_count = lax.axis_index("row"), lax.axis_size("row")
    col_rank, parts = lax.axis_index("col"), lax.axis_size("col")
    half = row_count // 2
    cols = parts * width
    place = jnp.stack(
        [row_rank, jnp.int32(row_count), col_rank, row_rank // half, row_rank % half]
    ).astype(jnp.int32)

    downward = [(i, i + 1) for i in range(row_count - 1)]
    upward = [(i + 1, i) for i in range(row_count - 1)]
    before = lax.ppermute(activations[:, rows - layers :], "row", downward)
    after = lax.ppermute(activations[:, :layers], "row", upward)
    extra = jnp.concatenate(
        [
            present.astype(jnp.bfloat16),
            jnp.zeros((16 - rows, width), jnp.bfloat16),
            jnp.broadcast_to(shifts.astype(jnp.bfloat16), (channels - 16, width)),
        ],
        axis=0,
    )
    edges = jnp.concatenate(
        [before.reshape(-1, channels, width), after.reshape(-1, channels, width), extra[None]],
        axis=0,
    )
    masks, tiles = spread(activations.reshape(2 * rows, channels, width), parts)
    _, edges = spread(edges, parts)

    f32, bf16 = jnp.float32, jnp.bfloat16
    lead = (OFF_MOST + 2 * width - 1) // width * width
    cost, own = call(
        functools.partial(band_kernel, masks),
        (
            jax.ShapeDtypeStruct((cols, rows, DISPARITIES), f32),
            jax.ShapeDtypeStruct((rows, DISPARITIES, width), bf16),
        ),
        [SMEM()] + [VMEM()] * (2 + 2 * parts),
        [
            pltpu.VMEM((high * channels, cols), bf16),
            pltpu.VMEM(((high - 2) * channels, cols), bf16),
            pltpu.VMEM((rows * channels, cols), bf16),
            pltpu.VMEM((rows * channels, lead + cols + width), bf16),
            pltpu.VMEM((16, cols), f32),
            pltpu.VMEM((parts, SUB, width), f32),
            pltpu.VMEM((layers, 3 * channels, 3 * channels), bf16),
        ],
        flops=10**10,
        vmem=40,
    )(place, filters, biases[:, :, None], *tiles, *edges)

    blocks = [own]
    for k in range(1, half):
        turn = [(i, i // half * half + (i + k) % half) for i in range(row_count)]
        blocks.append(lax.ppermute(own, "row", turn))

    halves = (
        jax.ShapeDtypeStruct((width, rows, DISPARITIES), f32),
        jax.ShapeDtypeStruct((DISPARITIES, 2 * rows), f32),
    )
    early, state = call(
        functools.partial(across_kernel, False),
        halves,
        [SMEM(), SMEM(), VMEM()],
        flops=10**10,
    )(place, smooth, cost)
    *blocks, state = lax.optimization_barrier((*blocks, state))

    joined = pltpu.VMEM((half, rows, DISPARITIES, width), bf16)
    kept, last = call(
        first_vertical_kernel,
        (
            jax.ShapeDtypeStruct((rows, DISPARITIES, width), f32),
            jax.ShapeDtypeStruct((DISPARITIES, width), bf16),
        ),
        [SMEM(), SMEM()] + [VMEM()] * half,
        [joined],
        flops=2 * 10**9,
    )(place, smooth, *blocks)

    swap = [(i, (i + half) % row_count) for i in range(row_count)]
    last, state = lax.optimization_barrier((last, state))
    came = lax.ppermute(last, "row", swap)
    late, _ = call(
        functools.partial(across_kernel, True),
        halves,
        [SMEM(), SMEM(), VMEM(), VMEM()],
        flops=10**10,
    )(place, smooth, cost, state)

    return call(
        second_vertical_kernel,
        jax.ShapeDtypeStruct((rows, width, DISPARITIES), f32),
        [SMEM(), SMEM()] + [VMEM()] * (half + 4),
        [pltpu.VMEM((rows, DISPARITIES, width), f32), joined],
        flops=3 * 10**9,
    )(place, smooth, *blocks, kept, came, early, late)


def solution(mesh):
    return jax.shard_map(
        per_device,
        mesh=mesh,
        in_specs=(P(None, "row", None, "col"), P(), P(), P("row", "col"), P("row", "col"), P()),
        out_specs=P("row", "col", None),
        check_vma=False,
    )
```

```python
import functools

import jax
import jax.numpy as jnp
from jax import lax
from jax.experimental import pallas as pl
from jax.experimental.pallas import tpu as pltpu
from jax.sharding import PartitionSpec as P

DISPARITIES = 128
OFF_MOST = 256
SUB = 8
REGS = DISPARITIES // SUB
MEBI = 1024 * 1024


def lane_to_disparity(lane):
    return (lane % SUB) * REGS + lane // SUB


def disparity_to_lane(disparity):
    return (disparity % REGS) * SUB + disparity // REGS


def least_of(values):
    while len(values) > 1:
        values = [jnp.minimum(a, b) for a, b in zip(values[::2], values[1::2])]
    turned = values + [pltpu.roll(values[0], turn, 0) for turn in range(1, SUB)]
    while len(turned) > 1:
        turned = [jnp.minimum(a, b) for a, b in zip(turned[::2], turned[1::2])]
    return turned[0]


def stepped(state, p1):
    row = lax.broadcasted_iota(jnp.int32, state[0].shape, 0)
    below = jnp.where(row == 0, jnp.inf, pltpu.roll(state[-1], 1, 0))
    above = jnp.where(row == SUB - 1, jnp.inf, pltpu.roll(state[0], SUB - 1, 0))
    lower = [below] + state[:-1]
    upper = state[1:] + [above]
    return [
        jnp.minimum(s, jnp.minimum(l, u) + p1) for s, l, u in zip(state, lower, upper)
    ]


def advance(state, cost, p1, p2):
    least = least_of(state)
    return [c + jnp.minimum(t - least, p2) for t, c in zip(stepped(state, p1), cost)]


def ends(values, depth):
    row = lax.broadcasted_iota(jnp.int32, values[0].shape, 0)
    low = [jnp.where(row == 0, jnp.inf, pltpu.roll(v, 1, 0)) for v in values[-depth:]]
    high = [jnp.where(row == SUB - 1, jnp.inf, pltpu.roll(v, SUB - 1, 0)) for v in values[:depth]]
    return low, high


def walk(wide, cost, p1):
    return [
        c + jnp.minimum(s, jnp.minimum(l, u) + p1)
        for l, s, u, c in zip(wide[:-2], wide[1:-1], wide[2:], cost)
    ]


def leap(walked, cost, jump):
    return [jnp.minimum(w, c + jump) for w, c in zip(walked, cost)]


def next_jump(walked, cost, jump, p2):
    cheapest = cost
    while len(cheapest) > 1:
        cheapest = [jnp.minimum(a, b) for a, b in zip(cheapest[::2], cheapest[1::2])]
    cheapest = cheapest[0]
    for turn in (4, 2, 1):
        cheapest = jnp.minimum(cheapest, pltpu.roll(cheapest, turn, 0))
    return jnp.minimum(least_of(walked) + p2, (cheapest + p2) + jump)


def advance_pair(wide, jump, first, second, p1, p2):
    low, high = ends(first, 1)
    beyond = low + first + high
    walked = walk(wide, beyond, p1)
    middle = leap(walked, beyond, jump)
    jump_between = next_jump(walked[1:-1], first, jump, p2)
    walked = walk(middle, second, p1)
    low, high = ends(walked, 2)
    cost_low, cost_high = ends(second, 2)
    wide = leap(low + walked + high, cost_low + second + cost_high, jump_between)
    return wide, middle[1:-1], jump_between, next_jump(walked, second, jump_between, p2)


def charges(charge_ref):
    return (
        charge_ref[0].astype(jnp.float32) * (1.0 / 64.0),
        charge_ref[1].astype(jnp.float32) * (1.0 / 64.0),
    )


def registers(array):
    return [array[SUB * v : SUB * (v + 1)] for v in range(REGS)]


def band_kernel(masks, place_ref, filter_ref, bias_ref, *refs):
    parts = len(masks)
    tile_refs, edge_refs, refs = refs[:parts], refs[parts : 2 * parts], refs[2 * parts :]
    cost_ref, own_ref, maps_a, maps_b, left_unit, right_unit, present, shifts, taps_ref = refs
    _, channels, width = tile_refs[0].shape
    layers = filter_ref.shape[0]
    rows = own_ref.shape[0]
    cols = parts * width
    high = rows + 2 * layers
    first_row = place_ref[0] * rows
    rows_total = place_ref[1] * rows
    own = place_ref[2]
    lead = (OFF_MOST + 2 * width - 1) // width * width

    for layer in range(layers):
        for a in range(3):
            for b in range(3):
                taps_ref[
                    layer, b * channels : (b + 1) * channels, a * channels : (a + 1) * channels
                ] = filter_ref[layer, a, b]

    for mask, edge_ref in zip(masks, edge_refs):
        member = own ^ mask
        extra = edge_ref[4 * layers].astype(jnp.float32)
        present[:, pl.ds(pl.multiple_of(member * width, width), width)] = extra[0:16]
        shifts[member] = extra[16:24]
    right_unit[:, 0:lead] = jnp.zeros((rows * channels, lead), jnp.bfloat16)
    right_unit[:, lead + cols :] = jnp.zeros((rows * channels, width), jnp.bfloat16)

    column = lax.broadcasted_iota(jnp.int32, (1, cols), 1)
    for image in range(2):

        for mask, tile_ref, edge_ref in zip(masks, tile_refs, edge_refs):
            there = pl.ds(pl.multiple_of((own ^ mask) * width, width), width)
            for row in range(high):
                if row < layers:
                    value = edge_ref[image * layers + row]
                elif row < layers + rows:
                    value = tile_ref[image * rows + row - layers]
                else:
                    value = edge_ref[(2 + image) * layers + row - layers - rows]
                maps_a[row * channels : (row + 1) * channels, there] = value

        for layer in range(layers):
            source, target = (maps_a, maps_b) if layer % 2 == 0 else (maps_b, maps_a)
            margin = layers - 1 - layer

            steps = rows + 2 * margin

            @pl.loop(0, steps, unroll=max(k for k in range(1, 6) if steps % k == 0))
            def _(row):
                start = pl.multiple_of(row * channels, channels)
                window = source[pl.ds(start, 3 * channels), :]
                taps = jnp.dot(taps_ref[layer], window, preferred_element_type=jnp.float32)
                before = pltpu.roll(taps[:channels], 1, 1)
                after = pltpu.roll(taps[2 * channels :], cols - 1, 1)
                z = taps[channels : 2 * channels] + jnp.where(column == 0, 0.0, before)
                z = z + jnp.where(column == cols - 1, 0.0, after) + bias_ref[layer]
                if layer < layers - 1:
                    there = first_row - margin + row
                    inside = jnp.logical_and(there >= 0, there < rows_total)
                    z = jnp.maximum(z, 0.0) * jnp.where(inside, 1.0, 0.0)
                    target[pl.ds(start, channels), :] = z.astype(jnp.bfloat16)
                else:
                    scale = lax.rsqrt(jnp.sum(z * z, axis=0, keepdims=True) + 1e-06)
                    unit = (z * scale).astype(jnp.bfloat16)
                    if image == 0:
                        seen = present[pl.ds(row, 1), :]
                        unit = jnp.where(seen > 0.5, unit.astype(jnp.float32), 0.0)
                        left_unit[pl.ds(start, channels), :] = unit.astype(jnp.bfloat16)
                    else:
                        right_unit[pl.ds(start, channels), lead : lead + cols] = unit

    lane = lax.broadcasted_iota(jnp.int32, (width, DISPARITIES), 1)
    place = lax.broadcasted_iota(jnp.int32, (width, DISPARITIES), 0)

    @pl.loop(0, parts)
    def _(p):
        shift = jnp.max(shifts[p]).astype(jnp.int32)
        base = p * width - shift + lead
        block = base // width
        ahead = place + (base - block * width)
        index = (ahead - lane_to_disparity(lane)) & (DISPARITIES - 1)
        start = pl.multiple_of((block - 1) * width, width)
        here = pl.multiple_of(p * width, width)

        def tile_costs(mine):
            for y in range(rows):
                left = left_unit[y * channels : (y + 1) * channels, pl.ds(here, width)]
                right = right_unit[y * channels : (y + 1) * channels, pl.ds(start, 3 * width)]
                product = lax.dot_general(
                    left, right, (((0,), (0,)), ((), ())), preferred_element_type=jnp.float32
                )
                chosen = jnp.where(lane <= ahead, product[:, width : 2 * width], product[:, :width])
                chosen = jnp.where(lane <= ahead - width, product[:, 2 * width :], chosen)
                chosen = jnp.take_along_axis(chosen, index, axis=1, mode="promise_in_bounds")
                chosen = 1.0 - chosen
                cost_ref[pl.ds(here, width), y, :] = chosen
                if mine:
                    own_ref[y] = chosen.T.astype(jnp.bfloat16)

        pl.when(p == own)(functools.partial(tile_costs, True))
        pl.when(p != own)(functools.partial(tile_costs, False))


def across_kernel(second, place_ref, charge_ref, cost_ref, *refs):
    kept_ref, last_ref = refs[-2:]
    cols = cost_ref.shape[0]
    width, rows, _ = kept_ref.shape
    parts = cols // width
    own = place_ref[2]
    p1, p2 = charges(charge_ref)

    def cost_at(step):
        step = jnp.minimum(step, cols - 1)
        pair = [cost_ref[step], cost_ref[cols - 1 - step]]
        return registers(jnp.concatenate(pair, axis=0).T)

    def segment(p, state):
        first_step = p * width

        def run(keep_right, keep_left, state):
            def keep(i, values, jump):
                back = jnp.concatenate([v - (jump - p2) for v in values], axis=0).T
                if keep_right:
                    kept_ref[i] = back[0:rows]
                else:
                    kept_ref[width - 1 - i] = back[rows : 2 * rows]

            def body(i, carry):
                wide, jump, first = carry
                second = cost_at(first_step + 2 * i + 1)
                ahead = cost_at(first_step + 2 * i + 2)
                wide, middle, between, following = advance_pair(
                    list(wide), jump, list(first), second, p1, p2
                )
                if keep_right or keep_left:
                    keep(2 * i, middle, jump)
                    keep(2 * i + 1, wide[2:-2], between)
                return tuple(wide), following, tuple(ahead)

            low, high = ends(list(state), 2)
            level = jnp.zeros((SUB, 2 * rows), jnp.float32) + p2
            carry = (tuple(low + list(state) + high), level, tuple(cost_at(first_step)))
            wide, jump, _ = lax.fori_loop(0, width // 2, body, carry, unroll=8)
            return tuple(s - (jump - p2) for s in wide[2:-2])

        choice = jnp.where(p == own, 1, 0) + jnp.where(parts - 1 - p == own, 2, 0)
        return lax.switch(
            choice,
            [functools.partial(run, k == 1, k == 2) for k in range(3)],
            state,
        )

    if second:
        state = tuple(registers(refs[0][...]))
        span = (parts // 2, parts)
    else:
        state = tuple(jnp.zeros((SUB, 2 * rows), jnp.float32) for _ in range(REGS))
        span = (0, parts // 2)
    last_ref[...] = jnp.concatenate(lax.fori_loop(*span, segment, state), axis=0)


def down_or_up(forward, first_own, cost_ref, state, p1, p2, keep):
    group, rows = cost_ref.shape[:2]

    def block(b, state):
        member = jnp.where(forward, b, group - 1 - b)

        def run(kept, state):
            for i in range(rows):
                inner = jnp.where(forward, i, rows - 1 - i)
                cost = cost_ref[member, inner].astype(jnp.float32)
                state = advance(list(state), registers(cost), p1, p2)
                if kept:
                    keep(inner, jnp.concatenate(state, axis=0))
            return tuple(state)

        return lax.cond(
            member == first_own,
            functools.partial(run, True),
            functools.partial(run, False),
            state,
        )

    return lax.fori_loop(0, group, block, state)


def first_vertical_kernel(place_ref, charge_ref, *refs):
    *block_refs, kept_ref, last_ref, cost_ref = refs
    p1, p2 = charges(charge_ref)
    group, _, _, width = cost_ref.shape
    for k, block_ref in enumerate(block_refs):
        cost_ref[lax.rem(place_ref[4] + group - k, group)] = block_ref[...]
    state = tuple(jnp.zeros((SUB, width), jnp.float32) for _ in range(REGS))

    def keep(row, value):
        kept_ref[row] = value

    final = down_or_up(place_ref[3] == 0, place_ref[4], cost_ref, state, p1, p2, keep)
    last_ref[...] = jnp.concatenate(final, axis=0).astype(jnp.bfloat16)


def second_vertical_kernel(place_ref, charge_ref, *refs):
    *block_refs, kept_ref, came_ref, early_ref, late_ref, out_ref, total, cost_ref = refs
    p1, p2 = charges(charge_ref)
    group = cost_ref.shape[0]
    for k, block_ref in enumerate(block_refs):
        cost_ref[lax.rem(place_ref[4] + group - k, group)] = block_ref[...]
    rows, _, width = kept_ref.shape
    state = tuple(registers(came_ref[...].astype(jnp.float32)))

    def keep(row, value):
        total[row] = value + kept_ref[row]

    down_or_up(place_ref[3] != 0, place_ref[4], cost_ref, state, p1, p2, keep)
    lane = lax.broadcasted_iota(jnp.int32, (width, DISPARITIES), 1)
    index = disparity_to_lane(lane)
    for row in range(rows):
        value = total[row].T + (early_ref[:, row, :] + late_ref[:, row, :])
        out_ref[row] = jnp.take_along_axis(value, index, axis=1, mode="promise_in_bounds")


SMEM = functools.partial(pl.BlockSpec, memory_space=pltpu.SMEM)
VMEM = functools.partial(pl.BlockSpec, memory_space=pltpu.VMEM)


def call(kernel, outs, specs, scratch=(), flops=0, vmem=20):
    return pl.pallas_call(
        kernel,
        out_shape=outs,
        in_specs=specs,
        out_specs=jax.tree.map(lambda _: VMEM(), outs),
        scratch_shapes=list(scratch),
        compiler_params=pltpu.CompilerParams(vmem_limit_bytes=vmem * MEBI),
        cost_estimate=pl.CostEstimate(flops=flops, bytes_accessed=1 << 22, transcendentals=0),
    )


def spread(block, parts):
    masks, blocks = [0], [block]
    bit = parts // 2
    while bit:
        route = [(i, i ^ bit) for i in range(parts)]
        blocks += [lax.ppermute(held, "col", route) for held in blocks]
        masks += [mask ^ bit for mask in masks]
        bit //= 2
    return masks, blocks


def per_device(activations, filters, biases, present, shifts, smooth):
    _, rows, channels, width = activations.shape
    layers = filters.shape[0]
    high = rows + 2 * layers
    row_rank, row_count = lax.axis_index("row"), lax.axis_size("row")
    col_rank, parts = lax.axis_index("col"), lax.axis_size("col")
    half = row_count // 2
    cols = parts * width
    place = jnp.stack(
        [row_rank, jnp.int32(row_count), col_rank, row_rank // half, row_rank % half]
    ).astype(jnp.int32)

    downward = [(i, i + 1) for i in range(row_count - 1)]
    upward = [(i + 1, i) for i in range(row_count - 1)]
    before = lax.ppermute(activations[:, rows - layers :], "row", downward)
    after = lax.ppermute(activations[:, :layers], "row", upward)
    extra = jnp.concatenate(
        [
            present.astype(jnp.bfloat16),
            jnp.zeros((16 - rows, width), jnp.bfloat16),
            jnp.broadcast_to(shifts.astype(jnp.bfloat16), (channels - 16, width)),
        ],
        axis=0,
    )
    edges = jnp.concatenate(
        [before.reshape(-1, channels, width), after.reshape(-1, channels, width), extra[None]],
        axis=0,
    )
    masks, tiles = spread(activations.reshape(2 * rows, channels, width), parts)
    _, edges = spread(edges, parts)

    f32, bf16 = jnp.float32, jnp.bfloat16
    lead = (OFF_MOST + 2 * width - 1) // width * width
    cost, own = call(
        functools.partial(band_kernel, masks),
        (
            jax.ShapeDtypeStruct((cols, rows, DISPARITIES), f32),
            jax.ShapeDtypeStruct((rows, DISPARITIES, width), bf16),
        ),
        [SMEM()] + [VMEM()] * (2 + 2 * parts),
        [
            pltpu.VMEM((high * channels, cols), bf16),
            pltpu.VMEM(((high - 2) * channels, cols), bf16),
            pltpu.VMEM((rows * channels, cols), bf16),
            pltpu.VMEM((rows * channels, lead + cols + width), bf16),
            pltpu.VMEM((16, cols), f32),
            pltpu.VMEM((parts, SUB, width), f32),
            pltpu.VMEM((layers, 3 * channels, 3 * channels), bf16),
        ],
        flops=10**10,
        vmem=40,
    )(place, filters, biases[:, :, None], *tiles, *edges)

    blocks = [own]
    for k in range(1, half):
        turn = [(i, i // half * half + (i + k) % half) for i in range(row_count)]
        blocks.append(lax.ppermute(own, "row", turn))

    halves = (
        jax.ShapeDtypeStruct((width, rows, DISPARITIES), f32),
        jax.ShapeDtypeStruct((DISPARITIES, 2 * rows), f32),
    )
    early, state = call(
        functools.partial(across_kernel, False),
        halves,
        [SMEM(), SMEM(), VMEM()],
        flops=10**10,
    )(place, smooth, cost)
    *blocks, state = lax.optimization_barrier((*blocks, state))

    joined = pltpu.VMEM((half, rows, DISPARITIES, width), bf16)
    kept, last = call(
        first_vertical_kernel,
        (
            jax.ShapeDtypeStruct((rows, DISPARITIES, width), f32),
            jax.ShapeDtypeStruct((DISPARITIES, width), bf16),
        ),
        [SMEM(), SMEM()] + [VMEM()] * half,
        [joined],
        flops=2 * 10**9,
    )(place, smooth, *blocks)

    swap = [(i, (i + half) % row_count) for i in range(row_count)]
    last, state = lax.optimization_barrier((last, state))
    came = lax.ppermute(last, "row", swap)
    late, _ = call(
        functools.partial(across_kernel, True),
        halves,
        [SMEM(), SMEM(), VMEM(), VMEM()],
        flops=10**10,
    )(place, smooth, cost, state)

    return call(
        second_vertical_kernel,
        jax.ShapeDtypeStruct((rows, width, DISPARITIES), f32),
        [SMEM(), SMEM()] + [VMEM()] * (half + 4),
        [pltpu.VMEM((rows, DISPARITIES, width), f32), joined],
        flops=3 * 10**9,
    )(place, smooth, *blocks, kept, came, early, late)


def solution(mesh):
    return jax.shard_map(
        per_device,
        mesh=mesh,
        in_specs=(P(None, "row", None, "col"), P(), P(), P("row", "col"), P("row", "col"), P()),
        out_specs=P("row", "col", None),
        check_vma=False,
    )
```

```python
import functools

import jax
import jax.numpy as jnp
from jax import lax
from jax.experimental import pallas as pl
from jax.experimental.pallas import tpu as pltpu
from jax.sharding import PartitionSpec as P

DISPARITIES = 128
OFF_MOST = 256
SUB = 8
REGS = DISPARITIES // SUB
MEBI = 1024 * 1024


def lane_to_disparity(lane):
    return (lane % SUB) * REGS + lane // SUB


def disparity_to_lane(disparity):
    return (disparity % REGS) * SUB + disparity // REGS


def least_of(values):
    while len(values) > 1:
        values = [jnp.minimum(a, b) for a, b in zip(values[::2], values[1::2])]
    turned = values + [pltpu.roll(values[0], turn, 0) for turn in range(1, SUB)]
    while len(turned) > 1:
        turned = [jnp.minimum(a, b) for a, b in zip(turned[::2], turned[1::2])]
    return turned[0]


def stepped(state, p1):
    row = lax.broadcasted_iota(jnp.int32, state[0].shape, 0)
    below = jnp.where(row == 0, jnp.inf, pltpu.roll(state[-1], 1, 0))
    above = jnp.where(row == SUB - 1, jnp.inf, pltpu.roll(state[0], SUB - 1, 0))
    lower = [below] + state[:-1]
    upper = state[1:] + [above]
    return [
        jnp.minimum(s, jnp.minimum(l, u) + p1) for s, l, u in zip(state, lower, upper)
    ]


def advance(state, cost, p1, p2):
    least = least_of(state)
    return [c + jnp.minimum(t - least, p2) for t, c in zip(stepped(state, p1), cost)]


def ends(values, depth):
    row = lax.broadcasted_iota(jnp.int32, values[0].shape, 0)
    low = [jnp.where(row == 0, jnp.inf, pltpu.roll(v, 1, 0)) for v in values[-depth:]]
    high = [jnp.where(row == SUB - 1, jnp.inf, pltpu.roll(v, SUB - 1, 0)) for v in values[:depth]]
    return low, high


def walk(wide, cost, p1):
    return [
        c + jnp.minimum(s, jnp.minimum(l, u) + p1)
        for l, s, u, c in zip(wide[:-2], wide[1:-1], wide[2:], cost)
    ]


def leap(walked, cost, jump):
    return [jnp.minimum(w, c + jump) for w, c in zip(walked, cost)]


def next_jump(walked, cost, jump, p2):
    cheapest = cost
    while len(cheapest) > 1:
        cheapest = [jnp.minimum(a, b) for a, b in zip(cheapest[::2], cheapest[1::2])]
    cheapest = cheapest[0]
    for turn in (4, 2, 1):
        cheapest = jnp.minimum(cheapest, pltpu.roll(cheapest, turn, 0))
    return jnp.minimum(least_of(walked) + p2, (cheapest + p2) + jump)


def advance_pair(wide, jump, first, second, p1, p2):
    low, high = ends(first, 1)
    beyond = low + first + high
    walked = walk(wide, beyond, p1)
    middle = leap(walked, beyond, jump)
    jump_between = next_jump(walked[1:-1], first, jump, p2)
    walked = walk(middle, second, p1)
    low, high = ends(walked, 2)
    cost_low, cost_high = ends(second, 2)
    wide = leap(low + walked + high, cost_low + second + cost_high, jump_between)
    return wide, middle[1:-1], jump_between, next_jump(walked, second, jump_between, p2)


def charges(charge_ref):
    return (
        charge_ref[0].astype(jnp.float32) * (1.0 / 64.0),
        charge_ref[1].astype(jnp.float32) * (1.0 / 64.0),
    )


def registers(array):
    return [array[SUB * v : SUB * (v + 1)] for v in range(REGS)]


def band_kernel(masks, place_ref, filter_ref, bias_ref, *refs):
    parts = len(masks)
    tile_refs, edge_refs, refs = refs[:parts], refs[parts : 2 * parts], refs[2 * parts :]
    cost_ref, own_ref, maps_a, maps_b, left_unit, right_unit, present, shifts, taps_ref = refs
    _, channels, width = tile_refs[0].shape
    layers = filter_ref.shape[0]
    rows = own_ref.shape[0]
    cols = parts * width
    high = rows + 2 * layers
    first_row = place_ref[0] * rows
    rows_total = place_ref[1] * rows
    own = place_ref[2]
    lead = (OFF_MOST + 2 * width - 1) // width * width

    for layer in range(layers):
        for a in range(3):
            for b in range(3):
                taps_ref[
                    layer, b * channels : (b + 1) * channels, a * channels : (a + 1) * channels
                ] = filter_ref[layer, a, b]

    for mask, edge_ref in zip(masks, edge_refs):
        member = own ^ mask
        extra = edge_ref[4 * layers].astype(jnp.float32)
        present[:, pl.ds(pl.multiple_of(member * width, width), width)] = extra[0:16]
        shifts[member] = extra[16:24]
    right_unit[:, 0:lead] = jnp.zeros((rows * channels, lead), jnp.bfloat16)
    right_unit[:, lead + cols :] = jnp.zeros((rows * channels, width), jnp.bfloat16)

    column = lax.broadcasted_iota(jnp.int32, (1, cols), 1)
    for image in range(2):

        for mask, tile_ref, edge_ref in zip(masks, tile_refs, edge_refs):
            there = pl.ds(pl.multiple_of((own ^ mask) * width, width), width)
            for row in range(high):
                if row < layers:
                    value = edge_ref[image * layers + row]
                elif row < layers + rows:
                    value = tile_ref[image * rows + row - layers]
                else:
                    value = edge_ref[(2 + image) * layers + row - layers - rows]
                maps_a[row * channels : (row + 1) * channels, there] = value

        for layer in range(layers):
            source, target = (maps_a, maps_b) if layer % 2 == 0 else (maps_b, maps_a)
            margin = layers - 1 - layer

            steps = rows + 2 * margin

            @pl.loop(0, steps, unroll=max(k for k in range(1, 6) if steps % k == 0))
            def _(row):
                start = pl.multiple_of(row * channels, channels)
                window = source[pl.ds(start, 3 * channels), :]
                taps = jnp.dot(taps_ref[layer], window, preferred_element_type=jnp.float32)
                before = pltpu.roll(taps[:channels], 1, 1)
                after = pltpu.roll(taps[2 * channels :], cols - 1, 1)
                z = taps[channels : 2 * channels] + jnp.where(column == 0, 0.0, before)
                z = z + jnp.where(column == cols - 1, 0.0, after) + bias_ref[layer]
                if layer < layers - 1:
                    there = first_row - margin + row
                    inside = jnp.logical_and(there >= 0, there < rows_total)
                    z = jnp.maximum(z, 0.0) * jnp.where(inside, 1.0, 0.0)
                    target[pl.ds(start, channels), :] = z.astype(jnp.bfloat16)
                else:
                    scale = lax.rsqrt(jnp.sum(z * z, axis=0, keepdims=True) + 1e-06)
                    unit = (z * scale).astype(jnp.bfloat16)
                    if image == 0:
                        seen = present[pl.ds(row, 1), :]
                        unit = jnp.where(seen > 0.5, unit.astype(jnp.float32), 0.0)
                        left_unit[pl.ds(start, channels), :] = unit.astype(jnp.bfloat16)
                    else:
                        right_unit[pl.ds(start, channels), lead : lead + cols] = unit

    lane = lax.broadcasted_iota(jnp.int32, (width, DISPARITIES), 1)
    place = lax.broadcasted_iota(jnp.int32, (width, DISPARITIES), 0)

    @pl.loop(0, parts)
    def _(p):
        shift = jnp.max(shifts[p]).astype(jnp.int32)
        base = p * width - shift + lead
        block = base // width
        ahead = place + (base - block * width)
        index = (ahead - lane_to_disparity(lane)) & (DISPARITIES - 1)
        start = pl.multiple_of((block - 1) * width, width)
        here = pl.multiple_of(p * width, width)

        def tile_costs(mine):
            for y in range(rows):
                left = left_unit[y * channels : (y + 1) * channels, pl.ds(here, width)]
                right = right_unit[y * channels : (y + 1) * channels, pl.ds(start, 3 * width)]
                product = lax.dot_general(
                    left, right, (((0,), (0,)), ((), ())), preferred_element_type=jnp.float32
                )
                chosen = jnp.where(lane <= ahead, product[:, width : 2 * width], product[:, :width])
                chosen = jnp.where(lane <= ahead - width, product[:, 2 * width :], chosen)
                chosen = jnp.take_along_axis(chosen, index, axis=1, mode="promise_in_bounds")
                chosen = 1.0 - chosen
                cost_ref[pl.ds(here, width), y, :] = chosen
                if mine:
                    own_ref[y] = chosen.T.astype(jnp.bfloat16)

        pl.when(p == own)(functools.partial(tile_costs, True))
        pl.when(p != own)(functools.partial(tile_costs, False))


def across_kernel(second, place_ref, charge_ref, cost_ref, *refs):
    kept_ref, last_ref, same_ref = refs[-3:]
    cols = cost_ref.shape[0]
    width, rows, _ = kept_ref.shape
    parts = cols // width
    own = place_ref[2]
    p1, p2 = charges(charge_ref)

    place = lax.broadcasted_iota(jnp.int32, (DISPARITIES, 2 * DISPARITIES), 0)
    other = lax.broadcasted_iota(jnp.int32, (DISPARITIES, 2 * DISPARITIES), 1)
    same_ref[...] = jnp.where(place == other % DISPARITIES, 1.0, 0.0).astype(jnp.bfloat16)
    same = same_ref[...]

    def cost_at(step):
        step = jnp.minimum(step, cols - 1)
        pair = jnp.concatenate([cost_ref[step], cost_ref[cols - 1 - step]], axis=0)
        coarse = pair.astype(jnp.bfloat16)
        fine = (pair - coarse.astype(jnp.float32)).astype(jnp.bfloat16)
        return registers(
            lax.dot_general(
                same,
                jnp.concatenate([coarse, fine], axis=1),
                (((1,), (1,)), ((), ())),
                preferred_element_type=jnp.float32,
            )
        )

    def segment(p, state):
        first_step = p * width

        def run(keep_right, keep_left, state):
            def keep(i, values, jump):
                back = jnp.concatenate([v - (jump - p2) for v in values], axis=0).T
                if keep_right:
                    kept_ref[i] = back[0:rows]
                else:
                    kept_ref[width - 1 - i] = back[rows : 2 * rows]

            def body(i, carry):
                wide, jump, first = carry
                second = cost_at(first_step + 2 * i + 1)
                ahead = cost_at(first_step + 2 * i + 2)
                wide, middle, between, following = advance_pair(
                    list(wide), jump, list(first), second, p1, p2
                )
                if keep_right or keep_left:
                    keep(2 * i, middle, jump)
                    keep(2 * i + 1, wide[2:-2], between)
                return tuple(wide), following, tuple(ahead)

            low, high = ends(list(state), 2)
            level = jnp.zeros((SUB, 2 * rows), jnp.float32) + p2
            carry = (tuple(low + list(state) + high), level, tuple(cost_at(first_step)))
            wide, jump, _ = lax.fori_loop(0, width // 2, body, carry, unroll=8)
            return tuple(s - (jump - p2) for s in wide[2:-2])

        choice = jnp.where(p == own, 1, 0) + jnp.where(parts - 1 - p == own, 2, 0)
        return lax.switch(
            choice,
            [functools.partial(run, k == 1, k == 2) for k in range(3)],
            state,
        )

    if second:
        state = tuple(registers(refs[0][...]))
        span = (parts // 2, parts)
    else:
        state = tuple(jnp.zeros((SUB, 2 * rows), jnp.float32) for _ in range(REGS))
        span = (0, parts // 2)
    last_ref[...] = jnp.concatenate(lax.fori_loop(*span, segment, state), axis=0)


def down_or_up(forward, first_own, cost_ref, state, p1, p2, keep):
    group, rows = cost_ref.shape[:2]

    def block(b, state):
        member = jnp.where(forward, b, group - 1 - b)

        def run(kept, state):
            for i in range(rows):
                inner = jnp.where(forward, i, rows - 1 - i)
                cost = cost_ref[member, inner].astype(jnp.float32)
                state = advance(list(state), registers(cost), p1, p2)
                if kept:
                    keep(inner, jnp.concatenate(state, axis=0))
            return tuple(state)

        return lax.cond(
            member == first_own,
            functools.partial(run, True),
            functools.partial(run, False),
            state,
        )

    return lax.fori_loop(0, group, block, state)


def first_vertical_kernel(place_ref, charge_ref, *refs):
    *block_refs, kept_ref, last_ref, cost_ref = refs
    p1, p2 = charges(charge_ref)
    group, _, _, width = cost_ref.shape
    for k, block_ref in enumerate(block_refs):
        cost_ref[lax.rem(place_ref[4] + group - k, group)] = block_ref[...]
    state = tuple(jnp.zeros((SUB, width), jnp.float32) for _ in range(REGS))

    def keep(row, value):
        kept_ref[row] = value

    final = down_or_up(place_ref[3] == 0, place_ref[4], cost_ref, state, p1, p2, keep)
    last_ref[...] = jnp.concatenate(final, axis=0).astype(jnp.bfloat16)


def second_vertical_kernel(place_ref, charge_ref, *refs):
    *block_refs, kept_ref, came_ref, early_ref, late_ref, out_ref, total, cost_ref = refs
    p1, p2 = charges(charge_ref)
    group = cost_ref.shape[0]
    for k, block_ref in enumerate(block_refs):
        cost_ref[lax.rem(place_ref[4] + group - k, group)] = block_ref[...]
    rows, _, width = kept_ref.shape
    state = tuple(registers(came_ref[...].astype(jnp.float32)))

    def keep(row, value):
        total[row] = value + kept_ref[row]

    down_or_up(place_ref[3] != 0, place_ref[4], cost_ref, state, p1, p2, keep)
    lane = lax.broadcasted_iota(jnp.int32, (width, DISPARITIES), 1)
    index = disparity_to_lane(lane)
    for row in range(rows):
        value = total[row].T + (early_ref[:, row, :] + late_ref[:, row, :])
        out_ref[row] = jnp.take_along_axis(value, index, axis=1, mode="promise_in_bounds")


SMEM = functools.partial(pl.BlockSpec, memory_space=pltpu.SMEM)
VMEM = functools.partial(pl.BlockSpec, memory_space=pltpu.VMEM)


def call(kernel, outs, specs, scratch=(), flops=0, vmem=20):
    return pl.pallas_call(
        kernel,
        out_shape=outs,
        in_specs=specs,
        out_specs=jax.tree.map(lambda _: VMEM(), outs),
        scratch_shapes=list(scratch),
        compiler_params=pltpu.CompilerParams(vmem_limit_bytes=vmem * MEBI),
        cost_estimate=pl.CostEstimate(flops=flops, bytes_accessed=1 << 22, transcendentals=0),
    )


def spread(block, parts):
    masks, blocks = [0], [block]
    bit = parts // 2
    while bit:
        route = [(i, i ^ bit) for i in range(parts)]
        blocks += [lax.ppermute(held, "col", route) for held in blocks]
        masks += [mask ^ bit for mask in masks]
        bit //= 2
    return masks, blocks


def per_device(activations, filters, biases, present, shifts, smooth):
    _, rows, channels, width = activations.shape
    layers = filters.shape[0]
    high = rows + 2 * layers
    row_rank, row_count = lax.axis_index("row"), lax.axis_size("row")
    col_rank, parts = lax.axis_index("col"), lax.axis_size("col")
    half = row_count // 2
    cols = parts * width
    place = jnp.stack(
        [row_rank, jnp.int32(row_count), col_rank, row_rank // half, row_rank % half]
    ).astype(jnp.int32)

    downward = [(i, i + 1) for i in range(row_count - 1)]
    upward = [(i + 1, i) for i in range(row_count - 1)]
    before = lax.ppermute(activations[:, rows - layers :], "row", downward)
    after = lax.ppermute(activations[:, :layers], "row", upward)
    extra = jnp.concatenate(
        [
            present.astype(jnp.bfloat16),
            jnp.zeros((16 - rows, width), jnp.bfloat16),
            jnp.broadcast_to(shifts.astype(jnp.bfloat16), (channels - 16, width)),
        ],
        axis=0,
    )
    edges = jnp.concatenate(
        [before.reshape(-1, channels, width), after.reshape(-1, channels, width), extra[None]],
        axis=0,
    )
    masks, tiles = spread(activations.reshape(2 * rows, channels, width), parts)
    _, edges = spread(edges, parts)

    f32, bf16 = jnp.float32, jnp.bfloat16
    lead = (OFF_MOST + 2 * width - 1) // width * width
    cost, own = call(
        functools.partial(band_kernel, masks),
        (
            jax.ShapeDtypeStruct((cols, rows, DISPARITIES), f32),
            jax.ShapeDtypeStruct((rows, DISPARITIES, width), bf16),
        ),
        [SMEM()] + [VMEM()] * (2 + 2 * parts),
        [
            pltpu.VMEM((high * channels, cols), bf16),
            pltpu.VMEM(((high - 2) * channels, cols), bf16),
            pltpu.VMEM((rows * channels, cols), bf16),
            pltpu.VMEM((rows * channels, lead + cols + width), bf16),
            pltpu.VMEM((16, cols), f32),
            pltpu.VMEM((parts, SUB, width), f32),
            pltpu.VMEM((layers, 3 * channels, 3 * channels), bf16),
        ],
        flops=10**10,
        vmem=40,
    )(place, filters, biases[:, :, None], *tiles, *edges)

    blocks = [own]
    for k in range(1, half):
        turn = [(i, i // half * half + (i + k) % half) for i in range(row_count)]
        blocks.append(lax.ppermute(own, "row", turn))

    halves = (
        jax.ShapeDtypeStruct((width, rows, DISPARITIES), f32),
        jax.ShapeDtypeStruct((DISPARITIES, 2 * rows), f32),
    )
    identity = [pltpu.VMEM((DISPARITIES, 2 * DISPARITIES), bf16)]
    early, state = call(
        functools.partial(across_kernel, False),
        halves,
        [SMEM(), SMEM(), VMEM()],
        identity,
        flops=10**10,
    )(place, smooth, cost)
    *blocks, state = lax.optimization_barrier((*blocks, state))

    joined = pltpu.VMEM((half, rows, DISPARITIES, width), bf16)
    kept, last = call(
        first_vertical_kernel,
        (
            jax.ShapeDtypeStruct((rows, DISPARITIES, width), f32),
            jax.ShapeDtypeStruct((DISPARITIES, width), bf16),
        ),
        [SMEM(), SMEM()] + [VMEM()] * half,
        [joined],
        flops=2 * 10**9,
    )(place, smooth, *blocks)

    swap = [(i, (i + half) % row_count) for i in range(row_count)]
    last, state = lax.optimization_barrier((last, state))
    came = lax.ppermute(last, "row", swap)
    late, _ = call(
        functools.partial(across_kernel, True),
        halves,
        [SMEM(), SMEM(), VMEM(), VMEM()],
        identity,
        flops=10**10,
    )(place, smooth, cost, state)

    return call(
        second_vertical_kernel,
        jax.ShapeDtypeStruct((rows, width, DISPARITIES), f32),
        [SMEM(), SMEM()] + [VMEM()] * (half + 4),
        [pltpu.VMEM((rows, DISPARITIES, width), f32), joined],
        flops=3 * 10**9,
    )(place, smooth, *blocks, kept, came, early, late)


def solution(mesh):
    return jax.shard_map(
        per_device,
        mesh=mesh,
        in_specs=(P(None, "row", None, "col"), P(), P(), P("row", "col"), P("row", "col"), P()),
        out_specs=P("row", "col", None),
        check_vma=False,
    )
```

```python
import functools

import jax
import jax.numpy as jnp
from jax import lax
from jax.experimental import pallas as pl
from jax.experimental.pallas import tpu as pltpu
from jax.sharding import PartitionSpec as P

DISPARITIES = 128
OFF_MOST = 256
SUB = 8
REGS = DISPARITIES // SUB
MEBI = 1024 * 1024


def lane_to_disparity(lane):
    return (lane % SUB) * REGS + lane // SUB


def disparity_to_lane(disparity):
    return (disparity % REGS) * SUB + disparity // REGS


def least_of(values):
    while len(values) > 1:
        values = [jnp.minimum(a, b) for a, b in zip(values[::2], values[1::2])]
    turned = values + [pltpu.roll(values[0], turn, 0) for turn in range(1, SUB)]
    while len(turned) > 1:
        turned = [jnp.minimum(a, b) for a, b in zip(turned[::2], turned[1::2])]
    return turned[0]


def stepped(state, p1):
    row = lax.broadcasted_iota(jnp.int32, state[0].shape, 0)
    below = jnp.where(row == 0, jnp.inf, pltpu.roll(state[-1], 1, 0))
    above = jnp.where(row == SUB - 1, jnp.inf, pltpu.roll(state[0], SUB - 1, 0))
    lower = [below] + state[:-1]
    upper = state[1:] + [above]
    return [
        jnp.minimum(s, jnp.minimum(l, u) + p1) for s, l, u in zip(state, lower, upper)
    ]


def advance(state, cost, p1, p2):
    least = least_of(state)
    return [c + jnp.minimum(t - least, p2) for t, c in zip(stepped(state, p1), cost)]


def ends(values, depth):
    row = lax.broadcasted_iota(jnp.int32, values[0].shape, 0)
    low = [jnp.where(row == 0, jnp.inf, pltpu.roll(v, 1, 0)) for v in values[-depth:]]
    high = [jnp.where(row == SUB - 1, jnp.inf, pltpu.roll(v, SUB - 1, 0)) for v in values[:depth]]
    return low, high


def walk(wide, cost, p1):
    return [
        c + jnp.minimum(s, jnp.minimum(l, u) + p1)
        for l, s, u, c in zip(wide[:-2], wide[1:-1], wide[2:], cost)
    ]


def leap(walked, cost, jump):
    return [jnp.minimum(w, c + jump) for w, c in zip(walked, cost)]


def next_jump(walked, cost, jump, p2):
    cheapest = cost
    while len(cheapest) > 1:
        cheapest = [jnp.minimum(a, b) for a, b in zip(cheapest[::2], cheapest[1::2])]
    cheapest = cheapest[0]
    for turn in (4, 2, 1):
        cheapest = jnp.minimum(cheapest, pltpu.roll(cheapest, turn, 0))
    return jnp.minimum(least_of(walked) + p2, (cheapest + p2) + jump)


def advance_pair(wide, jump, first, second, p1, p2):
    low, high = ends(first, 1)
    beyond = low + first + high
    walked = walk(wide, beyond, p1)
    middle = leap(walked, beyond, jump)
    jump_between = next_jump(walked[1:-1], first, jump, p2)
    walked = walk(middle, second, p1)
    low, high = ends(walked, 2)
    cost_low, cost_high = ends(second, 2)
    wide = leap(low + walked + high, cost_low + second + cost_high, jump_between)
    return wide, middle[1:-1], jump_between, next_jump(walked, second, jump_between, p2)


def charges(charge_ref):
    return (
        charge_ref[0].astype(jnp.float32) * (1.0 / 64.0),
        charge_ref[1].astype(jnp.float32) * (1.0 / 64.0),
    )


def registers(array):
    return [array[SUB * v : SUB * (v + 1)] for v in range(REGS)]


def band_kernel(masks, place_ref, filter_ref, bias_ref, *refs):
    parts = len(masks)
    tile_refs, edge_refs, refs = refs[:parts], refs[parts : 2 * parts], refs[2 * parts :]
    cost_ref, own_ref, maps_a, maps_b, left_unit, right_unit, present, shifts, taps_ref = refs
    _, channels, width = tile_refs[0].shape
    layers = filter_ref.shape[0]
    rows = own_ref.shape[0]
    cols = parts * width
    high = rows + 2 * layers
    first_row = place_ref[0] * rows
    rows_total = place_ref[1] * rows
    own = place_ref[2]
    lead = (OFF_MOST + 2 * width - 1) // width * width

    for layer in range(layers):
        for a in range(3):
            for b in range(3):
                taps_ref[
                    layer, b * channels : (b + 1) * channels, a * channels : (a + 1) * channels
                ] = filter_ref[layer, a, b]

    for mask, edge_ref in zip(masks, edge_refs):
        member = own ^ mask
        extra = edge_ref[4 * layers].astype(jnp.float32)
        present[:, pl.ds(pl.multiple_of(member * width, width), width)] = extra[0:16]
        shifts[member] = extra[16:24]
    right_unit[:, 0:lead] = jnp.zeros((rows * channels, lead), jnp.bfloat16)
    right_unit[:, lead + cols :] = jnp.zeros((rows * channels, width), jnp.bfloat16)

    column = lax.broadcasted_iota(jnp.int32, (1, cols), 1)
    for image in range(2):

        for mask, tile_ref, edge_ref in zip(masks, tile_refs, edge_refs):
            there = pl.ds(pl.multiple_of((own ^ mask) * width, width), width)
            for row in range(high):
                if row < layers:
                    value = edge_ref[image * layers + row]
                elif row < layers + rows:
                    value = tile_ref[image * rows + row - layers]
                else:
                    value = edge_ref[(2 + image) * layers + row - layers - rows]
                maps_a[row * channels : (row + 1) * channels, there] = value

        for layer in range(layers):
            source, target = (maps_a, maps_b) if layer % 2 == 0 else (maps_b, maps_a)
            margin = layers - 1 - layer

            steps = rows + 2 * margin

            @pl.loop(0, steps, unroll=max(k for k in range(1, 6) if steps % k == 0))
            def _(row):
                start = pl.multiple_of(row * channels, channels)
                window = source[pl.ds(start, 3 * channels), :]
                taps = jnp.dot(taps_ref[layer], window, preferred_element_type=jnp.float32)
                before = pltpu.roll(taps[:channels], 1, 1)
                after = pltpu.roll(taps[2 * channels :], cols - 1, 1)
                z = taps[channels : 2 * channels] + jnp.where(column == 0, 0.0, before)
                z = z + jnp.where(column == cols - 1, 0.0, after) + bias_ref[layer]
                if layer < layers - 1:
                    there = first_row - margin + row
                    inside = jnp.logical_and(there >= 0, there < rows_total)
                    z = jnp.maximum(z, 0.0) * jnp.where(inside, 1.0, 0.0)
                    target[pl.ds(start, channels), :] = z.astype(jnp.bfloat16)
                else:
                    scale = lax.rsqrt(jnp.sum(z * z, axis=0, keepdims=True) + 1e-06)
                    unit = (z * scale).astype(jnp.bfloat16)
                    if image == 0:
                        seen = present[pl.ds(row, 1), :]
                        unit = jnp.where(seen > 0.5, unit.astype(jnp.float32), 0.0)
                        left_unit[pl.ds(start, channels), :] = unit.astype(jnp.bfloat16)
                    else:
                        right_unit[pl.ds(start, channels), lead : lead + cols] = unit

    lane = lax.broadcasted_iota(jnp.int32, (width, DISPARITIES), 1)
    place = lax.broadcasted_iota(jnp.int32, (width, DISPARITIES), 0)

    @pl.loop(0, parts)
    def _(p):
        shift = jnp.max(shifts[p]).astype(jnp.int32)
        base = p * width - shift + lead
        block = base // width
        ahead = place + (base - block * width)
        index = (ahead - lane_to_disparity(lane)) & (DISPARITIES - 1)
        start = pl.multiple_of((block - 1) * width, width)
        here = pl.multiple_of(p * width, width)

        def tile_costs(mine):
            for y in range(rows):
                left = left_unit[y * channels : (y + 1) * channels, pl.ds(here, width)]
                right = right_unit[y * channels : (y + 1) * channels, pl.ds(start, 3 * width)]
                product = lax.dot_general(
                    left, right, (((0,), (0,)), ((), ())), preferred_element_type=jnp.float32
                )
                chosen = jnp.where(lane <= ahead, product[:, width : 2 * width], product[:, :width])
                chosen = jnp.where(lane <= ahead - width, product[:, 2 * width :], chosen)
                chosen = jnp.take_along_axis(chosen, index, axis=1, mode="promise_in_bounds")
                chosen = 1.0 - chosen
                cost_ref[pl.ds(here, width), y, :] = chosen
                if mine:
                    own_ref[y] = chosen.T.astype(jnp.bfloat16)

        pl.when(p == own)(functools.partial(tile_costs, True))
        pl.when(p != own)(functools.partial(tile_costs, False))


def across_kernel(second, place_ref, charge_ref, cost_ref, *refs):
    kept_ref, last_ref, same_ref = refs[-3:]
    cols = cost_ref.shape[0]
    width, rows, _ = kept_ref.shape
    parts = cols // width
    own = place_ref[2]
    p1, p2 = charges(charge_ref)

    place = lax.broadcasted_iota(jnp.int32, (DISPARITIES, 2 * DISPARITIES), 0)
    other = lax.broadcasted_iota(jnp.int32, (DISPARITIES, 2 * DISPARITIES), 1)
    same_ref[...] = jnp.where(place == other % DISPARITIES, 1.0, 0.0).astype(jnp.bfloat16)
    same = same_ref[...]

    def cost_at(step):
        step = jnp.minimum(step, cols - 1)
        pair = jnp.concatenate([cost_ref[step], cost_ref[cols - 1 - step]], axis=0)
        coarse = pair.astype(jnp.bfloat16)
        fine = (pair - coarse.astype(jnp.float32)).astype(jnp.bfloat16)
        return registers(
            lax.dot_general(
                same,
                jnp.concatenate([coarse, fine], axis=1),
                (((1,), (1,)), ((), ())),
                preferred_element_type=jnp.float32,
            )
        )

    def segment(p, state):
        first_step = p * width

        def run(keep_right, keep_left, state):
            def keep(i, values, jump):
                values = jnp.concatenate([v - (jump - p2) for v in values], axis=0)
                back = lax.dot_general(
                    same[: 2 * rows, : 2 * rows],
                    values.astype(jnp.bfloat16),
                    (((1,), (1,)), ((), ())),
                    preferred_element_type=jnp.float32,
                )
                if keep_right:
                    kept_ref[i] = back[0:rows]
                else:
                    kept_ref[width - 1 - i] = back[rows : 2 * rows]

            def body(i, carry):
                wide, jump, first = carry
                second = cost_at(first_step + 2 * i + 1)
                ahead = cost_at(first_step + 2 * i + 2)
                wide, middle, between, following = advance_pair(
                    list(wide), jump, list(first), second, p1, p2
                )
                if keep_right or keep_left:
                    keep(2 * i, middle, jump)
                    keep(2 * i + 1, wide[2:-2], between)
                return tuple(wide), following, tuple(ahead)

            low, high = ends(list(state), 2)
            level = jnp.zeros((SUB, 2 * rows), jnp.float32) + p2
            carry = (tuple(low + list(state) + high), level, tuple(cost_at(first_step)))
            wide, jump, _ = lax.fori_loop(0, width // 2, body, carry, unroll=8)
            return tuple(s - (jump - p2) for s in wide[2:-2])

        choice = jnp.where(p == own, 1, 0) + jnp.where(parts - 1 - p == own, 2, 0)
        return lax.switch(
            choice,
            [functools.partial(run, k == 1, k == 2) for k in range(3)],
            state,
        )

    if second:
        state = tuple(registers(refs[0][...]))
        span = (parts // 2, parts)
    else:
        state = tuple(jnp.zeros((SUB, 2 * rows), jnp.float32) for _ in range(REGS))
        span = (0, parts // 2)
    last_ref[...] = jnp.concatenate(lax.fori_loop(*span, segment, state), axis=0)


def down_or_up(forward, first_own, cost_ref, state, p1, p2, keep):
    group, rows = cost_ref.shape[:2]

    def block(b, state):
        member = jnp.where(forward, b, group - 1 - b)

        def run(kept, state):
            for i in range(rows):
                inner = jnp.where(forward, i, rows - 1 - i)
                cost = cost_ref[member, inner].astype(jnp.float32)
                state = advance(list(state), registers(cost), p1, p2)
                if kept:
                    keep(inner, jnp.concatenate(state, axis=0))
            return tuple(state)

        return lax.cond(
            member == first_own,
            functools.partial(run, True),
            functools.partial(run, False),
            state,
        )

    return lax.fori_loop(0, group, block, state)


def first_vertical_kernel(place_ref, charge_ref, *refs):
    *block_refs, kept_ref, last_ref, cost_ref = refs
    p1, p2 = charges(charge_ref)
    group, _, _, width = cost_ref.shape
    for k, block_ref in enumerate(block_refs):
        cost_ref[lax.rem(place_ref[4] + group - k, group)] = block_ref[...]
    state = tuple(jnp.zeros((SUB, width), jnp.float32) for _ in range(REGS))

    def keep(row, value):
        kept_ref[row] = value

    final = down_or_up(place_ref[3] == 0, place_ref[4], cost_ref, state, p1, p2, keep)
    last_ref[...] = jnp.concatenate(final, axis=0).astype(jnp.bfloat16)


def second_vertical_kernel(place_ref, charge_ref, *refs):
    *block_refs, kept_ref, came_ref, early_ref, late_ref, out_ref, total, cost_ref = refs
    p1, p2 = charges(charge_ref)
    group = cost_ref.shape[0]
    for k, block_ref in enumerate(block_refs):
        cost_ref[lax.rem(place_ref[4] + group - k, group)] = block_ref[...]
    rows, _, width = kept_ref.shape
    state = tuple(registers(came_ref[...].astype(jnp.float32)))

    def keep(row, value):
        total[row] = value + kept_ref[row]

    down_or_up(place_ref[3] != 0, place_ref[4], cost_ref, state, p1, p2, keep)
    lane = lax.broadcasted_iota(jnp.int32, (width, DISPARITIES), 1)
    index = disparity_to_lane(lane)
    for row in range(rows):
        value = total[row].T + (early_ref[:, row, :] + late_ref[:, row, :])
        out_ref[row] = jnp.take_along_axis(value, index, axis=1, mode="promise_in_bounds")


SMEM = functools.partial(pl.BlockSpec, memory_space=pltpu.SMEM)
VMEM = functools.partial(pl.BlockSpec, memory_space=pltpu.VMEM)


def call(kernel, outs, specs, scratch=(), flops=0, vmem=20):
    return pl.pallas_call(
        kernel,
        out_shape=outs,
        in_specs=specs,
        out_specs=jax.tree.map(lambda _: VMEM(), outs),
        scratch_shapes=list(scratch),
        compiler_params=pltpu.CompilerParams(vmem_limit_bytes=vmem * MEBI),
        cost_estimate=pl.CostEstimate(flops=flops, bytes_accessed=1 << 22, transcendentals=0),
    )


def spread(block, parts):
    masks, blocks = [0], [block]
    bit = parts // 2
    while bit:
        route = [(i, i ^ bit) for i in range(parts)]
        blocks += [lax.ppermute(held, "col", route) for held in blocks]
        masks += [mask ^ bit for mask in masks]
        bit //= 2
    return masks, blocks


def per_device(activations, filters, biases, present, shifts, smooth):
    _, rows, channels, width = activations.shape
    layers = filters.shape[0]
    high = rows + 2 * layers
    row_rank, row_count = lax.axis_index("row"), lax.axis_size("row")
    col_rank, parts = lax.axis_index("col"), lax.axis_size("col")
    half = row_count // 2
    cols = parts * width
    place = jnp.stack(
        [row_rank, jnp.int32(row_count), col_rank, row_rank // half, row_rank % half]
    ).astype(jnp.int32)

    downward = [(i, i + 1) for i in range(row_count - 1)]
    upward = [(i + 1, i) for i in range(row_count - 1)]
    before = lax.ppermute(activations[:, rows - layers :], "row", downward)
    after = lax.ppermute(activations[:, :layers], "row", upward)
    extra = jnp.concatenate(
        [
            present.astype(jnp.bfloat16),
            jnp.zeros((16 - rows, width), jnp.bfloat16),
            jnp.broadcast_to(shifts.astype(jnp.bfloat16), (channels - 16, width)),
        ],
        axis=0,
    )
    edges = jnp.concatenate(
        [before.reshape(-1, channels, width), after.reshape(-1, channels, width), extra[None]],
        axis=0,
    )
    masks, tiles = spread(activations.reshape(2 * rows, channels, width), parts)
    _, edges = spread(edges, parts)

    f32, bf16 = jnp.float32, jnp.bfloat16
    lead = (OFF_MOST + 2 * width - 1) // width * width
    cost, own = call(
        functools.partial(band_kernel, masks),
        (
            jax.ShapeDtypeStruct((cols, rows, DISPARITIES), f32),
            jax.ShapeDtypeStruct((rows, DISPARITIES, width), bf16),
        ),
        [SMEM()] + [VMEM()] * (2 + 2 * parts),
        [
            pltpu.VMEM((high * channels, cols), bf16),
            pltpu.VMEM(((high - 2) * channels, cols), bf16),
            pltpu.VMEM((rows * channels, cols), bf16),
            pltpu.VMEM((rows * channels, lead + cols + width), bf16),
            pltpu.VMEM((16, cols), f32),
            pltpu.VMEM((parts, SUB, width), f32),
            pltpu.VMEM((layers, 3 * channels, 3 * channels), bf16),
        ],
        flops=10**10,
        vmem=40,
    )(place, filters, biases[:, :, None], *tiles, *edges)

    blocks = [own]
    for k in range(1, half):
        turn = [(i, i // half * half + (i + k) % half) for i in range(row_count)]
        blocks.append(lax.ppermute(own, "row", turn))

    halves = (
        jax.ShapeDtypeStruct((width, rows, DISPARITIES), f32),
        jax.ShapeDtypeStruct((DISPARITIES, 2 * rows), f32),
    )
    identity = [pltpu.VMEM((DISPARITIES, 2 * DISPARITIES), bf16)]
    early, state = call(
        functools.partial(across_kernel, False),
        halves,
        [SMEM(), SMEM(), VMEM()],
        identity,
        flops=10**10,
    )(place, smooth, cost)
    *blocks, state = lax.optimization_barrier((*blocks, state))

    joined = pltpu.VMEM((half, rows, DISPARITIES, width), bf16)
    kept, last = call(
        first_vertical_kernel,
        (
            jax.ShapeDtypeStruct((rows, DISPARITIES, width), f32),
            jax.ShapeDtypeStruct((DISPARITIES, width), bf16),
        ),
        [SMEM(), SMEM()] + [VMEM()] * half,
        [joined],
        flops=2 * 10**9,
    )(place, smooth, *blocks)

    swap = [(i, (i + half) % row_count) for i in range(row_count)]
    last, state = lax.optimization_barrier((last, state))
    came = lax.ppermute(last, "row", swap)
    late, _ = call(
        functools.partial(across_kernel, True),
        halves,
        [SMEM(), SMEM(), VMEM(), VMEM()],
        identity,
        flops=10**10,
    )(place, smooth, cost, state)

    return call(
        second_vertical_kernel,
        jax.ShapeDtypeStruct((rows, width, DISPARITIES), f32),
        [SMEM(), SMEM()] + [VMEM()] * (half + 4),
        [pltpu.VMEM((rows, DISPARITIES, width), f32), joined],
        flops=3 * 10**9,
    )(place, smooth, *blocks, kept, came, early, late)


def solution(mesh):
    return jax.shard_map(
        per_device,
        mesh=mesh,
        in_specs=(P(None, "row", None, "col"), P(), P(), P("row", "col"), P("row", "col"), P()),
        out_specs=P("row", "col", None),
        check_vma=False,
    )
```

```python
import functools

import jax
import jax.numpy as jnp
from jax import lax
from jax.experimental import pallas as pl
from jax.experimental.pallas import tpu as pltpu
from jax.sharding import PartitionSpec as P

DISPARITIES = 128
OFF_MOST = 256
SUB = 8
REGS = DISPARITIES // SUB
MEBI = 1024 * 1024


def lane_to_disparity(lane):
    return (lane % SUB) * REGS + lane // SUB


def disparity_to_lane(disparity):
    return (disparity % REGS) * SUB + disparity // REGS


def least_of(values):
    while len(values) > 1:
        values = [jnp.minimum(a, b) for a, b in zip(values[::2], values[1::2])]
    turned = values + [pltpu.roll(values[0], turn, 0) for turn in range(1, SUB)]
    while len(turned) > 1:
        turned = [jnp.minimum(a, b) for a, b in zip(turned[::2], turned[1::2])]
    return turned[0]


def stepped(state, p1):
    row = lax.broadcasted_iota(jnp.int32, state[0].shape, 0)
    below = jnp.where(row == 0, jnp.inf, pltpu.roll(state[-1], 1, 0))
    above = jnp.where(row == SUB - 1, jnp.inf, pltpu.roll(state[0], SUB - 1, 0))
    lower = [below] + state[:-1]
    upper = state[1:] + [above]
    return [
        jnp.minimum(s, jnp.minimum(l, u) + p1) for s, l, u in zip(state, lower, upper)
    ]


def advance(state, cost, p1, p2):
    least = least_of(state)
    return [c + jnp.minimum(t - least, p2) for t, c in zip(stepped(state, p1), cost)]


def ends(values, depth):
    row = lax.broadcasted_iota(jnp.int32, values[0].shape, 0)
    low = [jnp.where(row == 0, jnp.inf, pltpu.roll(v, 1, 0)) for v in values[-depth:]]
    high = [jnp.where(row == SUB - 1, jnp.inf, pltpu.roll(v, SUB - 1, 0)) for v in values[:depth]]
    return low, high


def walk(wide, cost, p1):
    return [
        c + jnp.minimum(s, jnp.minimum(l, u) + p1)
        for l, s, u, c in zip(wide[:-2], wide[1:-1], wide[2:], cost)
    ]


def leap(walked, cost, jump):
    return [jnp.minimum(w, c + jump) for w, c in zip(walked, cost)]


def next_jump(walked, cost, jump, p2):
    cheapest = cost
    while len(cheapest) > 1:
        cheapest = [jnp.minimum(a, b) for a, b in zip(cheapest[::2], cheapest[1::2])]
    cheapest = cheapest[0]
    for turn in (4, 2, 1):
        cheapest = jnp.minimum(cheapest, pltpu.roll(cheapest, turn, 0))
    return jnp.minimum(least_of(walked) + p2, (cheapest + p2) + jump)


def advance_pair(wide, jump, first, second, p1, p2):
    low, high = ends(first, 1)
    beyond = low + first + high
    walked = walk(wide, beyond, p1)
    middle = leap(walked, beyond, jump)
    jump_between = next_jump(walked[1:-1], first, jump, p2)
    walked = walk(middle, second, p1)
    low, high = ends(walked, 2)
    cost_low, cost_high = ends(second, 2)
    wide = leap(low + walked + high, cost_low + second + cost_high, jump_between)
    return wide, middle[1:-1], jump_between, next_jump(walked, second, jump_between, p2)


def charges(charge_ref):
    return (
        charge_ref[0].astype(jnp.float32) * (1.0 / 64.0),
        charge_ref[1].astype(jnp.float32) * (1.0 / 64.0),
    )


def registers(array):
    return [array[SUB * v : SUB * (v + 1)] for v in range(REGS)]


def convolved(taps, window, bias):
    channels, cols = bias.shape[0], window.shape[1]
    column = lax.broadcasted_iota(jnp.int32, (1, cols), 1)
    by_tap = jnp.dot(taps, window, preferred_element_type=jnp.float32)
    before = pltpu.roll(by_tap[:channels], 1, 1)
    after = pltpu.roll(by_tap[2 * channels :], cols - 1, 1)
    z = by_tap[channels : 2 * channels] + jnp.where(column == 0, 0.0, before)
    return z + jnp.where(column == cols - 1, 0.0, after) + bias


def grouping(steps):
    return max(k for k in range(1, 6) if steps % k == 0)


def inner_kernel(masks, place_ref, filter_ref, bias_ref, *refs):
    parts = len(masks)
    tile_refs, (taps_ref, shift_ref, own_ref, *hidden_refs) = refs[:parts], refs[parts:]
    layers, _, _, channels, _ = filter_ref.shape
    width = tile_refs[0].shape[-1]
    rows = tile_refs[0].shape[0] // 2
    own = place_ref[2]

    one = lax.broadcasted_iota(jnp.int32, (channels, channels), 0)
    two = lax.broadcasted_iota(jnp.int32, (channels, channels), 1)
    for layer in range(layers):
        for a in range(3):
            for b in range(3):
                taps_ref[
                    layer, b * channels : (b + 1) * channels, a * channels : (a + 1) * channels
                ] = filter_ref[layer, a, b]
        spread_out = jnp.where(one == two, bias_ref[layer : layer + 1, :], 0.0)
        shift_ref[layer] = jnp.sum(spread_out, axis=1, keepdims=True)

    for image in range(2):
        for mask, tile_ref in zip(masks, tile_refs):
            there = pl.ds(pl.multiple_of((own ^ mask) * width, width), width)
            for row in range(rows):
                own_ref[image, row * channels : (row + 1) * channels, there] = tile_ref[
                    image * rows + row
                ]
        source = own_ref
        for layer, target in enumerate(hidden_refs):
            steps = rows - 2 * (layer + 1)

            @pl.loop(0, steps, unroll=grouping(steps))
            def _(row):
                start = pl.multiple_of(row * channels, channels)
                window = source[image, pl.ds(start, 3 * channels), :]
                z = convolved(taps_ref[layer], window, shift_ref[layer])
                target[image, pl.ds(start, channels), :] = jnp.maximum(z, 0.0).astype(jnp.bfloat16)

            source = target


def band_kernel(masks, place_ref, taps_ref, bias_ref, rows_ref, *refs):
    layers = taps_ref.shape[0]
    parts = len(masks)
    inner_refs, refs = (rows_ref, *refs[: layers - 1]), refs[layers - 1 :]
    edge_refs, refs = refs[:parts], refs[parts:]
    cost_ref, own_ref, left_unit, right_unit, present, shifts, *maps = refs
    _, channels, width = edge_refs[0].shape
    rows = own_ref.shape[0]
    cols = parts * width
    first_row = place_ref[0] * rows
    rows_total = place_ref[1] * rows
    own = place_ref[2]
    lead = (OFF_MOST + 2 * width - 1) // width * width

    for mask, edge_ref in zip(masks, edge_refs):
        member = own ^ mask
        extra = edge_ref[4 * layers].astype(jnp.float32)
        present[:, pl.ds(pl.multiple_of(member * width, width), width)] = extra[0:16]
        shifts[member] = extra[16:24]
    right_unit[:, 0:lead] = jnp.zeros((rows * channels, lead), jnp.bfloat16)
    right_unit[:, lead + cols :] = jnp.zeros((rows * channels, width), jnp.bfloat16)

    for image in range(2):
        for inner_ref, held in zip(inner_refs, maps):
            held[layers * channels : held.shape[0] - layers * channels, :] = inner_ref[image]
        for mask, edge_ref in zip(masks, edge_refs):
            there = pl.ds(pl.multiple_of((own ^ mask) * width, width), width)
            for row in range(layers):
                above, below = row * channels, (layers + rows + row) * channels
                maps[0][above : above + channels, there] = edge_ref[image * layers + row]
                maps[0][below : below + channels, there] = edge_ref[(2 + image) * layers + row]

        for layer in range(layers):
            margin = layers - 1 - layer
            last = layer == layers - 1
            skipped = 0 if last else rows - 2 * (layer + 1)
            steps = rows + 2 * margin - skipped

            @pl.loop(0, steps, unroll=grouping(steps))
            def _(row):
                if not last:
                    row = jnp.where(row < layers, row, row + skipped)
                start = pl.multiple_of(row * channels, channels)
                window = maps[layer][pl.ds(start, 3 * channels), :]
                z = convolved(taps_ref[layer], window, bias_ref[layer])
                if not last:
                    there = first_row - margin + row
                    inside = jnp.logical_and(there >= 0, there < rows_total)
                    z = jnp.maximum(z, 0.0) * jnp.where(inside, 1.0, 0.0)
                    maps[layer + 1][pl.ds(start, channels), :] = z.astype(jnp.bfloat16)
                else:
                    scale = lax.rsqrt(jnp.sum(z * z, axis=0, keepdims=True) + 1e-06)
                    unit = (z * scale).astype(jnp.bfloat16)
                    if image == 0:
                        seen = present[pl.ds(row, 1), :]
                        unit = jnp.where(seen > 0.5, unit.astype(jnp.float32), 0.0)
                        left_unit[pl.ds(start, channels), :] = unit.astype(jnp.bfloat16)
                    else:
                        right_unit[pl.ds(start, channels), lead : lead + cols] = unit

    lane = lax.broadcasted_iota(jnp.int32, (width, DISPARITIES), 1)
    place = lax.broadcasted_iota(jnp.int32, (width, DISPARITIES), 0)

    @pl.loop(0, parts)
    def _(p):
        shift = jnp.max(shifts[p]).astype(jnp.int32)
        base = p * width - shift + lead
        block = base // width
        ahead = place + (base - block * width)
        index = (ahead - lane_to_disparity(lane)) & (DISPARITIES - 1)
        start = pl.multiple_of((block - 1) * width, width)
        here = pl.multiple_of(p * width, width)

        def tile_costs(mine):
            for y in range(rows):
                left = left_unit[y * channels : (y + 1) * channels, pl.ds(here, width)]
                right = right_unit[y * channels : (y + 1) * channels, pl.ds(start, 3 * width)]
                product = lax.dot_general(
                    left, right, (((0,), (0,)), ((), ())), preferred_element_type=jnp.float32
                )
                chosen = jnp.where(lane <= ahead, product[:, width : 2 * width], product[:, :width])
                chosen = jnp.where(lane <= ahead - width, product[:, 2 * width :], chosen)
                chosen = jnp.take_along_axis(chosen, index, axis=1, mode="promise_in_bounds")
                chosen = 1.0 - chosen
                cost_ref[pl.ds(here, width), y, :] = chosen
                if mine:
                    own_ref[y] = chosen.T.astype(jnp.bfloat16)

        pl.when(p == own)(functools.partial(tile_costs, True))
        pl.when(p != own)(functools.partial(tile_costs, False))


def across_kernel(second, place_ref, charge_ref, cost_ref, *refs):
    kept_ref, last_ref, same_ref = refs[-3:]
    cols = cost_ref.shape[0]
    width, rows, _ = kept_ref.shape
    parts = cols // width
    own = place_ref[2]
    p1, p2 = charges(charge_ref)

    place = lax.broadcasted_iota(jnp.int32, (DISPARITIES, 2 * DISPARITIES), 0)
    other = lax.broadcasted_iota(jnp.int32, (DISPARITIES, 2 * DISPARITIES), 1)
    same_ref[...] = jnp.where(place == other % DISPARITIES, 1.0, 0.0).astype(jnp.bfloat16)
    same = same_ref[...]

    def cost_at(step):
        step = jnp.minimum(step, cols - 1)
        pair = jnp.concatenate([cost_ref[step], cost_ref[cols - 1 - step]], axis=0)
        coarse = pair.astype(jnp.bfloat16)
        fine = (pair - coarse.astype(jnp.float32)).astype(jnp.bfloat16)
        return registers(
            lax.dot_general(
                same,
                jnp.concatenate([coarse, fine], axis=1),
                (((1,), (1,)), ((), ())),
                preferred_element_type=jnp.float32,
            )
        )

    def segment(p, state):
        first_step = p * width

        def run(keep_right, keep_left, state):
            def keep(i, values, jump):
                back = jnp.concatenate([v - (jump - p2) for v in values], axis=0).T
                if keep_right:
                    kept_ref[i] = back[0:rows]
                else:
                    kept_ref[width - 1 - i] = back[rows : 2 * rows]

            def body(i, carry):
                wide, jump, first = carry
                second = cost_at(first_step + 2 * i + 1)
                ahead = cost_at(first_step + 2 * i + 2)
                wide, middle, between, following = advance_pair(
                    list(wide), jump, list(first), second, p1, p2
                )
                if keep_right or keep_left:
                    keep(2 * i, middle, jump)
                    keep(2 * i + 1, wide[2:-2], between)
                return tuple(wide), following, tuple(ahead)

            low, high = ends(list(state), 2)
            level = jnp.zeros((SUB, 2 * rows), jnp.float32) + p2
            carry = (tuple(low + list(state) + high), level, tuple(cost_at(first_step)))
            wide, jump, _ = lax.fori_loop(0, width // 2, body, carry, unroll=8)
            return tuple(s - (jump - p2) for s in wide[2:-2])

        choice = jnp.where(p == own, 1, 0) + jnp.where(parts - 1 - p == own, 2, 0)
        return lax.switch(
            choice,
            [functools.partial(run, k == 1, k == 2) for k in range(3)],
            state,
        )

    if second:
        state = tuple(registers(refs[0][...]))
        span = (parts // 2, parts)
    else:
        state = tuple(jnp.zeros((SUB, 2 * rows), jnp.float32) for _ in range(REGS))
        span = (0, parts // 2)
    last_ref[...] = jnp.concatenate(lax.fori_loop(*span, segment, state), axis=0)


def down_or_up(forward, first_own, cost_ref, state, p1, p2, keep):
    group, rows = cost_ref.shape[:2]

    def block(b, state):
        member = jnp.where(forward, b, group - 1 - b)

        def run(kept, state):
            for i in range(rows):
                inner = jnp.where(forward, i, rows - 1 - i)
                cost = cost_ref[member, inner].astype(jnp.float32)
                state = advance(list(state), registers(cost), p1, p2)
                if kept:
                    keep(inner, jnp.concatenate(state, axis=0))
            return tuple(state)

        return lax.cond(
            member == first_own,
            functools.partial(run, True),
            functools.partial(run, False),
            state,
        )

    return lax.fori_loop(0, group, block, state)


def first_vertical_kernel(place_ref, charge_ref, *refs):
    *block_refs, kept_ref, last_ref, cost_ref = refs
    p1, p2 = charges(charge_ref)
    group, _, _, width = cost_ref.shape
    for k, block_ref in enumerate(block_refs):
        cost_ref[lax.rem(place_ref[4] + group - k, group)] = block_ref[...]
    state = tuple(jnp.zeros((SUB, width), jnp.float32) for _ in range(REGS))

    def keep(row, value):
        kept_ref[row] = value

    final = down_or_up(place_ref[3] == 0, place_ref[4], cost_ref, state, p1, p2, keep)
    last_ref[...] = jnp.concatenate(final, axis=0).astype(jnp.bfloat16)


def second_vertical_kernel(place_ref, charge_ref, *refs):
    *block_refs, kept_ref, came_ref, early_ref, late_ref, out_ref, total, cost_ref = refs
    p1, p2 = charges(charge_ref)
    group = cost_ref.shape[0]
    for k, block_ref in enumerate(block_refs):
        cost_ref[lax.rem(place_ref[4] + group - k, group)] = block_ref[...]
    rows, _, width = kept_ref.shape
    state = tuple(registers(came_ref[...].astype(jnp.float32)))

    def keep(row, value):
        total[row] = value + kept_ref[row]

    down_or_up(place_ref[3] != 0, place_ref[4], cost_ref, state, p1, p2, keep)
    lane = lax.broadcasted_iota(jnp.int32, (width, DISPARITIES), 1)
    index = disparity_to_lane(lane)
    for row in range(rows):
        value = total[row].T + (early_ref[:, row, :] + late_ref[:, row, :])
        out_ref[row] = jnp.take_along_axis(value, index, axis=1, mode="promise_in_bounds")


SMEM = functools.partial(pl.BlockSpec, memory_space=pltpu.SMEM)
VMEM = functools.partial(pl.BlockSpec, memory_space=pltpu.VMEM)


def call(kernel, outs, specs, scratch=(), flops=0, vmem=20):
    return pl.pallas_call(
        kernel,
        out_shape=outs,
        in_specs=specs,
        out_specs=jax.tree.map(lambda _: VMEM(), outs),
        scratch_shapes=list(scratch),
        compiler_params=pltpu.CompilerParams(vmem_limit_bytes=vmem * MEBI),
        cost_estimate=pl.CostEstimate(flops=flops, bytes_accessed=1 << 22, transcendentals=0),
    )


def spread(block, parts, beside=()):
    masks, blocks = [0], [block]
    bit = parts // 2
    while bit:
        route = [(i, i ^ bit) for i in range(parts)]
        blocks += [lax.ppermute(held, "col", route) for held in blocks]
        masks += [mask ^ bit for mask in masks]
        if beside and bit == parts // 2:
            first, *beside = lax.optimization_barrier((blocks[1], *beside))
            blocks[1] = first
        bit //= 2
    return masks, blocks, beside


def per_device(activations, filters, biases, present, shifts, smooth):
    _, rows, channels, width = activations.shape
    layers = filters.shape[0]
    high = rows + 2 * layers
    row_rank, row_count = lax.axis_index("row"), lax.axis_size("row")
    col_rank, parts = lax.axis_index("col"), lax.axis_size("col")
    half = row_count // 2
    cols = parts * width
    place = jnp.stack(
        [row_rank, jnp.int32(row_count), col_rank, row_rank // half, row_rank % half]
    ).astype(jnp.int32)

    downward = [(i, i + 1) for i in range(row_count - 1)]
    upward = [(i + 1, i) for i in range(row_count - 1)]
    before = lax.ppermute(activations[:, rows - layers :], "row", downward)
    after = lax.ppermute(activations[:, :layers], "row", upward)
    extra = jnp.concatenate(
        [
            present.astype(jnp.bfloat16),
            jnp.zeros((16 - rows, width), jnp.bfloat16),
            jnp.broadcast_to(shifts.astype(jnp.bfloat16), (channels - 16, width)),
        ],
        axis=0,
    )
    edges = jnp.concatenate(
        [before.reshape(-1, channels, width), after.reshape(-1, channels, width), extra[None]],
        axis=0,
    )
    masks, tiles, _ = spread(activations.reshape(2 * rows, channels, width), parts)

    f32, bf16 = jnp.float32, jnp.bfloat16
    lead = (OFF_MOST + 2 * width - 1) // width * width
    inner = call(
        functools.partial(inner_kernel, masks),
        (
            jax.ShapeDtypeStruct((layers, 3 * channels, 3 * channels), bf16),
            jax.ShapeDtypeStruct((layers, channels, 1), f32),
            *(
                jax.ShapeDtypeStruct((2, (rows - 2 * layer) * channels, cols), bf16)
                for layer in range(layers)
            ),
        ),
        [SMEM()] + [VMEM()] * (2 + parts),
        flops=2 * 10**9,
        vmem=32,
    )(place, filters, biases, *tiles)
    _, edges, inner = spread(edges, parts, inner)
    cost, own = call(
        functools.partial(band_kernel, masks),
        (
            jax.ShapeDtypeStruct((cols, rows, DISPARITIES), f32),
            jax.ShapeDtypeStruct((rows, DISPARITIES, width), bf16),
        ),
        [SMEM()] + [VMEM()] * (2 + layers + parts),
        [
            pltpu.VMEM((rows * channels, cols), bf16),
            pltpu.VMEM((rows * channels, lead + cols + width), bf16),
            pltpu.VMEM((16, cols), f32),
            pltpu.VMEM((parts, SUB, width), f32),
            *(
                pltpu.VMEM(((high - 2 * layer) * channels, cols), bf16)
                for layer in range(layers)
            ),
        ],
        flops=10**10,
        vmem=40,
    )(place, *inner, *edges)

    blocks = [own]
    for k in range(1, half):
        turn = [(i, i // half * half + (i + k) % half) for i in range(row_count)]
        blocks.append(lax.ppermute(own, "row", turn))

    halves = (
        jax.ShapeDtypeStruct((width, rows, DISPARITIES), f32),
        jax.ShapeDtypeStruct((DISPARITIES, 2 * rows), f32),
    )
    identity = [pltpu.VMEM((DISPARITIES, 2 * DISPARITIES), bf16)]
    early, state = call(
        functools.partial(across_kernel, False),
        halves,
        [SMEM(), SMEM(), VMEM()],
        identity,
        flops=10**10,
    )(place, smooth, cost)
    *blocks, state = lax.optimization_barrier((*blocks, state))

    joined = pltpu.VMEM((half, rows, DISPARITIES, width), bf16)
    kept, last = call(
        first_vertical_kernel,
        (
            jax.ShapeDtypeStruct((rows, DISPARITIES, width), f32),
            jax.ShapeDtypeStruct((DISPARITIES, width), bf16),
        ),
        [SMEM(), SMEM()] + [VMEM()] * half,
        [joined],
        flops=2 * 10**9,
    )(place, smooth, *blocks)

    swap = [(i, (i + half) % row_count) for i in range(row_count)]
    last, state = lax.optimization_barrier((last, state))
    came = lax.ppermute(last, "row", swap)
    late, _ = call(
        functools.partial(across_kernel, True),
        halves,
        [SMEM(), SMEM(), VMEM(), VMEM()],
        identity,
        flops=10**10,
    )(place, smooth, cost, state)

    return call(
        second_vertical_kernel,
        jax.ShapeDtypeStruct((rows, width, DISPARITIES), f32),
        [SMEM(), SMEM()] + [VMEM()] * (half + 4),
        [pltpu.VMEM((rows, DISPARITIES, width), f32), joined],
        flops=3 * 10**9,
    )(place, smooth, *blocks, kept, came, early, late)


def solution(mesh):
    return jax.shard_map(
        per_device,
        mesh=mesh,
        in_specs=(P(None, "row", None, "col"), P(), P(), P("row", "col"), P("row", "col"), P()),
        out_specs=P("row", "col", None),
        check_vma=False,
    )
```

```python
import functools

import jax
import jax.numpy as jnp
from jax import lax
from jax.experimental import pallas as pl
from jax.experimental.pallas import tpu as pltpu
from jax.sharding import PartitionSpec as P

DISPARITIES = 128
OFF_MOST = 256
SUB = 8
REGS = DISPARITIES // SUB
MEBI = 1024 * 1024


def lane_to_disparity(lane):
    return (lane % SUB) * REGS + lane // SUB


def disparity_to_lane(disparity):
    return (disparity % REGS) * SUB + disparity // REGS


def least_of(values):
    while len(values) > 1:
        values = [jnp.minimum(a, b) for a, b in zip(values[::2], values[1::2])]
    turned = values + [pltpu.roll(values[0], turn, 0) for turn in range(1, SUB)]
    while len(turned) > 1:
        turned = [jnp.minimum(a, b) for a, b in zip(turned[::2], turned[1::2])]
    return turned[0]


def stepped(state, p1):
    row = lax.broadcasted_iota(jnp.int32, state[0].shape, 0)
    below = jnp.where(row == 0, jnp.inf, pltpu.roll(state[-1], 1, 0))
    above = jnp.where(row == SUB - 1, jnp.inf, pltpu.roll(state[0], SUB - 1, 0))
    lower = [below] + state[:-1]
    upper = state[1:] + [above]
    return [
        jnp.minimum(s, jnp.minimum(l, u) + p1) for s, l, u in zip(state, lower, upper)
    ]


def advance(state, cost, p1, p2):
    least = least_of(state)
    return [c + jnp.minimum(t - least, p2) for t, c in zip(stepped(state, p1), cost)]


def charges(charge_ref):
    return (
        charge_ref[0].astype(jnp.float32) * (1.0 / 64.0),
        charge_ref[1].astype(jnp.float32) * (1.0 / 64.0),
    )


def registers(array):
    return [array[SUB * v : SUB * (v + 1)] for v in range(REGS)]


def convolved(taps, window, bias):
    channels, cols = bias.shape[0], window.shape[1]
    column = lax.broadcasted_iota(jnp.int32, (1, cols), 1)
    by_tap = jnp.dot(taps, window, preferred_element_type=jnp.float32)
    before = pltpu.roll(by_tap[:channels], 1, 1)
    after = pltpu.roll(by_tap[2 * channels :], cols - 1, 1)
    z = by_tap[channels : 2 * channels] + jnp.where(column == 0, 0.0, before)
    return z + jnp.where(column == cols - 1, 0.0, after) + bias


def grouping(steps):
    return max(k for k in range(1, 6) if steps % k == 0)


def stage_kernel(filter_ref, bias_ref, tile_ref, taps_ref, shift_ref, tile_out):
    layers, _, _, channels, _ = filter_ref.shape
    one = lax.broadcasted_iota(jnp.int32, (channels, channels), 0)
    two = lax.broadcasted_iota(jnp.int32, (channels, channels), 1)
    for layer in range(layers):
        for a in range(3):
            for b in range(3):
                taps_ref[
                    layer, b * channels : (b + 1) * channels, a * channels : (a + 1) * channels
                ] = filter_ref[layer, a, b]
        spread_out = jnp.where(one == two, bias_ref[layer : layer + 1, :], 0.0)
        shift_ref[layer] = jnp.sum(spread_out, axis=1, keepdims=True)
    tile_out[...] = tile_ref[...]


def inner_kernel(masks, place_ref, taps_ref, shift_ref, *refs):
    parts = len(masks)
    tile_refs, (own_ref, *hidden_refs) = refs[:parts], refs[parts:]
    channels, width = tile_refs[0].shape[1:]
    rows = tile_refs[0].shape[0] // 2
    own = place_ref[2]
    for image in range(2):
        for mask, tile_ref in zip(masks, tile_refs):
            there = pl.ds(pl.multiple_of((own ^ mask) * width, width), width)
            for row in range(rows):
                own_ref[image, row * channels : (row + 1) * channels, there] = tile_ref[
                    image * rows + row
                ]
        source = own_ref
        for layer, target in enumerate(hidden_refs):
            steps = rows - 2 * (layer + 1)

            @pl.loop(0, steps, unroll=grouping(steps))
            def _(row):
                start = pl.multiple_of(row * channels, channels)
                window = source[image, pl.ds(start, 3 * channels), :]
                z = convolved(taps_ref[layer], window, shift_ref[layer])
                target[image, pl.ds(start, channels), :] = jnp.maximum(z, 0.0).astype(jnp.bfloat16)

            source = target


def band_kernel(masks, place_ref, taps_ref, bias_ref, rows_ref, *refs):
    layers = taps_ref.shape[0]
    parts = len(masks)
    inner_refs, refs = (rows_ref, *refs[: layers - 1]), refs[layers - 1 :]
    edge_refs, refs = refs[:parts], refs[parts:]
    cost_ref, own_ref, left_unit, right_unit, present, shifts, *maps = refs
    _, channels, width = edge_refs[0].shape
    rows = own_ref.shape[0]
    cols = parts * width
    first_row = place_ref[0] * rows
    rows_total = place_ref[1] * rows
    own = place_ref[2]
    lead = (OFF_MOST + 2 * width - 1) // width * width

    for mask, edge_ref in zip(masks, edge_refs):
        member = own ^ mask
        extra = edge_ref[4 * layers].astype(jnp.float32)
        present[:, pl.ds(pl.multiple_of(member * width, width), width)] = extra[0:16]
        shifts[member] = extra[16:24]
    right_unit[:, 0:lead] = jnp.zeros((rows * channels, lead), jnp.bfloat16)
    right_unit[:, lead + cols :] = jnp.zeros((rows * channels, width), jnp.bfloat16)

    for image in range(2):
        for inner_ref, held in zip(inner_refs, maps):
            held[layers * channels : held.shape[0] - layers * channels, :] = inner_ref[image]
        for mask, edge_ref in zip(masks, edge_refs):
            there = pl.ds(pl.multiple_of((own ^ mask) * width, width), width)
            for row in range(layers):
                above, below = row * channels, (layers + rows + row) * channels
                maps[0][above : above + channels, there] = edge_ref[image * layers + row]
                maps[0][below : below + channels, there] = edge_ref[(2 + image) * layers + row]

        for layer in range(layers):
            margin = layers - 1 - layer
            last = layer == layers - 1
            skipped = 0 if last else rows - 2 * (layer + 1)
            steps = rows + 2 * margin - skipped

            @pl.loop(0, steps, unroll=grouping(steps))
            def _(row):
                if not last:
                    row = jnp.where(row < layers, row, row + skipped)
                start = pl.multiple_of(row * channels, channels)
                window = maps[layer][pl.ds(start, 3 * channels), :]
                z = convolved(taps_ref[layer], window, bias_ref[layer])
                if not last:
                    there = first_row - margin + row
                    inside = jnp.logical_and(there >= 0, there < rows_total)
                    z = jnp.maximum(z, 0.0) * jnp.where(inside, 1.0, 0.0)
                    maps[layer + 1][pl.ds(start, channels), :] = z.astype(jnp.bfloat16)
                else:
                    scale = lax.rsqrt(jnp.sum(z * z, axis=0, keepdims=True) + 1e-06)
                    unit = (z * scale).astype(jnp.bfloat16)
                    if image == 0:
                        seen = present[pl.ds(row, 1), :]
                        unit = jnp.where(seen > 0.5, unit.astype(jnp.float32), 0.0)
                        left_unit[pl.ds(start, channels), :] = unit.astype(jnp.bfloat16)
                    else:
                        right_unit[pl.ds(start, channels), lead : lead + cols] = unit

    lane = lax.broadcasted_iota(jnp.int32, (width, DISPARITIES), 1)
    place = lax.broadcasted_iota(jnp.int32, (width, DISPARITIES), 0)

    @pl.loop(0, parts)
    def _(p):
        shift = jnp.max(shifts[p]).astype(jnp.int32)
        base = p * width - shift + lead
        block = base // width
        ahead = place + (base - block * width)
        index = (ahead - lane_to_disparity(lane)) & (DISPARITIES - 1)
        start = pl.multiple_of((block - 1) * width, width)
        here = pl.multiple_of(p * width, width)

        def tile_costs(mine):
            for y in range(rows):
                left = left_unit[y * channels : (y + 1) * channels, pl.ds(here, width)]
                right = right_unit[y * channels : (y + 1) * channels, pl.ds(start, 3 * width)]
                product = lax.dot_general(
                    left, right, (((0,), (0,)), ((), ())), preferred_element_type=jnp.float32
                )
                chosen = jnp.where(lane <= ahead, product[:, width : 2 * width], product[:, :width])
                chosen = jnp.where(lane <= ahead - width, product[:, 2 * width :], chosen)
                chosen = jnp.take_along_axis(chosen, index, axis=1, mode="promise_in_bounds")
                chosen = 1.0 - chosen
                cost_ref[pl.ds(here, width), y, :] = chosen
                if mine:
                    own_ref[y] = chosen.T.astype(jnp.bfloat16)

        pl.when(p == own)(functools.partial(tile_costs, True))
        pl.when(p != own)(functools.partial(tile_costs, False))


def across_kernel(second, place_ref, charge_ref, cost_ref, *refs):
    kept_ref, last_ref, same_ref = refs[-3:]
    cols = cost_ref.shape[0]
    width, rows, _ = kept_ref.shape
    parts = cols // width
    own = place_ref[2]
    p1, p2 = charges(charge_ref)

    place = lax.broadcasted_iota(jnp.int32, (DISPARITIES, 2 * DISPARITIES), 0)
    other = lax.broadcasted_iota(jnp.int32, (DISPARITIES, 2 * DISPARITIES), 1)
    same_ref[...] = jnp.where(place == other % DISPARITIES, 1.0, 0.0).astype(jnp.bfloat16)
    same = same_ref[...]

    def cost_at(step):
        step = jnp.minimum(step, cols - 1)
        pair = jnp.concatenate([cost_ref[step], cost_ref[cols - 1 - step]], axis=0)
        coarse = pair.astype(jnp.bfloat16)
        fine = (pair - coarse.astype(jnp.float32)).astype(jnp.bfloat16)
        return registers(
            lax.dot_general(
                same,
                jnp.concatenate([coarse, fine], axis=1),
                (((1,), (1,)), ((), ())),
                preferred_element_type=jnp.float32,
            )
        )

    def segment(p, state):
        first_step = p * width

        def run(keep_right, keep_left, state):
            def body(i, carry):
                sums, cost = carry
                ahead = cost_at(first_step + i + 1)
                fresh = advance(list(sums), list(cost), p1, p2)
                if keep_right or keep_left:
                    back = jnp.concatenate(fresh, axis=0).T
                if keep_right:
                    kept_ref[i] = back[0:rows]
                if keep_left:
                    kept_ref[width - 1 - i] = back[rows : 2 * rows]
                return tuple(fresh), tuple(ahead)

            carry = (state, tuple(cost_at(first_step)))
            return lax.fori_loop(0, width, body, carry, unroll=16)[0]

        choice = jnp.where(p == own, 1, 0) + jnp.where(parts - 1 - p == own, 2, 0)
        return lax.switch(
            choice,
            [functools.partial(run, k == 1, k == 2) for k in range(3)],
            state,
        )

    if second:
        state = tuple(registers(refs[0][...]))
        span = (parts // 2, parts)
    else:
        state = tuple(jnp.zeros((SUB, 2 * rows), jnp.float32) for _ in range(REGS))
        span = (0, parts // 2)
    last_ref[...] = jnp.concatenate(lax.fori_loop(*span, segment, state), axis=0)


def down_or_up(forward, first_own, cost_ref, state, p1, p2, keep):
    group, rows = cost_ref.shape[:2]

    def block(b, state):
        member = jnp.where(forward, b, group - 1 - b)

        def run(kept, state):
            for i in range(rows):
                inner = jnp.where(forward, i, rows - 1 - i)
                cost = cost_ref[member, inner].astype(jnp.float32)
                state = advance(list(state), registers(cost), p1, p2)
                if kept:
                    keep(inner, jnp.concatenate(state, axis=0))
            return tuple(state)

        return lax.cond(
            member == first_own,
            functools.partial(run, True),
            functools.partial(run, False),
            state,
        )

    return lax.fori_loop(0, group, block, state)


def first_vertical_kernel(place_ref, charge_ref, *refs):
    *block_refs, kept_ref, last_ref, cost_ref = refs
    p1, p2 = charges(charge_ref)
    group, _, _, width = cost_ref.shape
    for k, block_ref in enumerate(block_refs):
        cost_ref[lax.rem(place_ref[4] + group - k, group)] = block_ref[...]
    state = tuple(jnp.zeros((SUB, width), jnp.float32) for _ in range(REGS))

    def keep(row, value):
        kept_ref[row] = value

    final = down_or_up(place_ref[3] == 0, place_ref[4], cost_ref, state, p1, p2, keep)
    last_ref[...] = jnp.concatenate(final, axis=0).astype(jnp.bfloat16)


def second_vertical_kernel(place_ref, charge_ref, *refs):
    *block_refs, kept_ref, came_ref, early_ref, late_ref, out_ref, total, cost_ref = refs
    p1, p2 = charges(charge_ref)
    group = cost_ref.shape[0]
    for k, block_ref in enumerate(block_refs):
        cost_ref[lax.rem(place_ref[4] + group - k, group)] = block_ref[...]
    rows, _, width = kept_ref.shape
    state = tuple(registers(came_ref[...].astype(jnp.float32)))

    def keep(row, value):
        total[row] = value + kept_ref[row]

    down_or_up(place_ref[3] != 0, place_ref[4], cost_ref, state, p1, p2, keep)
    lane = lax.broadcasted_iota(jnp.int32, (width, DISPARITIES), 1)
    index = disparity_to_lane(lane)
    for row in range(rows):
        value = total[row].T + (early_ref[:, row, :] + late_ref[:, row, :])
        out_ref[row] = jnp.take_along_axis(value, index, axis=1, mode="promise_in_bounds")


SMEM = functools.partial(pl.BlockSpec, memory_space=pltpu.SMEM)
VMEM = functools.partial(pl.BlockSpec, memory_space=pltpu.VMEM)


def call(kernel, outs, specs, scratch=(), flops=0, vmem=20):
    return pl.pallas_call(
        kernel,
        out_shape=outs,
        in_specs=specs,
        out_specs=jax.tree.map(lambda _: VMEM(), outs),
        scratch_shapes=list(scratch),
        compiler_params=pltpu.CompilerParams(vmem_limit_bytes=vmem * MEBI),
        cost_estimate=pl.CostEstimate(flops=flops, bytes_accessed=1 << 22, transcendentals=0),
    )


def spread(block, parts, beside=()):
    masks, blocks = [0], [block]
    bit = parts // 2
    while bit:
        route = [(i, i ^ bit) for i in range(parts)]
        blocks += [lax.ppermute(held, "col", route) for held in blocks]
        masks += [mask ^ bit for mask in masks]
        if beside and bit == parts // 2:
            first, *beside = lax.optimization_barrier((blocks[1], *beside))
            blocks[1] = first
        bit //= 2
    return masks, blocks, beside


def per_device(activations, filters, biases, present, shifts, smooth):
    _, rows, channels, width = activations.shape
    layers = filters.shape[0]
    high = rows + 2 * layers
    row_rank, row_count = lax.axis_index("row"), lax.axis_size("row")
    col_rank, parts = lax.axis_index("col"), lax.axis_size("col")
    half = row_count // 2
    cols = parts * width
    place = jnp.stack(
        [row_rank, jnp.int32(row_count), col_rank, row_rank // half, row_rank % half]
    ).astype(jnp.int32)

    downward = [(i, i + 1) for i in range(row_count - 1)]
    upward = [(i + 1, i) for i in range(row_count - 1)]
    before = lax.ppermute(activations[:, rows - layers :], "row", downward)
    after = lax.ppermute(activations[:, :layers], "row", upward)
    f32, bf16 = jnp.float32, jnp.bfloat16
    tile = activations.reshape(2 * rows, channels, width)
    taps, upright, staged = call(
        stage_kernel,
        (
            jax.ShapeDtypeStruct((layers, 3 * channels, 3 * channels), bf16),
            jax.ShapeDtypeStruct((layers, channels, 1), f32),
            jax.ShapeDtypeStruct(tile.shape, bf16),
        ),
        [VMEM()] * 3,
        flops=10**8,
    )(filters, biases, tile)
    before, after, taps, upright, staged = lax.optimization_barrier(
        (before, after, taps, upright, staged)
    )
    extra = jnp.concatenate(
        [
            present.astype(jnp.bfloat16),
            jnp.zeros((16 - rows, width), jnp.bfloat16),
            jnp.broadcast_to(shifts.astype(jnp.bfloat16), (channels - 16, width)),
        ],
        axis=0,
    )
    edges = jnp.concatenate(
        [before.reshape(-1, channels, width), after.reshape(-1, channels, width), extra[None]],
        axis=0,
    )
    masks, tiles, _ = spread(tile, parts)

    lead = (OFF_MOST + 2 * width - 1) // width * width
    inner = call(
        functools.partial(inner_kernel, masks),
        tuple(
            jax.ShapeDtypeStruct((2, (rows - 2 * layer) * channels, cols), bf16)
            for layer in range(layers)
        ),
        [SMEM()] + [VMEM()] * (2 + parts),
        flops=2 * 10**9,
        vmem=32,
    )(place, taps, upright, staged, *tiles[1:])
    _, edges, inner = spread(edges, parts, inner)
    cost, own = call(
        functools.partial(band_kernel, masks),
        (
            jax.ShapeDtypeStruct((cols, rows, DISPARITIES), f32),
            jax.ShapeDtypeStruct((rows, DISPARITIES, width), bf16),
        ),
        [SMEM()] + [VMEM()] * (2 + layers + parts),
        [
            pltpu.VMEM((rows * channels, cols), bf16),
            pltpu.VMEM((rows * channels, lead + cols + width), bf16),
            pltpu.VMEM((16, cols), f32),
            pltpu.VMEM((parts, SUB, width), f32),
            *(
                pltpu.VMEM(((high - 2 * layer) * channels, cols), bf16)
                for layer in range(layers)
            ),
        ],
        flops=10**10,
        vmem=40,
    )(place, taps, upright, *inner, *edges)

    blocks = [own]
    for k in range(1, half):
        turn = [(i, i // half * half + (i + k) % half) for i in range(row_count)]
        blocks.append(lax.ppermute(own, "row", turn))

    halves = (
        jax.ShapeDtypeStruct((width, rows, DISPARITIES), f32),
        jax.ShapeDtypeStruct((DISPARITIES, 2 * rows), f32),
    )
    identity = [pltpu.VMEM((DISPARITIES, 2 * DISPARITIES), bf16)]
    early, state = call(
        functools.partial(across_kernel, False),
        halves,
        [SMEM(), SMEM(), VMEM()],
        identity,
        flops=10**10,
    )(place, smooth, cost)
    *blocks, state = lax.optimization_barrier((*blocks, state))

    joined = pltpu.VMEM((half, rows, DISPARITIES, width), bf16)
    kept, last = call(
        first_vertical_kernel,
        (
            jax.ShapeDtypeStruct((rows, DISPARITIES, width), f32),
            jax.ShapeDtypeStruct((DISPARITIES, width), bf16),
        ),
        [SMEM(), SMEM()] + [VMEM()] * half,
        [joined],
        flops=2 * 10**9,
    )(place, smooth, *blocks)

    swap = [(i, (i + half) % row_count) for i in range(row_count)]
    last, state = lax.optimization_barrier((last, state))
    came = lax.ppermute(last, "row", swap)
    late, _ = call(
        functools.partial(across_kernel, True),
        halves,
        [SMEM(), SMEM(), VMEM(), VMEM()],
        identity,
        flops=10**10,
    )(place, smooth, cost, state)

    return call(
        second_vertical_kernel,
        jax.ShapeDtypeStruct((rows, width, DISPARITIES), f32),
        [SMEM(), SMEM()] + [VMEM()] * (half + 4),
        [pltpu.VMEM((rows, DISPARITIES, width), f32), joined],
        flops=3 * 10**9,
    )(place, smooth, *blocks, kept, came, early, late)


def solution(mesh):
    return jax.shard_map(
        per_device,
        mesh=mesh,
        in_specs=(P(None, "row", None, "col"), P(), P(), P("row", "col"), P("row", "col"), P()),
        out_specs=P("row", "col", None),
        check_vma=False,
    )
```

```python
import functools

import jax
import jax.numpy as jnp
from jax import lax
from jax.experimental import pallas as pl
from jax.experimental.pallas import tpu as pltpu
from jax.sharding import PartitionSpec as P

DISPARITIES = 128
OFF_MOST = 256
SUB = 8
REGS = DISPARITIES // SUB
MEBI = 1024 * 1024


def lane_to_disparity(lane):
    return (lane % SUB) * REGS + lane // SUB


def disparity_to_lane(disparity):
    return (disparity % REGS) * SUB + disparity // REGS


def least_of(values):
    while len(values) > 1:
        values = [jnp.minimum(a, b) for a, b in zip(values[::2], values[1::2])]
    turned = values + [pltpu.roll(values[0], turn, 0) for turn in range(1, SUB)]
    while len(turned) > 1:
        turned = [jnp.minimum(a, b) for a, b in zip(turned[::2], turned[1::2])]
    return turned[0]


def stepped(state, p1):
    row = lax.broadcasted_iota(jnp.int32, state[0].shape, 0)
    below = jnp.where(row == 0, jnp.inf, pltpu.roll(state[-1], 1, 0))
    above = jnp.where(row == SUB - 1, jnp.inf, pltpu.roll(state[0], SUB - 1, 0))
    lower = [below] + state[:-1]
    upper = state[1:] + [above]
    return [
        jnp.minimum(s, jnp.minimum(l, u) + p1) for s, l, u in zip(state, lower, upper)
    ]


def advance(state, cost, p1, p2):
    least = least_of(state)
    return [c + jnp.minimum(t - least, p2) for t, c in zip(stepped(state, p1), cost)]


def charges(charge_ref):
    return (
        charge_ref[0].astype(jnp.float32) * (1.0 / 64.0),
        charge_ref[1].astype(jnp.float32) * (1.0 / 64.0),
    )


def registers(array):
    return [array[SUB * v : SUB * (v + 1)] for v in range(REGS)]


def convolved(taps, window, bias):
    channels, cols = bias.shape[0], window.shape[1]
    column = lax.broadcasted_iota(jnp.int32, (1, cols), 1)
    by_tap = jnp.dot(taps, window, preferred_element_type=jnp.float32)
    before = pltpu.roll(by_tap[:channels], 1, 1)
    after = pltpu.roll(by_tap[2 * channels :], cols - 1, 1)
    z = by_tap[channels : 2 * channels] + jnp.where(column == 0, 0.0, before)
    return z + jnp.where(column == cols - 1, 0.0, after) + bias


def grouping(steps):
    return max(k for k in range(1, 6) if steps % k == 0)


def stage_kernel(filter_ref, bias_ref, tile_ref, taps_ref, shift_ref, tile_out):
    layers, _, _, channels, _ = filter_ref.shape
    one = lax.broadcasted_iota(jnp.int32, (channels, channels), 0)
    two = lax.broadcasted_iota(jnp.int32, (channels, channels), 1)
    for layer in range(layers):
        for a in range(3):
            for b in range(3):
                taps_ref[
                    layer, b * channels : (b + 1) * channels, a * channels : (a + 1) * channels
                ] = filter_ref[layer, a, b]
        spread_out = jnp.where(one == two, bias_ref[layer : layer + 1, :], 0.0)
        shift_ref[layer] = jnp.sum(spread_out, axis=1, keepdims=True)
    tile_out[...] = tile_ref[...]


def inner_kernel(masks, place_ref, taps_ref, shift_ref, *refs):
    parts = len(masks)
    tile_refs, (own_ref, *hidden_refs) = refs[:parts], refs[parts:]
    channels, width = tile_refs[0].shape[1:]
    rows = tile_refs[0].shape[0] // 2
    own = place_ref[2]
    for image in range(2):
        for mask, tile_ref in zip(masks, tile_refs):
            there = pl.ds(pl.multiple_of((own ^ mask) * width, width), width)
            for row in range(rows):
                own_ref[image, row * channels : (row + 1) * channels, there] = tile_ref[
                    image * rows + row
                ]
        source = own_ref
        for layer, target in enumerate(hidden_refs):
            steps = rows - 2 * (layer + 1)

            @pl.loop(0, steps, unroll=grouping(steps))
            def _(row):
                start = pl.multiple_of(row * channels, channels)
                window = source[image, pl.ds(start, 3 * channels), :]
                z = convolved(taps_ref[layer], window, shift_ref[layer])
                target[image, pl.ds(start, channels), :] = jnp.maximum(z, 0.0).astype(jnp.bfloat16)

            source = target


def band_kernel(masks, place_ref, taps_ref, bias_ref, rows_ref, *refs):
    layers = taps_ref.shape[0]
    parts = len(masks)
    inner_refs, refs = (rows_ref, *refs[: layers - 1]), refs[layers - 1 :]
    edge_refs, refs = refs[:parts], refs[parts:]
    cost_ref, own_ref, left_unit, right_unit, present, shifts, *maps = refs
    _, channels, width = edge_refs[0].shape
    rows = own_ref.shape[0]
    cols = parts * width
    first_row = place_ref[0] * rows
    rows_total = place_ref[1] * rows
    own = place_ref[2]
    lead = (OFF_MOST + 2 * width - 1) // width * width

    for mask, edge_ref in zip(masks, edge_refs):
        member = own ^ mask
        extra = edge_ref[4 * layers].astype(jnp.float32)
        present[:, pl.ds(pl.multiple_of(member * width, width), width)] = extra[0:16]
        shifts[member] = extra[16:24]
    right_unit[:, 0:lead] = jnp.zeros((rows * channels, lead), jnp.bfloat16)
    right_unit[:, lead + cols :] = jnp.zeros((rows * channels, width), jnp.bfloat16)

    for image in range(2):
        for inner_ref, held in zip(inner_refs, maps):
            held[layers * channels : held.shape[0] - layers * channels, :] = inner_ref[image]
        for mask, edge_ref in zip(masks, edge_refs):
            there = pl.ds(pl.multiple_of((own ^ mask) * width, width), width)
            for row in range(layers):
                above, below = row * channels, (layers + rows + row) * channels
                maps[0][above : above + channels, there] = edge_ref[image * layers + row]
                maps[0][below : below + channels, there] = edge_ref[(2 + image) * layers + row]

        for layer in range(layers):
            margin = layers - 1 - layer
            last = layer == layers - 1
            skipped = 0 if last else rows - 2 * (layer + 1)
            steps = rows + 2 * margin - skipped

            @pl.loop(0, steps, unroll=grouping(steps))
            def _(row):
                if not last:
                    row = jnp.where(row < layers, row, row + skipped)
                start = pl.multiple_of(row * channels, channels)
                window = maps[layer][pl.ds(start, 3 * channels), :]
                z = convolved(taps_ref[layer], window, bias_ref[layer])
                if not last:
                    there = first_row - margin + row
                    inside = jnp.logical_and(there >= 0, there < rows_total)
                    z = jnp.maximum(z, 0.0) * jnp.where(inside, 1.0, 0.0)
                    maps[layer + 1][pl.ds(start, channels), :] = z.astype(jnp.bfloat16)
                else:
                    scale = lax.rsqrt(jnp.sum(z * z, axis=0, keepdims=True) + 1e-06)
                    unit = (z * scale).astype(jnp.bfloat16)
                    if image == 0:
                        seen = present[pl.ds(row, 1), :]
                        unit = jnp.where(seen > 0.5, unit.astype(jnp.float32), 0.0)
                        left_unit[pl.ds(start, channels), :] = unit.astype(jnp.bfloat16)
                    else:
                        right_unit[pl.ds(start, channels), lead : lead + cols] = unit

    lane = lax.broadcasted_iota(jnp.int32, (width, DISPARITIES), 1)
    place = lax.broadcasted_iota(jnp.int32, (width, DISPARITIES), 0)

    @pl.loop(0, parts)
    def _(p):
        shift = jnp.max(shifts[p]).astype(jnp.int32)
        base = p * width - shift + lead
        block = base // width
        ahead = place + (base - block * width)
        index = (ahead - lane_to_disparity(lane)) & (DISPARITIES - 1)
        start = pl.multiple_of((block - 1) * width, width)
        here = pl.multiple_of(p * width, width)

        def tile_costs(mine):
            for y in range(rows):
                left = left_unit[y * channels : (y + 1) * channels, pl.ds(here, width)]
                right = right_unit[y * channels : (y + 1) * channels, pl.ds(start, 3 * width)]
                product = lax.dot_general(
                    left, right, (((0,), (0,)), ((), ())), preferred_element_type=jnp.float32
                )
                chosen = jnp.where(lane <= ahead, product[:, width : 2 * width], product[:, :width])
                chosen = jnp.where(lane <= ahead - width, product[:, 2 * width :], chosen)
                chosen = jnp.take_along_axis(chosen, index, axis=1, mode="promise_in_bounds")
                chosen = 1.0 - chosen
                cost_ref[pl.ds(here, width), y, :] = chosen
                if mine:
                    own_ref[y] = chosen.T.astype(jnp.bfloat16)

        pl.when(p == own)(functools.partial(tile_costs, True))
        pl.when(p != own)(functools.partial(tile_costs, False))


def early_segments(parts):
    return parts - parts // 4


def across_kernel(second, place_ref, charge_ref, cost_ref, *refs):
    kept_ref, last_ref, same_ref = refs[-3:]
    cols = cost_ref.shape[0]
    _, width, rows, _ = kept_ref.shape
    parts = cols // width
    early = early_segments(parts)
    own = place_ref[2]
    p1, p2 = charges(charge_ref)

    place = lax.broadcasted_iota(jnp.int32, (DISPARITIES, 2 * DISPARITIES), 0)
    other = lax.broadcasted_iota(jnp.int32, (DISPARITIES, 2 * DISPARITIES), 1)
    same_ref[...] = jnp.where(place == other % DISPARITIES, 1.0, 0.0).astype(jnp.bfloat16)
    same = same_ref[...]

    def cost_at(step):
        step = jnp.minimum(step, cols - 1)
        pair = jnp.concatenate([cost_ref[step], cost_ref[cols - 1 - step]], axis=0)
        coarse = pair.astype(jnp.bfloat16)
        fine = (pair - coarse.astype(jnp.float32)).astype(jnp.bfloat16)
        return registers(
            lax.dot_general(
                same,
                jnp.concatenate([coarse, fine], axis=1),
                (((1,), (1,)), ((), ())),
                preferred_element_type=jnp.float32,
            )
        )

    def segment(p, state):
        first_step = p * width

        def run(keep_right, keep_left, state):
            def body(i, carry):
                sums, cost = carry
                ahead = cost_at(first_step + i + 1)
                least = least_of(list(sums))
                jump = least + p2
                fresh = [
                    c + jnp.minimum(t, jump) for t, c in zip(stepped(list(sums), p1), cost)
                ]
                if keep_right or keep_left:
                    back = jnp.concatenate([f - least for f in fresh], axis=0).T
                if keep_right:
                    kept_ref[0, i] = back[0:rows]
                if keep_left:
                    kept_ref[1, width - 1 - i] = back[rows : 2 * rows]
                return tuple(fresh), tuple(ahead)

            carry = (state, tuple(cost_at(first_step)))
            sums = lax.fori_loop(0, width, body, carry, unroll=16)[0]
            least = least_of(list(sums))
            return tuple(s - least for s in sums)

        choice = jnp.where(p == own, 1, 0) + jnp.where(parts - 1 - p == own, 2, 0)
        return lax.switch(
            choice,
            [functools.partial(run, k == 1, k == 2) for k in range(3)],
            state,
        )

    if second:
        state = tuple(registers(refs[0][...]))
        span = (early, parts)
    else:
        state = tuple(jnp.zeros((SUB, 2 * rows), jnp.float32) for _ in range(REGS))
        span = (0, early)
    last_ref[...] = jnp.concatenate(lax.fori_loop(*span, segment, state), axis=0)


def down_or_up(forward, first_own, cost_ref, state, p1, p2, keep):
    group, rows = cost_ref.shape[:2]

    def block(b, state):
        member = jnp.where(forward, b, group - 1 - b)

        def run(kept, state):
            for i in range(rows):
                inner = jnp.where(forward, i, rows - 1 - i)
                cost = cost_ref[member, inner].astype(jnp.float32)
                state = advance(list(state), registers(cost), p1, p2)
                if kept:
                    keep(inner, jnp.concatenate(state, axis=0))
            return tuple(state)

        return lax.cond(
            member == first_own,
            functools.partial(run, True),
            functools.partial(run, False),
            state,
        )

    return lax.fori_loop(0, group, block, state)


def first_vertical_kernel(place_ref, charge_ref, *refs):
    *block_refs, kept_ref, last_ref, cost_ref = refs
    p1, p2 = charges(charge_ref)
    group, _, _, width = cost_ref.shape
    for k, block_ref in enumerate(block_refs):
        cost_ref[lax.rem(place_ref[4] + group - k, group)] = block_ref[...]
    state = tuple(jnp.zeros((SUB, width), jnp.float32) for _ in range(REGS))

    def keep(row, value):
        kept_ref[row] = value

    final = down_or_up(place_ref[3] == 0, place_ref[4], cost_ref, state, p1, p2, keep)
    last_ref[...] = jnp.concatenate(final, axis=0).astype(jnp.bfloat16)


def second_vertical_kernel(place_ref, charge_ref, *refs):
    *block_refs, kept_ref, came_ref, early_ref, late_ref, out_ref, total, cost_ref = refs
    p1, p2 = charges(charge_ref)
    group = cost_ref.shape[0]
    for k, block_ref in enumerate(block_refs):
        cost_ref[lax.rem(place_ref[4] + group - k, group)] = block_ref[...]
    rows, _, width = kept_ref.shape
    state = tuple(registers(came_ref[...].astype(jnp.float32)))

    def keep(row, value):
        total[row] = value + kept_ref[row]

    down_or_up(place_ref[3] != 0, place_ref[4], cost_ref, state, p1, p2, keep)
    lane = lax.broadcasted_iota(jnp.int32, (width, DISPARITIES), 1)
    index = disparity_to_lane(lane)
    right_early = place_ref[2] < place_ref[6]
    left_early = place_ref[5] - 1 - place_ref[2] < place_ref[6]
    for row in range(rows):
        right = jnp.where(right_early, early_ref[0, :, row, :], late_ref[0, :, row, :])
        left = jnp.where(left_early, early_ref[1, :, row, :], late_ref[1, :, row, :])
        value = total[row].T + (right + left)
        out_ref[row] = jnp.take_along_axis(value, index, axis=1, mode="promise_in_bounds")


SMEM = functools.partial(pl.BlockSpec, memory_space=pltpu.SMEM)
VMEM = functools.partial(pl.BlockSpec, memory_space=pltpu.VMEM)


def call(kernel, outs, specs, scratch=(), flops=0, vmem=20):
    return pl.pallas_call(
        kernel,
        out_shape=outs,
        in_specs=specs,
        out_specs=jax.tree.map(lambda _: VMEM(), outs),
        scratch_shapes=list(scratch),
        compiler_params=pltpu.CompilerParams(vmem_limit_bytes=vmem * MEBI),
        cost_estimate=pl.CostEstimate(flops=flops, bytes_accessed=1 << 22, transcendentals=0),
    )


def spread(block, parts, beside=()):
    masks, blocks = [0], [block]
    bit = parts // 2
    while bit:
        route = [(i, i ^ bit) for i in range(parts)]
        blocks += [lax.ppermute(held, "col", route) for held in blocks]
        masks += [mask ^ bit for mask in masks]
        if beside and bit == parts // 2:
            first, *beside = lax.optimization_barrier((blocks[1], *beside))
            blocks[1] = first
        bit //= 2
    return masks, blocks, beside


def per_device(activations, filters, biases, present, shifts, smooth):
    _, rows, channels, width = activations.shape
    layers = filters.shape[0]
    high = rows + 2 * layers
    row_rank, row_count = lax.axis_index("row"), lax.axis_size("row")
    col_rank, parts = lax.axis_index("col"), lax.axis_size("col")
    half = row_count // 2
    cols = parts * width
    place = jnp.stack(
        [
            row_rank,
            jnp.int32(row_count),
            col_rank,
            row_rank // half,
            row_rank % half,
            jnp.int32(parts),
            jnp.int32(early_segments(parts)),
        ]
    ).astype(jnp.int32)

    downward = [(i, i + 1) for i in range(row_count - 1)]
    upward = [(i + 1, i) for i in range(row_count - 1)]
    before = lax.ppermute(activations[:, rows - layers :], "row", downward)
    after = lax.ppermute(activations[:, :layers], "row", upward)
    f32, bf16 = jnp.float32, jnp.bfloat16
    tile = activations.reshape(2 * rows, channels, width)
    taps, upright, staged = call(
        stage_kernel,
        (
            jax.ShapeDtypeStruct((layers, 3 * channels, 3 * channels), bf16),
            jax.ShapeDtypeStruct((layers, channels, 1), f32),
            jax.ShapeDtypeStruct(tile.shape, bf16),
        ),
        [VMEM()] * 3,
        flops=10**8,
    )(filters, biases, tile)
    before, after, taps, upright, staged = lax.optimization_barrier(
        (before, after, taps, upright, staged)
    )
    extra = jnp.concatenate(
        [
            present.astype(jnp.bfloat16),
            jnp.zeros((16 - rows, width), jnp.bfloat16),
            jnp.broadcast_to(shifts.astype(jnp.bfloat16), (channels - 16, width)),
        ],
        axis=0,
    )
    edges = jnp.concatenate(
        [before.reshape(-1, channels, width), after.reshape(-1, channels, width), extra[None]],
        axis=0,
    )
    masks, tiles, _ = spread(tile, parts)

    lead = (OFF_MOST + 2 * width - 1) // width * width
    inner = call(
        functools.partial(inner_kernel, masks),
        tuple(
            jax.ShapeDtypeStruct((2, (rows - 2 * layer) * channels, cols), bf16)
            for layer in range(layers)
        ),
        [SMEM()] + [VMEM()] * (2 + parts),
        flops=2 * 10**9,
        vmem=32,
    )(place, taps, upright, staged, *tiles[1:])
    _, edges, inner = spread(edges, parts, inner)
    cost, own = call(
        functools.partial(band_kernel, masks),
        (
            jax.ShapeDtypeStruct((cols, rows, DISPARITIES), f32),
            jax.ShapeDtypeStruct((rows, DISPARITIES, width), bf16),
        ),
        [SMEM()] + [VMEM()] * (2 + layers + parts),
        [
            pltpu.VMEM((rows * channels, cols), bf16),
            pltpu.VMEM((rows * channels, lead + cols + width), bf16),
            pltpu.VMEM((16, cols), f32),
            pltpu.VMEM((parts, SUB, width), f32),
            *(
                pltpu.VMEM(((high - 2 * layer) * channels, cols), bf16)
                for layer in range(layers)
            ),
        ],
        flops=10**10,
        vmem=40,
    )(place, taps, upright, *inner, *edges)

    blocks = [own]
    for k in range(1, half):
        turn = [(i, i // half * half + (i + k) % half) for i in range(row_count)]
        blocks.append(lax.ppermute(own, "row", turn))

    halves = (
        jax.ShapeDtypeStruct((2, width, rows, DISPARITIES), f32),
        jax.ShapeDtypeStruct((DISPARITIES, 2 * rows), f32),
    )
    identity = [pltpu.VMEM((DISPARITIES, 2 * DISPARITIES), bf16)]
    early, state = call(
        functools.partial(across_kernel, False),
        halves,
        [SMEM(), SMEM(), VMEM()],
        identity,
        flops=10**10,
    )(place, smooth, cost)
    *blocks, state = lax.optimization_barrier((*blocks, state))

    joined = pltpu.VMEM((half, rows, DISPARITIES, width), bf16)
    kept, last = call(
        first_vertical_kernel,
        (
            jax.ShapeDtypeStruct((rows, DISPARITIES, width), f32),
            jax.ShapeDtypeStruct((DISPARITIES, width), bf16),
        ),
        [SMEM(), SMEM()] + [VMEM()] * half,
        [joined],
        flops=2 * 10**9,
    )(place, smooth, *blocks)

    swap = [(i, (i + half) % row_count) for i in range(row_count)]
    last, state = lax.optimization_barrier((last, state))
    came = lax.ppermute(last, "row", swap)
    late, _ = call(
        functools.partial(across_kernel, True),
        halves,
        [SMEM(), SMEM(), VMEM(), VMEM()],
        identity,
        flops=10**10,
    )(place, smooth, cost, state)

    return call(
        second_vertical_kernel,
        jax.ShapeDtypeStruct((rows, width, DISPARITIES), f32),
        [SMEM(), SMEM()] + [VMEM()] * (half + 4),
        [pltpu.VMEM((rows, DISPARITIES, width), f32), joined],
        flops=3 * 10**9,
    )(place, smooth, *blocks, kept, came, early, late)


def solution(mesh):
    return jax.shard_map(
        per_device,
        mesh=mesh,
        in_specs=(P(None, "row", None, "col"), P(), P(), P("row", "col"), P("row", "col"), P()),
        out_specs=P("row", "col", None),
        check_vma=False,
    )
```

```python
import functools

import jax
import jax.numpy as jnp
from jax import lax
from jax.experimental import pallas as pl
from jax.experimental.pallas import tpu as pltpu
from jax.sharding import PartitionSpec as P

DISPARITIES = 128
OFF_MOST = 256
SUB = 8
REGS = DISPARITIES // SUB
MEBI = 1024 * 1024


def lane_to_disparity(lane):
    return (lane % SUB) * REGS + lane // SUB


def disparity_to_lane(disparity):
    return (disparity % REGS) * SUB + disparity // REGS


def least_of(values):
    while len(values) > 1:
        values = [jnp.minimum(a, b) for a, b in zip(values[::2], values[1::2])]
    turned = values + [pltpu.roll(values[0], turn, 0) for turn in range(1, SUB)]
    while len(turned) > 1:
        turned = [jnp.minimum(a, b) for a, b in zip(turned[::2], turned[1::2])]
    return turned[0]


def stepped(state, p1):
    row = lax.broadcasted_iota(jnp.int32, state[0].shape, 0)
    below = jnp.where(row == 0, jnp.inf, pltpu.roll(state[-1], 1, 0))
    above = jnp.where(row == SUB - 1, jnp.inf, pltpu.roll(state[0], SUB - 1, 0))
    lower = [below] + state[:-1]
    upper = state[1:] + [above]
    return [
        jnp.minimum(s, jnp.minimum(l, u) + p1) for s, l, u in zip(state, lower, upper)
    ]


def advance(state, cost, p1, p2):
    least = least_of(state)
    return [c + jnp.minimum(t - least, p2) for t, c in zip(stepped(state, p1), cost)]


def charges(charge_ref):
    return (
        charge_ref[0].astype(jnp.float32) * (1.0 / 64.0),
        charge_ref[1].astype(jnp.float32) * (1.0 / 64.0),
    )


def registers(array):
    return [array[SUB * v : SUB * (v + 1)] for v in range(REGS)]


def convolved(taps, window, bias):
    channels, cols = bias.shape[0], window.shape[1]
    column = lax.broadcasted_iota(jnp.int32, (1, cols), 1)
    by_tap = jnp.dot(taps, window, preferred_element_type=jnp.float32)
    before = pltpu.roll(by_tap[:channels], 1, 1)
    after = pltpu.roll(by_tap[2 * channels :], cols - 1, 1)
    z = by_tap[channels : 2 * channels] + jnp.where(column == 0, 0.0, before)
    return z + jnp.where(column == cols - 1, 0.0, after) + bias


def grouping(steps):
    return max(k for k in range(1, 6) if steps % k == 0)


def stage_kernel(filter_ref, bias_ref, tile_ref, taps_ref, shift_ref, tile_out):
    layers, _, _, channels, _ = filter_ref.shape
    one = lax.broadcasted_iota(jnp.int32, (channels, channels), 0)
    two = lax.broadcasted_iota(jnp.int32, (channels, channels), 1)
    for layer in range(layers):
        for a in range(3):
            for b in range(3):
                taps_ref[
                    layer, b * channels : (b + 1) * channels, a * channels : (a + 1) * channels
                ] = filter_ref[layer, a, b]
        spread_out = jnp.where(one == two, bias_ref[layer : layer + 1, :], 0.0)
        shift_ref[layer] = jnp.sum(spread_out, axis=1, keepdims=True)
    tile_out[...] = tile_ref[...]


def inner_kernel(masks, place_ref, taps_ref, shift_ref, *refs):
    parts = len(masks)
    tile_refs, (own_ref, *hidden_refs) = refs[:parts], refs[parts:]
    channels, width = tile_refs[0].shape[1:]
    rows = tile_refs[0].shape[0] // 2
    own = place_ref[2]
    for image in range(2):
        for mask, tile_ref in zip(masks, tile_refs):
            there = pl.ds(pl.multiple_of((own ^ mask) * width, width), width)
            for row in range(rows):
                own_ref[image, row * channels : (row + 1) * channels, there] = tile_ref[
                    image * rows + row
                ]
        source = own_ref
        for layer, target in enumerate(hidden_refs):
            steps = rows - 2 * (layer + 1)

            @pl.loop(0, steps, unroll=grouping(steps))
            def _(row):
                start = pl.multiple_of(row * channels, channels)
                window = source[image, pl.ds(start, 3 * channels), :]
                z = convolved(taps_ref[layer], window, shift_ref[layer])
                target[image, pl.ds(start, channels), :] = jnp.maximum(z, 0.0).astype(jnp.bfloat16)

            source = target


def band_kernel(masks, place_ref, taps_ref, bias_ref, rows_ref, *refs):
    layers = taps_ref.shape[0]
    parts = len(masks)
    inner_refs, refs = (rows_ref, *refs[: layers - 1]), refs[layers - 1 :]
    edge_refs, refs = refs[:parts], refs[parts:]
    cost_ref, own_ref, left_unit, right_unit, present, shifts, *maps = refs
    _, channels, width = edge_refs[0].shape
    rows = own_ref.shape[0]
    cols = parts * width
    first_row = place_ref[0] * rows
    rows_total = place_ref[1] * rows
    own = place_ref[2]
    lead = (OFF_MOST + 2 * width - 1) // width * width

    for mask, edge_ref in zip(masks, edge_refs):
        member = own ^ mask
        extra = edge_ref[4 * layers].astype(jnp.float32)
        present[:, pl.ds(pl.multiple_of(member * width, width), width)] = extra[0:16]
        shifts[member] = extra[16:24]
    right_unit[:, 0:lead] = jnp.zeros((rows * channels, lead), jnp.bfloat16)
    right_unit[:, lead + cols :] = jnp.zeros((rows * channels, width), jnp.bfloat16)

    for image in range(2):
        for inner_ref, held in zip(inner_refs, maps):
            held[layers * channels : held.shape[0] - layers * channels, :] = inner_ref[image]
        for mask, edge_ref in zip(masks, edge_refs):
            there = pl.ds(pl.multiple_of((own ^ mask) * width, width), width)
            for row in range(layers):
                above, below = row * channels, (layers + rows + row) * channels
                maps[0][above : above + channels, there] = edge_ref[image * layers + row]
                maps[0][below : below + channels, there] = edge_ref[(2 + image) * layers + row]

        for layer in range(layers):
            margin = layers - 1 - layer
            last = layer == layers - 1
            skipped = 0 if last else rows - 2 * (layer + 1)
            steps = rows + 2 * margin - skipped

            @pl.loop(0, steps, unroll=grouping(steps))
            def _(row):
                if not last:
                    row = jnp.where(row < layers, row, row + skipped)
                start = pl.multiple_of(row * channels, channels)
                window = maps[layer][pl.ds(start, 3 * channels), :]
                z = convolved(taps_ref[layer], window, bias_ref[layer])
                if not last:
                    there = first_row - margin + row
                    inside = jnp.logical_and(there >= 0, there < rows_total)
                    z = jnp.maximum(z, 0.0) * jnp.where(inside, 1.0, 0.0)
                    maps[layer + 1][pl.ds(start, channels), :] = z.astype(jnp.bfloat16)
                else:
                    scale = lax.rsqrt(jnp.sum(z * z, axis=0, keepdims=True) + 1e-06)
                    unit = (z * scale).astype(jnp.bfloat16)
                    if image == 0:
                        seen = present[pl.ds(row, 1), :]
                        unit = jnp.where(seen > 0.5, unit.astype(jnp.float32), 0.0)
                        left_unit[pl.ds(start, channels), :] = unit.astype(jnp.bfloat16)
                    else:
                        right_unit[pl.ds(start, channels), lead : lead + cols] = unit

    lane = lax.broadcasted_iota(jnp.int32, (width, DISPARITIES), 1)
    place = lax.broadcasted_iota(jnp.int32, (width, DISPARITIES), 0)

    @pl.loop(0, parts)
    def _(p):
        shift = jnp.max(shifts[p]).astype(jnp.int32)
        base = p * width - shift + lead
        block = base // width
        ahead = place + (base - block * width)
        index = (ahead - lane_to_disparity(lane)) & (DISPARITIES - 1)
        start = pl.multiple_of((block - 1) * width, width)
        here = pl.multiple_of(p * width, width)

        def tile_costs(mine):
            for y in range(rows):
                left = left_unit[y * channels : (y + 1) * channels, pl.ds(here, width)]
                right = right_unit[y * channels : (y + 1) * channels, pl.ds(start, 3 * width)]
                product = lax.dot_general(
                    left, right, (((0,), (0,)), ((), ())), preferred_element_type=jnp.float32
                )
                chosen = jnp.where(lane <= ahead, product[:, width : 2 * width], product[:, :width])
                chosen = jnp.where(lane <= ahead - width, product[:, 2 * width :], chosen)
                chosen = jnp.take_along_axis(chosen, index, axis=1, mode="promise_in_bounds")
                chosen = 1.0 - chosen
                cost_ref[pl.ds(pl.multiple_of(here * rows, rows) + y, width, stride=rows), :] = chosen
                if mine:
                    own_ref[y] = chosen.T.astype(jnp.bfloat16)

        pl.when(p == own)(functools.partial(tile_costs, True))
        pl.when(p != own)(functools.partial(tile_costs, False))


def early_segments(parts):
    return parts - parts // 4


def across_kernel(second, place_ref, charge_ref, cost_ref, *refs):
    kept_ref, last_ref, same_ref = refs[-3:]
    parts = cost_ref.shape[0] // kept_ref.shape[1]
    rows = last_ref.shape[1] // 2
    width = kept_ref.shape[1] // rows
    cols = parts * width
    early = early_segments(parts)
    own = place_ref[2]
    p1, p2 = charges(charge_ref)

    place = lax.broadcasted_iota(jnp.int32, (DISPARITIES, 2 * DISPARITIES), 0)
    other = lax.broadcasted_iota(jnp.int32, (DISPARITIES, 2 * DISPARITIES), 1)
    same_ref[...] = jnp.where(place == other % DISPARITIES, 1.0, 0.0).astype(jnp.bfloat16)
    same = same_ref[...]

    def at(column):
        return pl.ds(pl.multiple_of(column * rows, rows), rows)

    def cost_at(step):
        step = jnp.minimum(step, cols - 1)
        pair = jnp.concatenate([cost_ref[at(step)], cost_ref[at(cols - 1 - step)]], axis=0)
        coarse = pair.astype(jnp.bfloat16)
        fine = (pair - coarse.astype(jnp.float32)).astype(jnp.bfloat16)
        return registers(
            lax.dot_general(
                same,
                jnp.concatenate([coarse, fine], axis=1),
                (((1,), (1,)), ((), ())),
                preferred_element_type=jnp.float32,
            )
        )

    def segment(p, state):
        first_step = p * width

        def run(keep_right, keep_left, state):
            def body(i, carry):
                sums, cost = carry
                ahead = cost_at(first_step + i + 1)
                least = least_of(list(sums))
                jump = least + p2
                fresh = [
                    c + jnp.minimum(t, jump) for t, c in zip(stepped(list(sums), p1), cost)
                ]
                if keep_right or keep_left:
                    back = jnp.concatenate([f - least for f in fresh], axis=0).T
                if keep_right:
                    kept_ref[0, at(i)] = back[0:rows]
                if keep_left:
                    kept_ref[1, at(width - 1 - i)] = back[rows : 2 * rows]
                return tuple(fresh), tuple(ahead)

            carry = (state, tuple(cost_at(first_step)))
            sums = lax.fori_loop(0, width, body, carry, unroll=16)[0]
            least = least_of(list(sums))
            return tuple(s - least for s in sums)

        choice = jnp.where(p == own, 1, 0) + jnp.where(parts - 1 - p == own, 2, 0)
        return lax.switch(
            choice,
            [functools.partial(run, k == 1, k == 2) for k in range(3)],
            state,
        )

    if second:
        state = tuple(registers(refs[0][...]))
        span = (early, parts)
    else:
        state = tuple(jnp.zeros((SUB, 2 * rows), jnp.float32) for _ in range(REGS))
        span = (0, early)
    last_ref[...] = jnp.concatenate(lax.fori_loop(*span, segment, state), axis=0)


def down_or_up(forward, first_own, cost_ref, state, p1, p2, keep):
    group, rows = cost_ref.shape[:2]

    def block(b, state):
        member = jnp.where(forward, b, group - 1 - b)

        def run(kept, state):
            for i in range(rows):
                inner = jnp.where(forward, i, rows - 1 - i)
                cost = cost_ref[member, inner].astype(jnp.float32)
                state = advance(list(state), registers(cost), p1, p2)
                if kept:
                    keep(inner, jnp.concatenate(state, axis=0))
            return tuple(state)

        return lax.cond(
            member == first_own,
            functools.partial(run, True),
            functools.partial(run, False),
            state,
        )

    return lax.fori_loop(0, group, block, state)


def first_vertical_kernel(place_ref, charge_ref, *refs):
    *block_refs, kept_ref, last_ref, cost_ref = refs
    p1, p2 = charges(charge_ref)
    group, _, _, width = cost_ref.shape
    for k, block_ref in enumerate(block_refs):
        cost_ref[lax.rem(place_ref[4] + group - k, group)] = block_ref[...]
    state = tuple(jnp.zeros((SUB, width), jnp.float32) for _ in range(REGS))

    def keep(row, value):
        kept_ref[row] = value

    final = down_or_up(place_ref[3] == 0, place_ref[4], cost_ref, state, p1, p2, keep)
    last_ref[...] = jnp.concatenate(final, axis=0).astype(jnp.bfloat16)


def second_vertical_kernel(place_ref, charge_ref, *refs):
    *block_refs, kept_ref, came_ref, early_ref, late_ref, out_ref, total, cost_ref = refs
    p1, p2 = charges(charge_ref)
    group = cost_ref.shape[0]
    for k, block_ref in enumerate(block_refs):
        cost_ref[lax.rem(place_ref[4] + group - k, group)] = block_ref[...]
    rows, _, width = kept_ref.shape
    state = tuple(registers(came_ref[...].astype(jnp.float32)))

    def keep(row, value):
        total[row] = value + kept_ref[row]

    down_or_up(place_ref[3] != 0, place_ref[4], cost_ref, state, p1, p2, keep)
    lane = lax.broadcasted_iota(jnp.int32, (width, DISPARITIES), 1)
    index = disparity_to_lane(lane)
    right_early = place_ref[2] < place_ref[6]
    left_early = place_ref[5] - 1 - place_ref[2] < place_ref[6]
    for row in range(rows):
        this = pl.ds(row, width, stride=rows)
        right = jnp.where(right_early, early_ref[0, this, :], late_ref[0, this, :])
        left = jnp.where(left_early, early_ref[1, this, :], late_ref[1, this, :])
        value = total[row].T + (right + left)
        out_ref[row] = jnp.take_along_axis(value, index, axis=1, mode="promise_in_bounds")


SMEM = functools.partial(pl.BlockSpec, memory_space=pltpu.SMEM)
VMEM = functools.partial(pl.BlockSpec, memory_space=pltpu.VMEM)


def call(kernel, outs, specs, scratch=(), flops=0, vmem=20):
    return pl.pallas_call(
        kernel,
        out_shape=outs,
        in_specs=specs,
        out_specs=jax.tree.map(lambda _: VMEM(), outs),
        scratch_shapes=list(scratch),
        compiler_params=pltpu.CompilerParams(vmem_limit_bytes=vmem * MEBI),
        cost_estimate=pl.CostEstimate(flops=flops, bytes_accessed=1 << 22, transcendentals=0),
    )


def spread(block, parts, beside=()):
    masks, blocks = [0], [block]
    bit = parts // 2
    while bit:
        route = [(i, i ^ bit) for i in range(parts)]
        blocks += [lax.ppermute(held, "col", route) for held in blocks]
        masks += [mask ^ bit for mask in masks]
        if beside and bit == parts // 2:
            first, *beside = lax.optimization_barrier((blocks[1], *beside))
            blocks[1] = first
        bit //= 2
    return masks, blocks, beside


def per_device(activations, filters, biases, present, shifts, smooth):
    _, rows, channels, width = activations.shape
    layers = filters.shape[0]
    high = rows + 2 * layers
    row_rank, row_count = lax.axis_index("row"), lax.axis_size("row")
    col_rank, parts = lax.axis_index("col"), lax.axis_size("col")
    half = row_count // 2
    cols = parts * width
    place = jnp.stack(
        [
            row_rank,
            jnp.int32(row_count),
            col_rank,
            row_rank // half,
            row_rank % half,
            jnp.int32(parts),
            jnp.int32(early_segments(parts)),
        ]
    ).astype(jnp.int32)

    downward = [(i, i + 1) for i in range(row_count - 1)]
    upward = [(i + 1, i) for i in range(row_count - 1)]
    before = lax.ppermute(activations[:, rows - layers :], "row", downward)
    after = lax.ppermute(activations[:, :layers], "row", upward)
    f32, bf16 = jnp.float32, jnp.bfloat16
    tile = activations.reshape(2 * rows, channels, width)
    taps, upright, staged = call(
        stage_kernel,
        (
            jax.ShapeDtypeStruct((layers, 3 * channels, 3 * channels), bf16),
            jax.ShapeDtypeStruct((layers, channels, 1), f32),
            jax.ShapeDtypeStruct(tile.shape, bf16),
        ),
        [VMEM()] * 3,
        flops=10**8,
    )(filters, biases, tile)
    before, after, taps, upright, staged = lax.optimization_barrier(
        (before, after, taps, upright, staged)
    )
    extra = jnp.concatenate(
        [
            present.astype(jnp.bfloat16),
            jnp.zeros((16 - rows, width), jnp.bfloat16),
            jnp.broadcast_to(shifts.astype(jnp.bfloat16), (channels - 16, width)),
        ],
        axis=0,
    )
    edges = jnp.concatenate(
        [before.reshape(-1, channels, width), after.reshape(-1, channels, width), extra[None]],
        axis=0,
    )
    masks, tiles, _ = spread(tile, parts)

    lead = (OFF_MOST + 2 * width - 1) // width * width
    inner = call(
        functools.partial(inner_kernel, masks),
        tuple(
            jax.ShapeDtypeStruct((2, (rows - 2 * layer) * channels, cols), bf16)
            for layer in range(layers)
        ),
        [SMEM()] + [VMEM()] * (2 + parts),
        flops=2 * 10**9,
        vmem=32,
    )(place, taps, upright, staged, *tiles[1:])
    _, edges, inner = spread(edges, parts, inner)
    cost, own = call(
        functools.partial(band_kernel, masks),
        (
            jax.ShapeDtypeStruct((cols * rows, DISPARITIES), f32),
            jax.ShapeDtypeStruct((rows, DISPARITIES, width), bf16),
        ),
        [SMEM()] + [VMEM()] * (2 + layers + parts),
        [
            pltpu.VMEM((rows * channels, cols), bf16),
            pltpu.VMEM((rows * channels, lead + cols + width), bf16),
            pltpu.VMEM((16, cols), f32),
            pltpu.VMEM((parts, SUB, width), f32),
            *(
                pltpu.VMEM(((high - 2 * layer) * channels, cols), bf16)
                for layer in range(layers)
            ),
        ],
        flops=10**10,
        vmem=40,
    )(place, taps, upright, *inner, *edges)

    blocks = [own]
    for k in range(1, half):
        turn = [(i, i // half * half + (i + k) % half) for i in range(row_count)]
        blocks.append(lax.ppermute(own, "row", turn))

    halves = (
        jax.ShapeDtypeStruct((2, width * rows, DISPARITIES), f32),
        jax.ShapeDtypeStruct((DISPARITIES, 2 * rows), f32),
    )
    identity = [pltpu.VMEM((DISPARITIES, 2 * DISPARITIES), bf16)]
    early, state = call(
        functools.partial(across_kernel, False),
        halves,
        [SMEM(), SMEM(), VMEM()],
        identity,
        flops=10**10,
    )(place, smooth, cost)
    *blocks, state = lax.optimization_barrier((*blocks, state))

    joined = pltpu.VMEM((half, rows, DISPARITIES, width), bf16)
    kept, last = call(
        first_vertical_kernel,
        (
            jax.ShapeDtypeStruct((rows, DISPARITIES, width), f32),
            jax.ShapeDtypeStruct((DISPARITIES, width), bf16),
        ),
        [SMEM(), SMEM()] + [VMEM()] * half,
        [joined],
        flops=2 * 10**9,
    )(place, smooth, *blocks)

    swap = [(i, (i + half) % row_count) for i in range(row_count)]
    last, state = lax.optimization_barrier((last, state))
    came = lax.ppermute(last, "row", swap)
    late, _ = call(
        functools.partial(across_kernel, True),
        halves,
        [SMEM(), SMEM(), VMEM(), VMEM()],
        identity,
        flops=10**10,
    )(place, smooth, cost, state)

    return call(
        second_vertical_kernel,
        jax.ShapeDtypeStruct((rows, width, DISPARITIES), f32),
        [SMEM(), SMEM()] + [VMEM()] * (half + 4),
        [pltpu.VMEM((rows, DISPARITIES, width), f32), joined],
        flops=3 * 10**9,
    )(place, smooth, *blocks, kept, came, early, late)


def solution(mesh):
    return jax.shard_map(
        per_device,
        mesh=mesh,
        in_specs=(P(None, "row", None, "col"), P(), P(), P("row", "col"), P("row", "col"), P()),
        out_specs=P("row", "col", None),
        check_vma=False,
    )
```

```python
import functools

import jax
import jax.numpy as jnp
from jax import lax
from jax.experimental import pallas as pl
from jax.experimental.pallas import tpu as pltpu
from jax.sharding import PartitionSpec as P

DISPARITIES = 128
OFF_MOST = 256
SUB = 8
REGS = DISPARITIES // SUB
MEBI = 1024 * 1024


def lane_to_disparity(lane):
    return (lane % SUB) * REGS + lane // SUB


def disparity_to_lane(disparity):
    return (disparity % REGS) * SUB + disparity // REGS


def least_of(values):
    while len(values) > 1:
        values = [jnp.minimum(a, b) for a, b in zip(values[::2], values[1::2])]
    turned = values + [pltpu.roll(values[0], turn, 0) for turn in range(1, SUB)]
    while len(turned) > 1:
        turned = [jnp.minimum(a, b) for a, b in zip(turned[::2], turned[1::2])]
    return turned[0]


def stepped(state, p1):
    row = lax.broadcasted_iota(jnp.int32, state[0].shape, 0)
    below = jnp.where(row == 0, jnp.inf, pltpu.roll(state[-1], 1, 0))
    above = jnp.where(row == SUB - 1, jnp.inf, pltpu.roll(state[0], SUB - 1, 0))
    lower = [below] + state[:-1]
    upper = state[1:] + [above]
    return [
        jnp.minimum(s, jnp.minimum(l, u) + p1) for s, l, u in zip(state, lower, upper)
    ]


def advance(state, cost, p1, p2):
    least = least_of(state)
    return [c + jnp.minimum(t - least, p2) for t, c in zip(stepped(state, p1), cost)]


def charges(charge_ref):
    return (
        charge_ref[0].astype(jnp.float32) * (1.0 / 64.0),
        charge_ref[1].astype(jnp.float32) * (1.0 / 64.0),
    )


def registers(array):
    return [array[SUB * v : SUB * (v + 1)] for v in range(REGS)]


def convolved(taps, window, bias):
    channels, cols = bias.shape[0], window.shape[1]
    column = lax.broadcasted_iota(jnp.int32, (1, cols), 1)
    by_tap = jnp.dot(taps, window, preferred_element_type=jnp.float32)
    before = pltpu.roll(by_tap[:channels], 1, 1)
    after = pltpu.roll(by_tap[2 * channels :], cols - 1, 1)
    z = by_tap[channels : 2 * channels] + jnp.where(column == 0, 0.0, before)
    return z + jnp.where(column == cols - 1, 0.0, after) + bias


def grouping(steps):
    return max(k for k in range(1, 9) if steps % k == 0)


def stage_kernel(filter_ref, bias_ref, tile_ref, taps_ref, shift_ref, tile_out):
    layers, _, _, channels, _ = filter_ref.shape
    one = lax.broadcasted_iota(jnp.int32, (channels, channels), 0)
    two = lax.broadcasted_iota(jnp.int32, (channels, channels), 1)
    for layer in range(layers):
        for a in range(3):
            for b in range(3):
                taps_ref[
                    layer, b * channels : (b + 1) * channels, a * channels : (a + 1) * channels
                ] = filter_ref[layer, a, b]
        spread_out = jnp.where(one == two, bias_ref[layer : layer + 1, :], 0.0)
        shift_ref[layer] = jnp.sum(spread_out, axis=1, keepdims=True)
    tile_out[...] = tile_ref[...]


def inner_kernel(masks, place_ref, taps_ref, shift_ref, *refs):
    parts = len(masks)
    tile_refs, (own_ref, *hidden_refs) = refs[:parts], refs[parts:]
    channels, width = tile_refs[0].shape[1:]
    rows = tile_refs[0].shape[0] // 2
    own = place_ref[2]
    for image in range(2):
        for mask, tile_ref in zip(masks, tile_refs):
            there = pl.ds(pl.multiple_of((own ^ mask) * width, width), width)
            for row in range(rows):
                own_ref[image, row * channels : (row + 1) * channels, there] = tile_ref[
                    image * rows + row
                ]
        source = own_ref
        for layer, target in enumerate(hidden_refs):
            steps = rows - 2 * (layer + 1)

            @pl.loop(0, steps, unroll=grouping(steps))
            def _(row):
                start = pl.multiple_of(row * channels, channels)
                window = source[image, pl.ds(start, 3 * channels), :]
                z = convolved(taps_ref[layer], window, shift_ref[layer])
                target[image, pl.ds(start, channels), :] = jnp.maximum(z, 0.0).astype(jnp.bfloat16)

            source = target


def band_kernel(masks, place_ref, taps_ref, bias_ref, rows_ref, *refs):
    layers = taps_ref.shape[0]
    parts = len(masks)
    inner_refs, refs = (rows_ref, *refs[: layers - 1]), refs[layers - 1 :]
    edge_refs, refs = refs[:parts], refs[parts:]
    cost_ref, own_ref, left_unit, right_unit, present, shifts, *maps = refs
    _, channels, width = edge_refs[0].shape
    rows = own_ref.shape[0]
    cols = parts * width
    first_row = place_ref[0] * rows
    rows_total = place_ref[1] * rows
    own = place_ref[2]
    lead = (OFF_MOST + 2 * width - 1) // width * width

    for mask, edge_ref in zip(masks, edge_refs):
        member = own ^ mask
        extra = edge_ref[4 * layers].astype(jnp.float32)
        present[:, pl.ds(pl.multiple_of(member * width, width), width)] = extra[0:16]
        shifts[member] = extra[16:24]
    right_unit[:, 0:lead] = jnp.zeros((rows * channels, lead), jnp.bfloat16)
    right_unit[:, lead + cols :] = jnp.zeros((rows * channels, width), jnp.bfloat16)

    for image in range(2):
        for inner_ref, held in zip(inner_refs, maps):
            held[layers * channels : held.shape[0] - layers * channels, :] = inner_ref[image]
        for mask, edge_ref in zip(masks, edge_refs):
            there = pl.ds(pl.multiple_of((own ^ mask) * width, width), width)
            for row in range(layers):
                above, below = row * channels, (layers + rows + row) * channels
                maps[0][above : above + channels, there] = edge_ref[image * layers + row]
                maps[0][below : below + channels, there] = edge_ref[(2 + image) * layers + row]

        for layer in range(layers):
            margin = layers - 1 - layer
            last = layer == layers - 1
            skipped = 0 if last else rows - 2 * (layer + 1)
            steps = rows + 2 * margin - skipped

            @pl.loop(0, steps, unroll=grouping(steps))
            def _(row):
                if not last:
                    row = jnp.where(row < layers, row, row + skipped)
                start = pl.multiple_of(row * channels, channels)
                window = maps[layer][pl.ds(start, 3 * channels), :]
                z = convolved(taps_ref[layer], window, bias_ref[layer])
                if not last:
                    there = first_row - margin + row
                    inside = jnp.logical_and(there >= 0, there < rows_total)
                    z = jnp.maximum(z, 0.0) * jnp.where(inside, 1.0, 0.0)
                    maps[layer + 1][pl.ds(start, channels), :] = z.astype(jnp.bfloat16)
                else:
                    scale = lax.rsqrt(jnp.sum(z * z, axis=0, keepdims=True) + 1e-06)
                    unit = (z * scale).astype(jnp.bfloat16)
                    if image == 0:
                        seen = present[pl.ds(row, 1), :]
                        unit = jnp.where(seen > 0.5, unit.astype(jnp.float32), 0.0)
                        left_unit[pl.ds(start, channels), :] = unit.astype(jnp.bfloat16)
                    else:
                        right_unit[pl.ds(start, channels), lead : lead + cols] = unit

    lane = lax.broadcasted_iota(jnp.int32, (width, DISPARITIES), 1)
    place = lax.broadcasted_iota(jnp.int32, (width, DISPARITIES), 0)

    @pl.loop(0, parts)
    def _(p):
        shift = jnp.max(shifts[p]).astype(jnp.int32)
        base = p * width - shift + lead
        block = base // width
        ahead = place + (base - block * width)
        index = (ahead - lane_to_disparity(lane)) & (DISPARITIES - 1)
        start = pl.multiple_of((block - 1) * width, width)
        here = pl.multiple_of(p * width, width)

        def tile_costs(mine):
            for y in range(rows):
                left = left_unit[y * channels : (y + 1) * channels, pl.ds(here, width)]
                right = right_unit[y * channels : (y + 1) * channels, pl.ds(start, 3 * width)]
                product = lax.dot_general(
                    left, right, (((0,), (0,)), ((), ())), preferred_element_type=jnp.float32
                )
                chosen = jnp.where(lane <= ahead, product[:, width : 2 * width], product[:, :width])
                chosen = jnp.where(lane <= ahead - width, product[:, 2 * width :], chosen)
                chosen = jnp.take_along_axis(chosen, index, axis=1, mode="promise_in_bounds")
                chosen = 1.0 - chosen
                cost_ref[pl.ds(pl.multiple_of(here * rows, rows) + y, width, stride=rows), :] = chosen
                if mine:
                    own_ref[y] = chosen.T.astype(jnp.bfloat16)

        pl.when(p == own)(functools.partial(tile_costs, True))
        pl.when(p != own)(functools.partial(tile_costs, False))


def early_segments(parts):
    return parts - parts // 4


def across_kernel(second, place_ref, charge_ref, cost_ref, *refs):
    kept_ref, last_ref, same_ref = refs[-3:]
    parts = cost_ref.shape[0] // kept_ref.shape[1]
    rows = last_ref.shape[1] // 2
    width = kept_ref.shape[1] // rows
    cols = parts * width
    early = early_segments(parts)
    own = place_ref[2]
    p1, p2 = charges(charge_ref)

    place = lax.broadcasted_iota(jnp.int32, (DISPARITIES, 2 * DISPARITIES), 0)
    other = lax.broadcasted_iota(jnp.int32, (DISPARITIES, 2 * DISPARITIES), 1)
    same_ref[...] = jnp.where(place == other % DISPARITIES, 1.0, 0.0).astype(jnp.bfloat16)
    same = same_ref[...]

    def at(column):
        return pl.ds(pl.multiple_of(column * rows, rows), rows)

    def cost_at(step):
        step = jnp.minimum(step, cols - 1)
        pair = jnp.concatenate([cost_ref[at(step)], cost_ref[at(cols - 1 - step)]], axis=0)
        coarse = pair.astype(jnp.bfloat16)
        fine = (pair - coarse.astype(jnp.float32)).astype(jnp.bfloat16)
        return registers(
            lax.dot_general(
                same,
                jnp.concatenate([coarse, fine], axis=1),
                (((1,), (1,)), ((), ())),
                preferred_element_type=jnp.float32,
            )
        )

    def segment(p, state):
        first_step = p * width

        def run(keep_right, keep_left, state):
            def body(i, carry):
                sums, cost = carry
                ahead = cost_at(first_step + i + 1)
                least = least_of(list(sums))
                jump = least + p2
                fresh = [
                    c + jnp.minimum(t, jump) for t, c in zip(stepped(list(sums), p1), cost)
                ]
                if keep_right or keep_left:
                    back = jnp.concatenate([f - least for f in fresh], axis=0).T
                if keep_right:
                    kept_ref[0, at(i)] = back[0:rows]
                if keep_left:
                    kept_ref[1, at(width - 1 - i)] = back[rows : 2 * rows]
                return tuple(fresh), tuple(ahead)

            carry = (state, tuple(cost_at(first_step)))
            sums = lax.fori_loop(0, width, body, carry, unroll=32)[0]
            least = least_of(list(sums))
            return tuple(s - least for s in sums)

        choice = jnp.where(p == own, 1, 0) + jnp.where(parts - 1 - p == own, 2, 0)
        return lax.switch(
            choice,
            [functools.partial(run, k == 1, k == 2) for k in range(3)],
            state,
        )

    if second:
        state = tuple(registers(refs[0][...]))
        span = (early, parts)
    else:
        state = tuple(jnp.zeros((SUB, 2 * rows), jnp.float32) for _ in range(REGS))
        span = (0, early)
    last_ref[...] = jnp.concatenate(lax.fori_loop(*span, segment, state), axis=0)


def down_or_up(forward, first_own, cost_ref, state, p1, p2, keep):
    group, rows = cost_ref.shape[:2]

    def block(b, state):
        member = jnp.where(forward, b, group - 1 - b)

        def run(kept, state):
            for i in range(rows):
                inner = jnp.where(forward, i, rows - 1 - i)
                cost = cost_ref[member, inner].astype(jnp.float32)
                state = advance(list(state), registers(cost), p1, p2)
                if kept:
                    keep(inner, jnp.concatenate(state, axis=0))
            return tuple(state)

        return lax.cond(
            member == first_own,
            functools.partial(run, True),
            functools.partial(run, False),
            state,
        )

    return lax.fori_loop(0, group, block, state)


def first_vertical_kernel(place_ref, charge_ref, *refs):
    *block_refs, kept_ref, last_ref, cost_ref = refs
    p1, p2 = charges(charge_ref)
    group, _, _, width = cost_ref.shape
    for k, block_ref in enumerate(block_refs):
        cost_ref[lax.rem(place_ref[4] + group - k, group)] = block_ref[...]
    state = tuple(jnp.zeros((SUB, width), jnp.float32) for _ in range(REGS))

    def keep(row, value):
        kept_ref[row] = value

    final = down_or_up(place_ref[3] == 0, place_ref[4], cost_ref, state, p1, p2, keep)
    last_ref[...] = jnp.concatenate(final, axis=0).astype(jnp.bfloat16)


def second_vertical_kernel(place_ref, charge_ref, *refs):
    *block_refs, kept_ref, came_ref, early_ref, late_ref, out_ref, total, cost_ref = refs
    p1, p2 = charges(charge_ref)
    group = cost_ref.shape[0]
    for k, block_ref in enumerate(block_refs):
        cost_ref[lax.rem(place_ref[4] + group - k, group)] = block_ref[...]
    rows, _, width = kept_ref.shape
    state = tuple(registers(came_ref[...].astype(jnp.float32)))

    def keep(row, value):
        total[row] = value + kept_ref[row]

    down_or_up(place_ref[3] != 0, place_ref[4], cost_ref, state, p1, p2, keep)
    lane = lax.broadcasted_iota(jnp.int32, (width, DISPARITIES), 1)
    index = disparity_to_lane(lane)
    right_early = place_ref[2] < place_ref[6]
    left_early = place_ref[5] - 1 - place_ref[2] < place_ref[6]
    for row in range(rows):
        this = pl.ds(row, width, stride=rows)
        right = jnp.where(right_early, early_ref[0, this, :], late_ref[0, this, :])
        left = jnp.where(left_early, early_ref[1, this, :], late_ref[1, this, :])
        value = total[row].T + (right + left)
        out_ref[row] = jnp.take_along_axis(value, index, axis=1, mode="promise_in_bounds")


SMEM = functools.partial(pl.BlockSpec, memory_space=pltpu.SMEM)
VMEM = functools.partial(pl.BlockSpec, memory_space=pltpu.VMEM)


def call(kernel, outs, specs, scratch=(), flops=0, vmem=20):
    return pl.pallas_call(
        kernel,
        out_shape=outs,
        in_specs=specs,
        out_specs=jax.tree.map(lambda _: VMEM(), outs),
        scratch_shapes=list(scratch),
        compiler_params=pltpu.CompilerParams(vmem_limit_bytes=vmem * MEBI),
        cost_estimate=pl.CostEstimate(flops=flops, bytes_accessed=1 << 22, transcendentals=0),
    )


def spread(block, parts, beside=()):
    masks, blocks = [0], [block]
    bit = parts // 2
    while bit:
        route = [(i, i ^ bit) for i in range(parts)]
        blocks += [lax.ppermute(held, "col", route) for held in blocks]
        masks += [mask ^ bit for mask in masks]
        if beside and bit == parts // 2:
            first, *beside = lax.optimization_barrier((blocks[1], *beside))
            blocks[1] = first
        bit //= 2
    return masks, blocks, beside


def per_device(activations, filters, biases, present, shifts, smooth):
    _, rows, channels, width = activations.shape
    layers = filters.shape[0]
    high = rows + 2 * layers
    row_rank, row_count = lax.axis_index("row"), lax.axis_size("row")
    col_rank, parts = lax.axis_index("col"), lax.axis_size("col")
    half = row_count // 2
    cols = parts * width
    place = jnp.stack(
        [
            row_rank,
            jnp.int32(row_count),
            col_rank,
            row_rank // half,
            row_rank % half,
            jnp.int32(parts),
            jnp.int32(early_segments(parts)),
        ]
    ).astype(jnp.int32)

    downward = [(i, i + 1) for i in range(row_count - 1)]
    upward = [(i + 1, i) for i in range(row_count - 1)]
    before = lax.ppermute(activations[:, rows - layers :], "row", downward)
    after = lax.ppermute(activations[:, :layers], "row", upward)
    f32, bf16 = jnp.float32, jnp.bfloat16
    tile = activations.reshape(2 * rows, channels, width)
    taps, upright, staged = call(
        stage_kernel,
        (
            jax.ShapeDtypeStruct((layers, 3 * channels, 3 * channels), bf16),
            jax.ShapeDtypeStruct((layers, channels, 1), f32),
            jax.ShapeDtypeStruct(tile.shape, bf16),
        ),
        [VMEM()] * 3,
        flops=10**8,
    )(filters, biases, tile)
    before, after, taps, upright, staged = lax.optimization_barrier(
        (before, after, taps, upright, staged)
    )
    extra = jnp.concatenate(
        [
            present.astype(jnp.bfloat16),
            jnp.zeros((16 - rows, width), jnp.bfloat16),
            jnp.broadcast_to(shifts.astype(jnp.bfloat16), (channels - 16, width)),
        ],
        axis=0,
    )
    edges = jnp.concatenate(
        [before.reshape(-1, channels, width), after.reshape(-1, channels, width), extra[None]],
        axis=0,
    )
    masks, tiles, _ = spread(tile, parts)

    lead = (OFF_MOST + 2 * width - 1) // width * width
    inner = call(
        functools.partial(inner_kernel, masks),
        tuple(
            jax.ShapeDtypeStruct((2, (rows - 2 * layer) * channels, cols), bf16)
            for layer in range(layers)
        ),
        [SMEM()] + [VMEM()] * (2 + parts),
        flops=2 * 10**9,
        vmem=32,
    )(place, taps, upright, staged, *tiles[1:])
    _, edges, inner = spread(edges, parts, inner)
    cost, own = call(
        functools.partial(band_kernel, masks),
        (
            jax.ShapeDtypeStruct((cols * rows, DISPARITIES), f32),
            jax.ShapeDtypeStruct((rows, DISPARITIES, width), bf16),
        ),
        [SMEM()] + [VMEM()] * (2 + layers + parts),
        [
            pltpu.VMEM((rows * channels, cols), bf16),
            pltpu.VMEM((rows * channels, lead + cols + width), bf16),
            pltpu.VMEM((16, cols), f32),
            pltpu.VMEM((parts, SUB, width), f32),
            *(
                pltpu.VMEM(((high - 2 * layer) * channels, cols), bf16)
                for layer in range(layers)
            ),
        ],
        flops=10**10,
        vmem=40,
    )(place, taps, upright, *inner, *edges)

    blocks = [own]
    for k in range(1, half):
        turn = [(i, i // half * half + (i + k) % half) for i in range(row_count)]
        blocks.append(lax.ppermute(own, "row", turn))

    halves = (
        jax.ShapeDtypeStruct((2, width * rows, DISPARITIES), f32),
        jax.ShapeDtypeStruct((DISPARITIES, 2 * rows), f32),
    )
    identity = [pltpu.VMEM((DISPARITIES, 2 * DISPARITIES), bf16)]
    early, state = call(
        functools.partial(across_kernel, False),
        halves,
        [SMEM(), SMEM(), VMEM()],
        identity,
        flops=10**10,
    )(place, smooth, cost)
    *blocks, state = lax.optimization_barrier((*blocks, state))

    joined = pltpu.VMEM((half, rows, DISPARITIES, width), bf16)
    kept, last = call(
        first_vertical_kernel,
        (
            jax.ShapeDtypeStruct((rows, DISPARITIES, width), f32),
            jax.ShapeDtypeStruct((DISPARITIES, width), bf16),
        ),
        [SMEM(), SMEM()] + [VMEM()] * half,
        [joined],
        flops=2 * 10**9,
    )(place, smooth, *blocks)

    swap = [(i, (i + half) % row_count) for i in range(row_count)]
    last, state = lax.optimization_barrier((last, state))
    came = lax.ppermute(last, "row", swap)
    late, _ = call(
        functools.partial(across_kernel, True),
        halves,
        [SMEM(), SMEM(), VMEM(), VMEM()],
        identity,
        flops=10**10,
    )(place, smooth, cost, state)

    return call(
        second_vertical_kernel,
        jax.ShapeDtypeStruct((rows, width, DISPARITIES), f32),
        [SMEM(), SMEM()] + [VMEM()] * (half + 4),
        [pltpu.VMEM((rows, DISPARITIES, width), f32), joined],
        flops=3 * 10**9,
    )(place, smooth, *blocks, kept, came, early, late)


def solution(mesh):
    return jax.shard_map(
        per_device,
        mesh=mesh,
        in_specs=(P(None, "row", None, "col"), P(), P(), P("row", "col"), P("row", "col"), P()),
        out_specs=P("row", "col", None),
        check_vma=False,
    )
```

```python
import functools

import jax
import jax.numpy as jnp
from jax import lax
from jax.experimental import pallas as pl
from jax.experimental.pallas import tpu as pltpu
from jax.sharding import PartitionSpec as P

DISPARITIES = 128
OFF_MOST = 256
SUB = 8
REGS = DISPARITIES // SUB
MEBI = 1024 * 1024


def lane_to_disparity(lane):
    return (lane % SUB) * REGS + lane // SUB


def disparity_to_lane(disparity):
    return (disparity % REGS) * SUB + disparity // REGS


def least_of(values):
    while len(values) > 1:
        values = [jnp.minimum(a, b) for a, b in zip(values[::2], values[1::2])]
    turned = values + [pltpu.roll(values[0], turn, 0) for turn in range(1, SUB)]
    while len(turned) > 1:
        turned = [jnp.minimum(a, b) for a, b in zip(turned[::2], turned[1::2])]
    return turned[0]


def stepped(state, p1):
    row = lax.broadcasted_iota(jnp.int32, state[0].shape, 0)
    below = jnp.where(row == 0, jnp.inf, pltpu.roll(state[-1], 1, 0))
    above = jnp.where(row == SUB - 1, jnp.inf, pltpu.roll(state[0], SUB - 1, 0))
    lower = [below] + state[:-1]
    upper = state[1:] + [above]
    return [
        jnp.minimum(s, jnp.minimum(l, u) + p1) for s, l, u in zip(state, lower, upper)
    ]


def advance(state, cost, p1, p2):
    least = least_of(state)
    return [c + jnp.minimum(t - least, p2) for t, c in zip(stepped(state, p1), cost)]


def charges(charge_ref):
    return (
        charge_ref[0].astype(jnp.float32) * (1.0 / 64.0),
        charge_ref[1].astype(jnp.float32) * (1.0 / 64.0),
    )


def registers(array):
    return [array[SUB * v : SUB * (v + 1)] for v in range(REGS)]


def convolved(taps, window, bias):
    channels, cols = bias.shape[0], window.shape[1]
    column = lax.broadcasted_iota(jnp.int32, (1, cols), 1)
    by_tap = jnp.dot(taps, window, preferred_element_type=jnp.float32)
    before = pltpu.roll(by_tap[:channels], 1, 1)
    after = pltpu.roll(by_tap[2 * channels :], cols - 1, 1)
    z = by_tap[channels : 2 * channels] + jnp.where(column == 0, 0.0, before)
    return z + jnp.where(column == cols - 1, 0.0, after) + bias


def grouping(steps):
    return max(k for k in range(1, 9) if steps % k == 0)


def stage_kernel(filter_ref, bias_ref, tile_ref, taps_ref, shift_ref, tile_out):
    layers, _, _, channels, _ = filter_ref.shape
    one = lax.broadcasted_iota(jnp.int32, (channels, channels), 0)
    two = lax.broadcasted_iota(jnp.int32, (channels, channels), 1)
    for layer in range(layers):
        for a in range(3):
            for b in range(3):
                taps_ref[
                    layer, b * channels : (b + 1) * channels, a * channels : (a + 1) * channels
                ] = filter_ref[layer, a, b]
        spread_out = jnp.where(one == two, bias_ref[layer : layer + 1, :], 0.0)
        shift_ref[layer] = jnp.sum(spread_out, axis=1, keepdims=True)
    tile_out[...] = tile_ref[...]


def inner_kernel(masks, place_ref, taps_ref, shift_ref, *refs):
    parts = len(masks)
    tile_refs, (own_ref, *hidden_refs) = refs[:parts], refs[parts:]
    channels, width = tile_refs[0].shape[1:]
    rows = tile_refs[0].shape[0] // 2
    own = place_ref[2]
    for image in range(2):
        for mask, tile_ref in zip(masks, tile_refs):
            there = pl.ds(pl.multiple_of((own ^ mask) * width, width), width)
            for row in range(rows):
                own_ref[image, row * channels : (row + 1) * channels, there] = tile_ref[
                    image * rows + row
                ]
        source = own_ref
        for layer, target in enumerate(hidden_refs):
            steps = rows - 2 * (layer + 1)

            @pl.loop(0, steps, unroll=grouping(steps))
            def _(row):
                start = pl.multiple_of(row * channels, channels)
                window = source[image, pl.ds(start, 3 * channels), :]
                z = convolved(taps_ref[layer], window, shift_ref[layer])
                target[image, pl.ds(start, channels), :] = jnp.maximum(z, 0.0).astype(jnp.bfloat16)

            source = target


def band_kernel(masks, place_ref, taps_ref, bias_ref, rows_ref, *refs):
    layers = taps_ref.shape[0]
    parts = len(masks)
    inner_refs, refs = (rows_ref, *refs[: layers - 1]), refs[layers - 1 :]
    edge_refs, refs = refs[:parts], refs[parts:]
    cost_ref, own_ref, left_unit, right_unit, present, shifts, *maps = refs
    _, channels, width = edge_refs[0].shape
    rows = own_ref.shape[0]
    cols = parts * width
    first_row = place_ref[0] * rows
    rows_total = place_ref[1] * rows
    own = place_ref[2]
    lead = (OFF_MOST + 2 * width - 1) // width * width

    for mask, edge_ref in zip(masks, edge_refs):
        member = own ^ mask
        extra = edge_ref[4 * layers].astype(jnp.float32)
        present[:, pl.ds(pl.multiple_of(member * width, width), width)] = extra[0:16]
        shifts[member] = extra[16:24]
    right_unit[:, 0:lead] = jnp.zeros((rows * channels, lead), jnp.bfloat16)
    right_unit[:, lead + cols :] = jnp.zeros((rows * channels, width), jnp.bfloat16)

    for image in range(2):
        for inner_ref, held in zip(inner_refs, maps):
            held[layers * channels : held.shape[0] - layers * channels, :] = inner_ref[image]
        for mask, edge_ref in zip(masks, edge_refs):
            there = pl.ds(pl.multiple_of((own ^ mask) * width, width), width)
            for row in range(layers):
                above, below = row * channels, (layers + rows + row) * channels
                maps[0][above : above + channels, there] = edge_ref[image * layers + row]
                maps[0][below : below + channels, there] = edge_ref[(2 + image) * layers + row]

        for layer in range(layers):
            margin = layers - 1 - layer
            last = layer == layers - 1
            skipped = 0 if last else rows - 2 * (layer + 1)
            steps = rows + 2 * margin - skipped

            @pl.loop(0, steps, unroll=grouping(steps))
            def _(row):
                if not last:
                    row = jnp.where(row < layers, row, row + skipped)
                start = pl.multiple_of(row * channels, channels)
                window = maps[layer][pl.ds(start, 3 * channels), :]
                z = convolved(taps_ref[layer], window, bias_ref[layer])
                if not last:
                    there = first_row - margin + row
                    inside = jnp.logical_and(there >= 0, there < rows_total)
                    z = jnp.maximum(z, 0.0) * jnp.where(inside, 1.0, 0.0)
                    maps[layer + 1][pl.ds(start, channels), :] = z.astype(jnp.bfloat16)
                else:
                    scale = lax.rsqrt(jnp.sum(z * z, axis=0, keepdims=True) + 1e-06)
                    unit = (z * scale).astype(jnp.bfloat16)
                    if image == 0:
                        seen = present[pl.ds(row, 1), :]
                        unit = jnp.where(seen > 0.5, unit.astype(jnp.float32), 0.0)
                        left_unit[pl.ds(start, channels), :] = unit.astype(jnp.bfloat16)
                    else:
                        right_unit[pl.ds(start, channels), lead : lead + cols] = unit

    lane = lax.broadcasted_iota(jnp.int32, (width, DISPARITIES), 1)
    place = lax.broadcasted_iota(jnp.int32, (width, DISPARITIES), 0)

    @pl.loop(0, parts)
    def _(p):
        shift = jnp.max(shifts[p]).astype(jnp.int32)
        base = p * width - shift + lead
        block = base // width
        ahead = place + (base - block * width)
        index = (ahead - lane_to_disparity(lane)) & (DISPARITIES - 1)
        start = pl.multiple_of((block - 1) * width, width)
        here = pl.multiple_of(p * width, width)

        def tile_costs(mine):
            for y in range(rows):
                left = left_unit[y * channels : (y + 1) * channels, pl.ds(here, width)]
                right = right_unit[y * channels : (y + 1) * channels, pl.ds(start, 3 * width)]
                product = lax.dot_general(
                    left, right, (((0,), (0,)), ((), ())), preferred_element_type=jnp.float32
                )
                chosen = jnp.where(lane <= ahead, product[:, width : 2 * width], product[:, :width])
                chosen = jnp.where(lane <= ahead - width, product[:, 2 * width :], chosen)
                chosen = jnp.take_along_axis(chosen, index, axis=1, mode="promise_in_bounds")
                chosen = 1.0 - chosen
                cost_ref[pl.ds(pl.multiple_of(here * rows, rows) + y, width, stride=rows), :] = chosen
                if mine:
                    own_ref[y] = chosen.T.astype(jnp.bfloat16)

        pl.when(p == own)(functools.partial(tile_costs, True))
        pl.when(p != own)(functools.partial(tile_costs, False))


def early_segments(parts):
    return parts - parts // 4


def across_kernel(second, place_ref, charge_ref, cost_ref, *refs):
    kept_ref, last_ref, same_ref = refs[-3:]
    parts = cost_ref.shape[0] // kept_ref.shape[1]
    rows = last_ref.shape[1] // 2
    width = kept_ref.shape[1] // rows
    cols = parts * width
    early = early_segments(parts)
    own = place_ref[2]
    p1, p2 = charges(charge_ref)

    place = lax.broadcasted_iota(jnp.int32, (DISPARITIES, 2 * DISPARITIES), 0)
    other = lax.broadcasted_iota(jnp.int32, (DISPARITIES, 2 * DISPARITIES), 1)
    same_ref[...] = jnp.where(place == other % DISPARITIES, 1.0, 0.0).astype(jnp.bfloat16)
    same = same_ref[...]

    def at(column):
        return pl.ds(pl.multiple_of(column * rows, rows), rows)

    def cost_at(step):
        step = jnp.minimum(step, cols - 1)
        pair = jnp.concatenate([cost_ref[at(step)], cost_ref[at(cols - 1 - step)]], axis=0)
        coarse = pair.astype(jnp.bfloat16)
        fine = (pair - coarse.astype(jnp.float32)).astype(jnp.bfloat16)
        return registers(
            lax.dot_general(
                same,
                jnp.concatenate([coarse, fine], axis=1),
                (((1,), (1,)), ((), ())),
                preferred_element_type=jnp.float32,
            )
        )

    def segment(p, state):
        first_step = p * width

        def run(keep_right, keep_left, state):
            def body(i, carry):
                sums, cost = carry
                ahead = cost_at(first_step + i + 1)
                least = least_of(list(sums))
                jump = least + p2
                fresh = [
                    c + jnp.minimum(t, jump) for t, c in zip(stepped(list(sums), p1), cost)
                ]
                if keep_right or keep_left:
                    back = jnp.concatenate([f - least for f in fresh], axis=0).T
                if keep_right:
                    kept_ref[0, at(i)] = back[0:rows]
                if keep_left:
                    kept_ref[1, at(width - 1 - i)] = back[rows : 2 * rows]
                return tuple(fresh), tuple(ahead)

            carry = (state, tuple(cost_at(first_step)))
            sums = lax.fori_loop(0, width, body, carry, unroll=64)[0]
            least = least_of(list(sums))
            return tuple(s - least for s in sums)

        choice = jnp.where(p == own, 1, 0) + jnp.where(parts - 1 - p == own, 2, 0)
        return lax.switch(
            choice,
            [functools.partial(run, k == 1, k == 2) for k in range(3)],
            state,
        )

    if second:
        state = tuple(registers(refs[0][...]))
        span = (early, parts)
    else:
        state = tuple(jnp.zeros((SUB, 2 * rows), jnp.float32) for _ in range(REGS))
        span = (0, early)
    last_ref[...] = jnp.concatenate(lax.fori_loop(*span, segment, state), axis=0)


def down_or_up(forward, first_own, cost_ref, state, p1, p2, keep):
    group, rows = cost_ref.shape[:2]

    def block(b, state):
        member = jnp.where(forward, b, group - 1 - b)

        def run(kept, state):
            for i in range(rows):
                inner = jnp.where(forward, i, rows - 1 - i)
                cost = cost_ref[member, inner].astype(jnp.float32)
                state = advance(list(state), registers(cost), p1, p2)
                if kept:
                    keep(inner, jnp.concatenate(state, axis=0))
            return tuple(state)

        return lax.cond(
            member == first_own,
            functools.partial(run, True),
            functools.partial(run, False),
            state,
        )

    return lax.fori_loop(0, group, block, state)


def first_vertical_kernel(place_ref, charge_ref, *refs):
    *block_refs, kept_ref, last_ref, cost_ref = refs
    p1, p2 = charges(charge_ref)
    group, _, _, width = cost_ref.shape
    for k, block_ref in enumerate(block_refs):
        cost_ref[lax.rem(place_ref[4] + group - k, group)] = block_ref[...]
    state = tuple(jnp.zeros((SUB, width), jnp.float32) for _ in range(REGS))

    def keep(row, value):
        kept_ref[row] = value

    final = down_or_up(place_ref[3] == 0, place_ref[4], cost_ref, state, p1, p2, keep)
    last_ref[...] = jnp.concatenate(final, axis=0).astype(jnp.bfloat16)


def second_vertical_kernel(place_ref, charge_ref, *refs):
    *block_refs, kept_ref, came_ref, early_ref, late_ref, out_ref, total, cost_ref = refs
    p1, p2 = charges(charge_ref)
    group = cost_ref.shape[0]
    for k, block_ref in enumerate(block_refs):
        cost_ref[lax.rem(place_ref[4] + group - k, group)] = block_ref[...]
    rows, _, width = kept_ref.shape
    state = tuple(registers(came_ref[...].astype(jnp.float32)))

    def keep(row, value):
        total[row] = value + kept_ref[row]

    down_or_up(place_ref[3] != 0, place_ref[4], cost_ref, state, p1, p2, keep)
    lane = lax.broadcasted_iota(jnp.int32, (width, DISPARITIES), 1)
    index = disparity_to_lane(lane)
    right_early = place_ref[2] < place_ref[6]
    left_early = place_ref[5] - 1 - place_ref[2] < place_ref[6]
    for row in range(rows):
        this = pl.ds(row, width, stride=rows)
        right = jnp.where(right_early, early_ref[0, this, :], late_ref[0, this, :])
        left = jnp.where(left_early, early_ref[1, this, :], late_ref[1, this, :])
        value = total[row].T + (right + left)
        out_ref[row] = jnp.take_along_axis(value, index, axis=1, mode="promise_in_bounds")


SMEM = functools.partial(pl.BlockSpec, memory_space=pltpu.SMEM)
VMEM = functools.partial(pl.BlockSpec, memory_space=pltpu.VMEM)


def call(kernel, outs, specs, scratch=(), flops=0, vmem=20):
    return pl.pallas_call(
        kernel,
        out_shape=outs,
        in_specs=specs,
        out_specs=jax.tree.map(lambda _: VMEM(), outs),
        scratch_shapes=list(scratch),
        compiler_params=pltpu.CompilerParams(vmem_limit_bytes=vmem * MEBI),
        cost_estimate=pl.CostEstimate(flops=flops, bytes_accessed=1 << 22, transcendentals=0),
    )


def spread(block, parts, beside=()):
    masks, blocks = [0], [block]
    bit = parts // 2
    while bit:
        route = [(i, i ^ bit) for i in range(parts)]
        blocks += [lax.ppermute(held, "col", route) for held in blocks]
        masks += [mask ^ bit for mask in masks]
        if beside and bit == parts // 2:
            first, *beside = lax.optimization_barrier((blocks[1], *beside))
            blocks[1] = first
        bit //= 2
    return masks, blocks, beside


def per_device(activations, filters, biases, present, shifts, smooth):
    _, rows, channels, width = activations.shape
    layers = filters.shape[0]
    high = rows + 2 * layers
    row_rank, row_count = lax.axis_index("row"), lax.axis_size("row")
    col_rank, parts = lax.axis_index("col"), lax.axis_size("col")
    half = row_count // 2
    cols = parts * width
    place = jnp.stack(
        [
            row_rank,
            jnp.int32(row_count),
            col_rank,
            row_rank // half,
            row_rank % half,
            jnp.int32(parts),
            jnp.int32(early_segments(parts)),
        ]
    ).astype(jnp.int32)

    downward = [(i, i + 1) for i in range(row_count - 1)]
    upward = [(i + 1, i) for i in range(row_count - 1)]
    before = lax.ppermute(activations[:, rows - layers :], "row", downward)
    after = lax.ppermute(activations[:, :layers], "row", upward)
    f32, bf16 = jnp.float32, jnp.bfloat16
    tile = activations.reshape(2 * rows, channels, width)
    taps, upright, staged = call(
        stage_kernel,
        (
            jax.ShapeDtypeStruct((layers, 3 * channels, 3 * channels), bf16),
            jax.ShapeDtypeStruct((layers, channels, 1), f32),
            jax.ShapeDtypeStruct(tile.shape, bf16),
        ),
        [VMEM()] * 3,
        flops=10**8,
    )(filters, biases, tile)
    before, after, taps, upright, staged = lax.optimization_barrier(
        (before, after, taps, upright, staged)
    )
    extra = jnp.concatenate(
        [
            present.astype(jnp.bfloat16),
            jnp.zeros((16 - rows, width), jnp.bfloat16),
            jnp.broadcast_to(shifts.astype(jnp.bfloat16), (channels - 16, width)),
        ],
        axis=0,
    )
    edges = jnp.concatenate(
        [before.reshape(-1, channels, width), after.reshape(-1, channels, width), extra[None]],
        axis=0,
    )
    masks, tiles, _ = spread(tile, parts)

    lead = (OFF_MOST + 2 * width - 1) // width * width
    inner = call(
        functools.partial(inner_kernel, masks),
        tuple(
            jax.ShapeDtypeStruct((2, (rows - 2 * layer) * channels, cols), bf16)
            for layer in range(layers)
        ),
        [SMEM()] + [VMEM()] * (2 + parts),
        flops=2 * 10**9,
        vmem=32,
    )(place, taps, upright, staged, *tiles[1:])
    _, edges, inner = spread(edges, parts, inner)
    cost, own = call(
        functools.partial(band_kernel, masks),
        (
            jax.ShapeDtypeStruct((cols * rows, DISPARITIES), f32),
            jax.ShapeDtypeStruct((rows, DISPARITIES, width), bf16),
        ),
        [SMEM()] + [VMEM()] * (2 + layers + parts),
        [
            pltpu.VMEM((rows * channels, cols), bf16),
            pltpu.VMEM((rows * channels, lead + cols + width), bf16),
            pltpu.VMEM((16, cols), f32),
            pltpu.VMEM((parts, SUB, width), f32),
            *(
                pltpu.VMEM(((high - 2 * layer) * channels, cols), bf16)
                for layer in range(layers)
            ),
        ],
        flops=10**10,
        vmem=40,
    )(place, taps, upright, *inner, *edges)

    blocks = [own]
    for k in range(1, half):
        turn = [(i, i // half * half + (i + k) % half) for i in range(row_count)]
        blocks.append(lax.ppermute(own, "row", turn))

    halves = (
        jax.ShapeDtypeStruct((2, width * rows, DISPARITIES), f32),
        jax.ShapeDtypeStruct((DISPARITIES, 2 * rows), f32),
    )
    identity = [pltpu.VMEM((DISPARITIES, 2 * DISPARITIES), bf16)]
    early, state = call(
        functools.partial(across_kernel, False),
        halves,
        [SMEM(), SMEM(), VMEM()],
        identity,
        flops=10**10,
    )(place, smooth, cost)
    *blocks, state = lax.optimization_barrier((*blocks, state))

    joined = pltpu.VMEM((half, rows, DISPARITIES, width), bf16)
    kept, last = call(
        first_vertical_kernel,
        (
            jax.ShapeDtypeStruct((rows, DISPARITIES, width), f32),
            jax.ShapeDtypeStruct((DISPARITIES, width), bf16),
        ),
        [SMEM(), SMEM()] + [VMEM()] * half,
        [joined],
        flops=2 * 10**9,
    )(place, smooth, *blocks)

    swap = [(i, (i + half) % row_count) for i in range(row_count)]
    last, state = lax.optimization_barrier((last, state))
    came = lax.ppermute(last, "row", swap)
    late, _ = call(
        functools.partial(across_kernel, True),
        halves,
        [SMEM(), SMEM(), VMEM(), VMEM()],
        identity,
        flops=10**10,
    )(place, smooth, cost, state)

    return call(
        second_vertical_kernel,
        jax.ShapeDtypeStruct((rows, width, DISPARITIES), f32),
        [SMEM(), SMEM()] + [VMEM()] * (half + 4),
        [pltpu.VMEM((rows, DISPARITIES, width), f32), joined],
        flops=3 * 10**9,
    )(place, smooth, *blocks, kept, came, early, late)


def solution(mesh):
    return jax.shard_map(
        per_device,
        mesh=mesh,
        in_specs=(P(None, "row", None, "col"), P(), P(), P("row", "col"), P("row", "col"), P()),
        out_specs=P("row", "col", None),
        check_vma=False,
    )
```

```python
import functools

import jax
import jax.numpy as jnp
from jax import lax
from jax.experimental import pallas as pl
from jax.experimental.pallas import tpu as pltpu
from jax.sharding import PartitionSpec as P

DISPARITIES = 128
OFF_MOST = 256
SUB = 8
REGS = DISPARITIES // SUB
MEBI = 1024 * 1024


def lane_to_disparity(lane):
    return (lane % SUB) * REGS + lane // SUB


def disparity_to_lane(disparity):
    return (disparity % REGS) * SUB + disparity // REGS


def least_of(values):
    while len(values) > 1:
        values = [jnp.minimum(a, b) for a, b in zip(values[::2], values[1::2])]
    turned = values + [pltpu.roll(values[0], turn, 0) for turn in range(1, SUB)]
    while len(turned) > 1:
        turned = [jnp.minimum(a, b) for a, b in zip(turned[::2], turned[1::2])]
    return turned[0]


def stepped(state, p1):
    row = lax.broadcasted_iota(jnp.int32, state[0].shape, 0)
    below = jnp.where(row == 0, jnp.inf, pltpu.roll(state[-1], 1, 0))
    above = jnp.where(row == SUB - 1, jnp.inf, pltpu.roll(state[0], SUB - 1, 0))
    lower = [below] + state[:-1]
    upper = state[1:] + [above]
    return [
        jnp.minimum(s, jnp.minimum(l, u) + p1) for s, l, u in zip(state, lower, upper)
    ]


def advance(state, cost, p1, p2):
    least = least_of(state)
    return [c + jnp.minimum(t - least, p2) for t, c in zip(stepped(state, p1), cost)]


def charges(charge_ref):
    return (
        charge_ref[0].astype(jnp.float32) * (1.0 / 64.0),
        charge_ref[1].astype(jnp.float32) * (1.0 / 64.0),
    )


def registers(array):
    return [array[SUB * v : SUB * (v + 1)] for v in range(REGS)]


def convolved(taps, window, bias):
    channels, cols = bias.shape[0], window.shape[1]
    column = lax.broadcasted_iota(jnp.int32, (1, cols), 1)
    by_tap = jnp.dot(taps, window, preferred_element_type=jnp.float32)
    before = pltpu.roll(by_tap[:channels], 1, 1)
    after = pltpu.roll(by_tap[2 * channels :], cols - 1, 1)
    z = by_tap[channels : 2 * channels] + jnp.where(column == 0, 0.0, before)
    return z + jnp.where(column == cols - 1, 0.0, after) + bias


def grouping(steps):
    return max(k for k in range(1, 9) if steps % k == 0)


def stage_kernel(filter_ref, bias_ref, tile_ref, taps_ref, shift_ref, tile_out):
    layers, _, _, channels, _ = filter_ref.shape
    one = lax.broadcasted_iota(jnp.int32, (channels, channels), 0)
    two = lax.broadcasted_iota(jnp.int32, (channels, channels), 1)
    for layer in range(layers):
        for a in range(3):
            for b in range(3):
                taps_ref[
                    layer, b * channels : (b + 1) * channels, a * channels : (a + 1) * channels
                ] = filter_ref[layer, a, b]
        spread_out = jnp.where(one == two, bias_ref[layer : layer + 1, :], 0.0)
        shift_ref[layer] = jnp.sum(spread_out, axis=1, keepdims=True)
    tile_out[...] = tile_ref[...]


def inner_kernel(masks, place_ref, taps_ref, shift_ref, *refs):
    parts = len(masks)
    tile_refs, (own_ref, *hidden_refs) = refs[:parts], refs[parts:]
    channels, width = tile_refs[0].shape[1:]
    rows = tile_refs[0].shape[0] // 2
    own = place_ref[2]
    for image in range(2):
        for mask, tile_ref in zip(masks, tile_refs):
            there = pl.ds(pl.multiple_of((own ^ mask) * width, width), width)
            for row in range(rows):
                own_ref[image, row * channels : (row + 1) * channels, there] = tile_ref[
                    image * rows + row
                ]
        source = own_ref
        for layer, target in enumerate(hidden_refs):
            steps = rows - 2 * (layer + 1)

            @pl.loop(0, steps, unroll=grouping(steps))
            def _(row):
                start = pl.multiple_of(row * channels, channels)
                window = source[image, pl.ds(start, 3 * channels), :]
                z = convolved(taps_ref[layer], window, shift_ref[layer])
                target[image, pl.ds(start, channels), :] = jnp.maximum(z, 0.0).astype(jnp.bfloat16)

            source = target


def band_kernel(masks, place_ref, taps_ref, bias_ref, rows_ref, *refs):
    layers = taps_ref.shape[0]
    parts = len(masks)
    inner_refs, refs = (rows_ref, *refs[: layers - 1]), refs[layers - 1 :]
    edge_refs, refs = refs[:parts], refs[parts:]
    cost_ref, own_ref, left_unit, right_unit, present, shifts, *maps = refs
    _, channels, width = edge_refs[0].shape
    rows = own_ref.shape[0]
    cols = parts * width
    first_row = place_ref[0] * rows
    rows_total = place_ref[1] * rows
    own = place_ref[2]
    lead = (OFF_MOST + 2 * width - 1) // width * width

    for mask, edge_ref in zip(masks, edge_refs):
        member = own ^ mask
        extra = edge_ref[4 * layers].astype(jnp.float32)
        present[:, pl.ds(pl.multiple_of(member * width, width), width)] = extra[0:16]
        shifts[member] = extra[16:24]
    right_unit[:, 0:lead] = jnp.zeros((rows * channels, lead), jnp.bfloat16)
    right_unit[:, lead + cols :] = jnp.zeros((rows * channels, width), jnp.bfloat16)

    for image in range(2):
        for inner_ref, held in zip(inner_refs, maps):
            held[layers * channels : held.shape[0] - layers * channels, :] = inner_ref[image]
        for mask, edge_ref in zip(masks, edge_refs):
            there = pl.ds(pl.multiple_of((own ^ mask) * width, width), width)
            for row in range(layers):
                above, below = row * channels, (layers + rows + row) * channels
                maps[0][above : above + channels, there] = edge_ref[image * layers + row]
                maps[0][below : below + channels, there] = edge_ref[(2 + image) * layers + row]

        for layer in range(layers):
            margin = layers - 1 - layer
            last = layer == layers - 1
            skipped = 0 if last else rows - 2 * (layer + 1)
            steps = rows + 2 * margin - skipped

            @pl.loop(0, steps, unroll=grouping(steps))
            def _(row):
                if not last:
                    row = jnp.where(row < layers, row, row + skipped)
                start = pl.multiple_of(row * channels, channels)
                window = maps[layer][pl.ds(start, 3 * channels), :]
                z = convolved(taps_ref[layer], window, bias_ref[layer])
                if not last:
                    there = first_row - margin + row
                    inside = jnp.logical_and(there >= 0, there < rows_total)
                    z = jnp.maximum(z, 0.0) * jnp.where(inside, 1.0, 0.0)
                    maps[layer + 1][pl.ds(start, channels), :] = z.astype(jnp.bfloat16)
                else:
                    scale = lax.rsqrt(jnp.sum(z * z, axis=0, keepdims=True) + 1e-06)
                    unit = (z * scale).astype(jnp.bfloat16)
                    if image == 0:
                        seen = present[pl.ds(row, 1), :]
                        unit = jnp.where(seen > 0.5, unit.astype(jnp.float32), 0.0)
                        left_unit[pl.ds(start, channels), :] = unit.astype(jnp.bfloat16)
                    else:
                        right_unit[pl.ds(start, channels), lead : lead + cols] = unit

    lane = lax.broadcasted_iota(jnp.int32, (width, DISPARITIES), 1)
    place = lax.broadcasted_iota(jnp.int32, (width, DISPARITIES), 0)

    @pl.loop(0, parts)
    def _(p):
        shift = jnp.max(shifts[p]).astype(jnp.int32)
        base = p * width - shift + lead
        block = base // width
        ahead = place + (base - block * width)
        index = (ahead - lane_to_disparity(lane)) & (DISPARITIES - 1)
        start = pl.multiple_of((block - 1) * width, width)
        here = pl.multiple_of(p * width, width)

        def tile_costs(mine):
            for y in range(rows):
                left = left_unit[y * channels : (y + 1) * channels, pl.ds(here, width)]
                right = right_unit[y * channels : (y + 1) * channels, pl.ds(start, 3 * width)]
                product = lax.dot_general(
                    left, right, (((0,), (0,)), ((), ())), preferred_element_type=jnp.float32
                )
                chosen = jnp.where(lane <= ahead, product[:, width : 2 * width], product[:, :width])
                chosen = jnp.where(lane <= ahead - width, product[:, 2 * width :], chosen)
                chosen = jnp.take_along_axis(chosen, index, axis=1, mode="promise_in_bounds")
                chosen = 1.0 - chosen
                cost_ref[pl.ds(pl.multiple_of(here * rows, rows) + y, width, stride=rows), :] = chosen
                if mine:
                    own_ref[y] = chosen.T.astype(jnp.bfloat16)

        pl.when(p == own)(functools.partial(tile_costs, True))
        pl.when(p != own)(functools.partial(tile_costs, False))


def early_segments(parts):
    return 2 * parts - parts // 4


def across_kernel(second, place_ref, charge_ref, cost_ref, *refs):
    kept_ref, last_ref, same_ref = refs[-3:]
    parts = cost_ref.shape[0] // kept_ref.shape[1]
    rows = last_ref.shape[1] // 2
    width = kept_ref.shape[1] // rows
    cols = parts * width
    early = early_segments(parts)
    own = place_ref[2]
    p1, p2 = charges(charge_ref)

    place = lax.broadcasted_iota(jnp.int32, (DISPARITIES, 2 * DISPARITIES), 0)
    other = lax.broadcasted_iota(jnp.int32, (DISPARITIES, 2 * DISPARITIES), 1)
    same_ref[...] = jnp.where(place == other % DISPARITIES, 1.0, 0.0).astype(jnp.bfloat16)
    same = same_ref[...]

    def at(column):
        return pl.ds(pl.multiple_of(column * rows, rows), rows)

    def cost_at(step):
        step = jnp.minimum(step, cols - 1)
        pair = jnp.concatenate([cost_ref[at(step)], cost_ref[at(cols - 1 - step)]], axis=0)
        coarse = pair.astype(jnp.bfloat16)
        fine = (pair - coarse.astype(jnp.float32)).astype(jnp.bfloat16)
        return registers(
            lax.dot_general(
                same,
                jnp.concatenate([coarse, fine], axis=1),
                (((1,), (1,)), ((), ())),
                preferred_element_type=jnp.float32,
            )
        )

    def segment(p, state):
        half = width // 2
        first_step = p * half
        tile = p // 2
        inner = (p % 2) * half

        def run(keep_right, keep_left, state):
            def body(i, carry):
                sums, cost = carry
                ahead = cost_at(first_step + i + 1)
                least = least_of(list(sums))
                jump = least + p2
                fresh = [
                    c + jnp.minimum(t, jump) for t, c in zip(stepped(list(sums), p1), cost)
                ]
                if keep_right or keep_left:
                    back = jnp.concatenate([f - least for f in fresh], axis=0).T
                if keep_right:
                    kept_ref[0, at(inner + i)] = back[0:rows]
                if keep_left:
                    kept_ref[1, at(width - 1 - inner - i)] = back[rows : 2 * rows]
                return tuple(fresh), tuple(ahead)

            carry = (state, tuple(cost_at(first_step)))
            sums = lax.fori_loop(0, half, body, carry, unroll=64)[0]
            least = least_of(list(sums))
            return tuple(s - least for s in sums)

        choice = jnp.where(tile == own, 1, 0) + jnp.where(parts - 1 - tile == own, 2, 0)
        return lax.switch(
            choice,
            [functools.partial(run, k == 1, k == 2) for k in range(3)],
            state,
        )

    if second:
        state = tuple(registers(refs[0][...]))
        span = (early, 2 * parts)
    else:
        state = tuple(jnp.zeros((SUB, 2 * rows), jnp.float32) for _ in range(REGS))
        span = (0, early)
    last_ref[...] = jnp.concatenate(lax.fori_loop(*span, segment, state), axis=0)


def down_or_up(forward, first_own, cost_ref, state, p1, p2, keep):
    group, rows = cost_ref.shape[:2]

    def block(b, state):
        member = jnp.where(forward, b, group - 1 - b)

        def run(kept, state):
            for i in range(rows):
                inner = jnp.where(forward, i, rows - 1 - i)
                cost = cost_ref[member, inner].astype(jnp.float32)
                state = advance(list(state), registers(cost), p1, p2)
                if kept:
                    keep(inner, jnp.concatenate(state, axis=0))
            return tuple(state)

        return lax.cond(
            member == first_own,
            functools.partial(run, True),
            functools.partial(run, False),
            state,
        )

    return lax.fori_loop(0, group, block, state)


def first_vertical_kernel(place_ref, charge_ref, *refs):
    *block_refs, kept_ref, last_ref, cost_ref = refs
    p1, p2 = charges(charge_ref)
    group, _, _, width = cost_ref.shape
    for k, block_ref in enumerate(block_refs):
        cost_ref[lax.rem(place_ref[4] + group - k, group)] = block_ref[...]
    state = tuple(jnp.zeros((SUB, width), jnp.float32) for _ in range(REGS))

    def keep(row, value):
        kept_ref[row] = value

    final = down_or_up(place_ref[3] == 0, place_ref[4], cost_ref, state, p1, p2, keep)
    last_ref[...] = jnp.concatenate(final, axis=0).astype(jnp.bfloat16)


def second_vertical_kernel(place_ref, charge_ref, *refs):
    *block_refs, kept_ref, came_ref, early_ref, late_ref, out_ref, total, cost_ref = refs
    p1, p2 = charges(charge_ref)
    group = cost_ref.shape[0]
    for k, block_ref in enumerate(block_refs):
        cost_ref[lax.rem(place_ref[4] + group - k, group)] = block_ref[...]
    rows, _, width = kept_ref.shape
    state = tuple(registers(came_ref[...].astype(jnp.float32)))

    def keep(row, value):
        total[row] = value + kept_ref[row]

    down_or_up(place_ref[3] != 0, place_ref[4], cost_ref, state, p1, p2, keep)
    lane = lax.broadcasted_iota(jnp.int32, (width, DISPARITIES), 1)
    index = disparity_to_lane(lane)
    column = place_ref[2] * width + lax.broadcasted_iota(jnp.int32, (width, DISPARITIES), 0)
    right_early = column < place_ref[6]
    left_early = place_ref[5] * width - 1 - column < place_ref[6]
    for row in range(rows):
        this = pl.ds(row, width, stride=rows)
        right = jnp.where(right_early, early_ref[0, this, :], late_ref[0, this, :])
        left = jnp.where(left_early, early_ref[1, this, :], late_ref[1, this, :])
        value = total[row].T + (right + left)
        out_ref[row] = jnp.take_along_axis(value, index, axis=1, mode="promise_in_bounds")


SMEM = functools.partial(pl.BlockSpec, memory_space=pltpu.SMEM)
VMEM = functools.partial(pl.BlockSpec, memory_space=pltpu.VMEM)


def call(kernel, outs, specs, scratch=(), flops=0, vmem=20):
    return pl.pallas_call(
        kernel,
        out_shape=outs,
        in_specs=specs,
        out_specs=jax.tree.map(lambda _: VMEM(), outs),
        scratch_shapes=list(scratch),
        compiler_params=pltpu.CompilerParams(vmem_limit_bytes=vmem * MEBI),
        cost_estimate=pl.CostEstimate(flops=flops, bytes_accessed=1 << 22, transcendentals=0),
    )


def spread(block, parts, beside=()):
    masks, blocks = [0], [block]
    bit = parts // 2
    while bit:
        route = [(i, i ^ bit) for i in range(parts)]
        blocks += [lax.ppermute(held, "col", route) for held in blocks]
        masks += [mask ^ bit for mask in masks]
        if beside and bit == parts // 2:
            first, *beside = lax.optimization_barrier((blocks[1], *beside))
            blocks[1] = first
        bit //= 2
    return masks, blocks, beside


def per_device(activations, filters, biases, present, shifts, smooth):
    _, rows, channels, width = activations.shape
    layers = filters.shape[0]
    high = rows + 2 * layers
    row_rank, row_count = lax.axis_index("row"), lax.axis_size("row")
    col_rank, parts = lax.axis_index("col"), lax.axis_size("col")
    half = row_count // 2
    cols = parts * width
    place = jnp.stack(
        [
            row_rank,
            jnp.int32(row_count),
            col_rank,
            row_rank // half,
            row_rank % half,
            jnp.int32(parts),
            jnp.int32(early_segments(parts) * (width // 2)),
        ]
    ).astype(jnp.int32)

    downward = [(i, i + 1) for i in range(row_count - 1)]
    upward = [(i + 1, i) for i in range(row_count - 1)]
    before = lax.ppermute(activations[:, rows - layers :], "row", downward)
    after = lax.ppermute(activations[:, :layers], "row", upward)
    f32, bf16 = jnp.float32, jnp.bfloat16
    tile = activations.reshape(2 * rows, channels, width)
    taps, upright, staged = call(
        stage_kernel,
        (
            jax.ShapeDtypeStruct((layers, 3 * channels, 3 * channels), bf16),
            jax.ShapeDtypeStruct((layers, channels, 1), f32),
            jax.ShapeDtypeStruct(tile.shape, bf16),
        ),
        [VMEM()] * 3,
        flops=10**8,
    )(filters, biases, tile)
    before, after, taps, upright, staged = lax.optimization_barrier(
        (before, after, taps, upright, staged)
    )
    extra = jnp.concatenate(
        [
            present.astype(jnp.bfloat16),
            jnp.zeros((16 - rows, width), jnp.bfloat16),
            jnp.broadcast_to(shifts.astype(jnp.bfloat16), (channels - 16, width)),
        ],
        axis=0,
    )
    edges = jnp.concatenate(
        [before.reshape(-1, channels, width), after.reshape(-1, channels, width), extra[None]],
        axis=0,
    )
    masks, tiles, _ = spread(tile, parts)

    lead = (OFF_MOST + 2 * width - 1) // width * width
    inner = call(
        functools.partial(inner_kernel, masks),
        tuple(
            jax.ShapeDtypeStruct((2, (rows - 2 * layer) * channels, cols), bf16)
            for layer in range(layers)
        ),
        [SMEM()] + [VMEM()] * (2 + parts),
        flops=2 * 10**9,
        vmem=32,
    )(place, taps, upright, staged, *tiles[1:])
    _, edges, inner = spread(edges, parts, inner)
    cost, own = call(
        functools.partial(band_kernel, masks),
        (
            jax.ShapeDtypeStruct((cols * rows, DISPARITIES), f32),
            jax.ShapeDtypeStruct((rows, DISPARITIES, width), bf16),
        ),
        [SMEM()] + [VMEM()] * (2 + layers + parts),
        [
            pltpu.VMEM((rows * channels, cols), bf16),
            pltpu.VMEM((rows * channels, lead + cols + width), bf16),
            pltpu.VMEM((16, cols), f32),
            pltpu.VMEM((parts, SUB, width), f32),
            *(
                pltpu.VMEM(((high - 2 * layer) * channels, cols), bf16)
                for layer in range(layers)
            ),
        ],
        flops=10**10,
        vmem=40,
    )(place, taps, upright, *inner, *edges)

    blocks = [own]
    for k in range(1, half):
        turn = [(i, i // half * half + (i + k) % half) for i in range(row_count)]
        blocks.append(lax.ppermute(own, "row", turn))

    halves = (
        jax.ShapeDtypeStruct((2, width * rows, DISPARITIES), f32),
        jax.ShapeDtypeStruct((DISPARITIES, 2 * rows), f32),
    )
    identity = [pltpu.VMEM((DISPARITIES, 2 * DISPARITIES), bf16)]
    early, state = call(
        functools.partial(across_kernel, False),
        halves,
        [SMEM(), SMEM(), VMEM()],
        identity,
        flops=10**10,
    )(place, smooth, cost)
    *blocks, state = lax.optimization_barrier((*blocks, state))

    joined = pltpu.VMEM((half, rows, DISPARITIES, width), bf16)
    kept, last = call(
        first_vertical_kernel,
        (
            jax.ShapeDtypeStruct((rows, DISPARITIES, width), f32),
            jax.ShapeDtypeStruct((DISPARITIES, width), bf16),
        ),
        [SMEM(), SMEM()] + [VMEM()] * half,
        [joined],
        flops=2 * 10**9,
    )(place, smooth, *blocks)

    swap = [(i, (i + half) % row_count) for i in range(row_count)]
    last, state = lax.optimization_barrier((last, state))
    came = lax.ppermute(last, "row", swap)
    late, _ = call(
        functools.partial(across_kernel, True),
        halves,
        [SMEM(), SMEM(), VMEM(), VMEM()],
        identity,
        flops=10**10,
    )(place, smooth, cost, state)

    return call(
        second_vertical_kernel,
        jax.ShapeDtypeStruct((rows, width, DISPARITIES), f32),
        [SMEM(), SMEM()] + [VMEM()] * (half + 4),
        [pltpu.VMEM((rows, DISPARITIES, width), f32), joined],
        flops=3 * 10**9,
    )(place, smooth, *blocks, kept, came, early, late)


def solution(mesh):
    return jax.shard_map(
        per_device,
        mesh=mesh,
        in_specs=(P(None, "row", None, "col"), P(), P(), P("row", "col"), P("row", "col"), P()),
        out_specs=P("row", "col", None),
        check_vma=False,
    )
```
